256 devices in a mesh: enc: 8 (over z), mb: 2 (over core), tp: 16 (over y, x).
Axes of the slice: x: 4, y: 4, z: 8, core: 2. Of those that a mesh axis runs over, the one named last changes fastest.
Arguments:
- patches: bfloat16 [8, 2, 1024, 1280], P('enc', 'mb', 'tp'), may hold values from -6 to 6
- patch_counts: int32 [8, 2, 32], P('enc', 'mb'), may hold values from 4 to 32, as said below
- dest_pos: int32 [8, 2, 256], P('enc', 'mb'), may hold values from 0 to 2047, as said below
- merge_gain: float32 [1280], replicated, may hold values from 0.25 to 1.75
- merge_bias: float32 [1280], replicated, may hold values from -3 to 3
- up_weight: bfloat16 [5120, 5120], P(('enc', 'mb'), 'tp'), may hold values from -0.078125 to 0.078125
- up_bias: float32 [5120], replicated, may hold values from -3 to 3
- down_weight: bfloat16 [5120, 8192], P('tp', ('enc', 'mb')), may hold values from -0.078125 to 0.078125
- down_bias: float32 [8192], replicated, may hold values from -3 to 3
- text_embed: bfloat16 [8, 2, 2048, 8192], P('enc', 'mb', 'tp'), may hold values from -6 to 6
- norm_gain: float32 [8192], replicated, may hold values from 0.25 to 1.75
- kv_weight: bfloat16 [8192, 2048], P('tp'), may hold values from -0.0625 to 0.0625
- kv_bias: float32 [2048], replicated, may hold values from -3 to 3
Outputs:
- embedded: bfloat16 [8, 2, 2048, 8192], P('enc', 'mb', 'tp')
- keys_values: bfloat16 [8, 2, 2048, 2048], P('enc', 'mb', 'tp')
The draws below stay inside these ranges and needn't reach their ends.
Inputs may be any that keep to these rules, and one draw needn't show every extreme that they name: `patch_counts`: each image's patch count is four times its merged rows; in every sequence some image has 32 patches. The image slots of enc index e and mb index m feed sequence (e, m); slot j of device t of tp is image t * 2 + j. `dest_pos`: the 8 slots of an image hold consecutive positions; slots past the image's merged rows are not live and their positions are used by no live slot; no two live slots of a sequence share a position.
All inputs are finite; a program needn't handle non-finite values.
Results may differ from the reference program's by a relative error of at most 0.02.
Values may be sent and summed in bfloat16 or wider, within the bound.
No kernel may reach another device: no remote copies, remote signals or barrier semaphores. Data moves between devices by JAX's collectives and lax.ppermute only.
A program may use at most 64 MiB of HBM per device.

```python
import jax
import jax.numpy as jnp
from jax import lax

DV = 1280
MERGED = 5120
HID = 5120
D = 8192
KV_COLS = 2048
TOK_DEV = 128
IMG_DEV = 2
SLOT = 8
SLOTS_DEV = 16
GS = 256
SEQ = 2048
N_ENC = 8
N_MB = 2
N_TP = 16


def image_layout(key):
    groups = N_ENC * N_MB
    images = N_TP * IMG_DEV
    segment = TOK_DEV // IMG_DEV
    keys = jax.random.split(key, 6)
    heavy = jax.random.randint(keys[0], (groups, N_TP, 1), 0, 2)
    broad = jax.random.randint(keys[1], (groups, N_TP, IMG_DEV), 1, SLOT + 1)
    slim = jax.random.randint(keys[2], (groups, N_TP, IMG_DEV), 1, max(SLOT // 4, 1) + 1)
    rows = jnp.where(heavy == 1, broad, slim).reshape(groups, images)
    filled = jax.random.randint(keys[3], (groups, 1), 0, images)
    rows = jnp.where(jnp.arange(images)[None, :] == filled, SLOT, rows)
    order = jax.vmap(lambda sub: jax.random.permutation(sub, images))(jax.random.split(keys[4], groups))
    offset = jax.random.randint(keys[5], (groups, images), 0, segment - SLOT + 1)
    first = order * segment + offset
    places = first[:, :, None] + jnp.arange(SLOT)[None, None, :]
    return (rows.astype(jnp.int32), places.reshape(groups, GS).astype(jnp.int32))


def draw_patch_counts(key, part):
    rows, places = image_layout(key)
    return (4 * rows).reshape(N_ENC, N_MB, N_TP * IMG_DEV)


def draw_dest_pos(key, part):
    rows, places = image_layout(key)
    return places.reshape(N_ENC, N_MB, GS)


def steps_of(rng, dims, cuts, least, top_value):
    loudness, own = 1.0, jax.random.fold_in(rng, 6)
    for position, blocks in cuts:
        heights = jnp.exp(jax.random.uniform(jax.random.fold_in(own, position), (blocks,), jnp.float32, least / len(cuts), top_value / len(cuts)))
        loudness = loudness * jnp.repeat(heights, dims[position] // blocks).reshape([-1 if axis == position else 1 for axis in range(len(dims))])
    return loudness


def gaussian(rng, extent, scale, reach, pieces=(), kind=jnp.bfloat16):
    drawn = scale * jax.random.normal(rng, extent, jnp.float32)
    if pieces:
        drawn = drawn * steps_of(rng, extent, pieces, -0.22, 0.18)
    return jnp.clip(drawn, -reach, reach).astype(kind)


def setup_inputs(seed: int = 0) -> dict:
    arg_keys = jax.random.split(jax.random.key(seed), 14)
    return {
        "patches": gaussian(arg_keys[0], (N_ENC, N_MB, N_TP * 4 * SLOTS_DEV, DV), 1.0, 6.0, ((0, 8), (1, 2), (2, 16))),
        "patch_counts": draw_patch_counts(jax.random.fold_in(arg_keys[13], 71), 0),
        "dest_pos": draw_dest_pos(jax.random.fold_in(arg_keys[13], 71), 0),
        "merge_gain": jnp.clip(1.0 + 0.15 * jax.random.normal(arg_keys[3], (DV,), jnp.float32), 0.25, 1.75),
        "merge_bias": gaussian(arg_keys[4], (DV,), 0.5, 3.0, (), jnp.float32),
        "up_weight": gaussian(arg_keys[5], (MERGED, HID), MERGED ** -0.5, 0.078125, ((0, 16), (1, 16))),
        "up_bias": gaussian(arg_keys[6], (HID,), 0.5, 3.0, (), jnp.float32),
        "down_weight": gaussian(arg_keys[7], (HID, D), HID ** -0.5, 0.078125, ((0, 16), (1, 16))),
        "down_bias": gaussian(arg_keys[8], (D,), 0.5, 3.0, (), jnp.float32),
        "text_embed": gaussian(arg_keys[9], (N_ENC, N_MB, SEQ, D), 1.0, 6.0, ((0, 8), (1, 2), (2, 16))),
        "norm_gain": jnp.clip(1.0 + 0.15 * jax.random.normal(arg_keys[10], (D,), jnp.float32), 0.25, 1.75),
        "kv_weight": gaussian(arg_keys[11], (D, KV_COLS), D ** -0.5, 0.0625, ((0, 16),)),
        "kv_bias": gaussian(arg_keys[12], (KV_COLS,), 0.5, 3.0, (), jnp.float32),
    }


def layer_norm(rows, gain, bias):
    values = rows.astype(jnp.float32)
    center = values - lax.optimization_barrier(jnp.mean(values, axis=-1, keepdims=True))
    spread = lax.optimization_barrier(jnp.mean(center * center, axis=-1, keepdims=True))
    return center * lax.rsqrt(spread + 1e-06) * gain + bias

def root_scale(values, gain):
    return (values * lax.rsqrt(lax.optimization_barrier(jnp.mean(values * values, axis=-1, keepdims=True)) + 1e-06) * gain).astype(jnp.bfloat16)

def block_sum(left, right, blocks):
    width = left.shape[1] // blocks

    def step(total, block):
        start = (block * width).astype(jnp.int32)
        piece = lax.dynamic_slice_in_dim(left, start, width, 1)
        rows = lax.dynamic_slice_in_dim(right, start, width, 0)
        term = jnp.dot(piece, rows, preferred_element_type=jnp.float32)
        term = lax.optimization_barrier(term.astype(jnp.bfloat16)).astype(jnp.float32)
        return (total + term, 0)
    empty = jnp.zeros((left.shape[0], right.shape[1]), jnp.float32)
    total, unused = lax.scan(step, empty, jnp.arange(blocks, dtype=jnp.int32))
    return total

def reference(patches, patch_counts, dest_pos, merge_gain, merge_bias, up_weight, up_bias, down_weight, down_bias, text_embed, norm_gain, kv_weight, kv_bias):
    groups = N_ENC * N_MB
    patch_all = patches.reshape(groups, 4 * GS, DV)
    count_all = patch_counts.reshape(groups, N_TP * IMG_DEV)
    place_all = dest_pos.reshape(groups, GS)
    text_all = text_embed.reshape(groups, SEQ, D)

    def one_group(inputs):
        patch, counts, places, text = inputs
        normal = layer_norm(patch, merge_gain, merge_bias).astype(jnp.bfloat16)
        merged = normal.reshape(GS, MERGED)
        raised = jnp.dot(merged, up_weight, preferred_element_type=jnp.float32) + up_bias
        hidden = jax.nn.gelu(raised, approximate=False).astype(jnp.bfloat16)
        total = block_sum(hidden, down_weight, N_TP) + down_bias
        visual = total.astype(jnp.bfloat16)
        live_rows = counts // 4
        live = (jnp.arange(SLOT, dtype=jnp.int32)[None, :] < live_rows[:, None]).reshape(GS)
        target = jnp.where(live, places, SEQ).astype(jnp.int32)
        embedded = text.at[target].set(visual, mode='drop')
        normed = root_scale(embedded.astype(jnp.float32), norm_gain)
        kv_total = block_sum(normed, kv_weight, N_TP) + kv_bias
        return (embedded, kv_total.astype(jnp.bfloat16))
    embedded, keys_values = lax.map(one_group, (patch_all, count_all, place_all, text_all))
    return (embedded.reshape(N_ENC, N_MB, SEQ, D), keys_values.reshape(N_ENC, N_MB, SEQ, KV_COLS))
```

```python
import jax
import jax.numpy as jnp
import numpy as np
from jax import lax
from jax.experimental import pallas as pl
from jax.experimental.pallas import tpu as pltpu
from jax.sharding import PartitionSpec as P

SLOT = 8
RING = (0, -1, 1, 2)
MIB = 1 << 20
BF16, F32 = jnp.bfloat16, jnp.float32


def place(core, tp, which, step):
    y, x = tp // 4, tp % 4
    if (core == 0) == (which == 1):
        return y * 4 + (x + step) % 4
    return (y + step) % 4 * 4 + x


TABLE = np.array(
    [
        [place(core, place(core, tp, 2, o2), 1, o1) for o2 in RING for o1 in RING]
        for core in range(2)
        for tp in range(16)
    ],
    np.int32,
)
HOPS = {
    (which, step): [(c * 16 + t, c * 16 + place(c, t, which, step)) for c in range(2) for t in range(16)]
    for which in (1, 2)
    for step in (1, -1)
}
SWAP = [(a * 16 + b, b * 16 + a) for a in range(16) for b in range(16)]


def hop(value, which, step):
    return lax.ppermute(value, ("mb", "tp"), HOPS[which, step])


def ring(value, which, axis=0):
    half = value.shape[axis] // 2
    right = hop(value, which, 1)
    left = hop(value, which, -1)
    far_a = hop(lax.slice_in_dim(right, 0, half, axis=axis), which, 1)
    far_b = hop(lax.slice_in_dim(left, half, 2 * half, axis=axis), which, -1)
    return right, left, far_a, far_b


def cost(flops, moved):
    return pl.CostEstimate(flops=flops, bytes_accessed=moved, transcendentals=0)


def params(mib):
    return pltpu.CompilerParams(vmem_limit_bytes=mib * MIB)


VMEM = pl.BlockSpec(memory_space=pltpu.VMEM)
SMEM = pl.BlockSpec(memory_space=pltpu.SMEM)
ANY = pl.BlockSpec(memory_space=pl.ANY)


def merge_kernel(p_ref, gain_ref, bias_ref, out_ref, rows):
    values = p_ref[...].astype(F32)
    center = values - jnp.mean(values, axis=-1, keepdims=True)
    spread = jnp.mean(center * center, axis=-1, keepdims=True)
    normal = center * lax.rsqrt(spread + 1e-06) * gain_ref[...] + bias_ref[...]
    for k in range(10):
        rows[k] = normal[:, k * 128 : (k + 1) * 128]
    for j in range(4):
        for k in range(10):
            start = j * 1280 + k * 128
            out_ref[:, start : start + 128] = rows[k, pl.ds(j, 16, stride=4), :].astype(BF16)


def merge(patches, gain, bias):
    return pl.pallas_call(
        merge_kernel,
        out_shape=jax.ShapeDtypeStruct((16, 5120), BF16),
        in_specs=[VMEM] * 3,
        out_specs=VMEM,
        scratch_shapes=[pltpu.VMEM((10, 64, 128), F32)],
        cost_estimate=cost(10**6, 330000),
    )(patches, gain, bias)


def pack_kernel(tab, text, to_right, to_left, own, sems):
    copies = []
    for j in range(4):
        at = pl.ds(j * 512, 512)

        def columns(i2):
            return pl.ds(pl.multiple_of(tab[i2 * 4 + j] * 512, 512), 512)

        copies += [
            (text.at[:, columns(2)], to_right.at[pl.ds(0, 128), at]),
            (text.at[pl.ds(0, 64), columns(3)], to_right.at[pl.ds(128, 64), at]),
            (text.at[pl.ds(64, 64), columns(3)], to_left.at[pl.ds(0, 64), at]),
            (text.at[:, columns(1)], to_left.at[pl.ds(64, 128), at]),
            (text.at[:, columns(0)], own.at[:, at]),
        ]
    copies = [pltpu.make_async_copy(a, b, sems.at[i]) for i, (a, b) in enumerate(copies)]
    for copy in copies:
        copy.start()
    for copy in copies:
        copy.wait()


def pack(tab, text):
    return pl.pallas_call(
        pack_kernel,
        out_shape=[jax.ShapeDtypeStruct((n, 2048), BF16) for n in (192, 192, 128)],
        in_specs=[SMEM, ANY],
        out_specs=[ANY] * 3,
        scratch_shapes=[pltpu.SemaphoreType.DMA((20,))],
        cost_estimate=cost(0, 4 * MIB),
    )(tab, text)


def up_kernel(tab, s0, s1, s2, s3a, s3b, weight, bias_ref, out_ref, rows, held, sems):
    copies = []
    for i2, piece in enumerate((s0, s1, s2, None)):
        for i1 in range(4):
            if piece is None:
                source = (s3a, s3b)[i1 // 2].at[pl.ds(i1 % 2 * 16, 16)]
            else:
                source = piece.at[pl.ds(i1 * 16, 16)]
            target = rows.at[pl.ds(pl.multiple_of(tab[i2 * 4 + i1] * 16, 16), 16)]
            copies.append((source, target))
    copies.append((weight, held))
    copies = [pltpu.make_async_copy(a, b, sems.at[i]) for i, (a, b) in enumerate(copies)]
    for copy in copies:
        copy.start()
    for copy in copies:
        copy.wait()
    raised = jnp.dot(rows[...], held[...], preferred_element_type=F32) + bias_ref[tab[0]]
    out_ref[...] = (0.5 * raised * (1.0 + lax.erf(raised * np.float32(0.5**0.5)))).astype(BF16)


def up(tab, pieces, weight, bias):
    return pl.pallas_call(
        up_kernel,
        out_shape=jax.ShapeDtypeStruct((256, 320), BF16),
        in_specs=[SMEM] + [ANY] * 6 + [VMEM],
        out_specs=VMEM,
        scratch_shapes=[
            pltpu.VMEM((256, 5120), BF16),
            pltpu.VMEM((5120, 320), BF16),
            pltpu.SemaphoreType.DMA((17,)),
        ],
        compiler_params=params(32),
        cost_estimate=cost(840 * 10**6, 6 * MIB),
    )(tab, *pieces, weight, bias)


def down_kernel(tab, h0, h1, h2, h3a, h3b, weight, bias_ref, out_ref, held, sems):
    copies = []
    for k in range(16):
        source = weight.at[pl.ds(pl.multiple_of(tab[k] * 320, 320), 320)]
        copies.append(pltpu.make_async_copy(source, held.at[pl.ds(k * 320, 320)], sems.at[k]))
    for copy in copies:
        copy.start()
    for copy in copies:
        copy.wait()
    total = bias_ref[tab[0]]
    for i2, piece in enumerate((h0[...], h1[...], h2[...], jnp.concatenate([h3a[...], h3b[...]], axis=0))):
        total = total + jnp.dot(piece, held[i2 * 1280 : (i2 + 1) * 1280, :], preferred_element_type=F32)
    out_ref[...] = total.astype(BF16)


def down(tab, pieces, weight, bias):
    return pl.pallas_call(
        down_kernel,
        out_shape=jax.ShapeDtypeStruct((256, 512), BF16),
        in_specs=[SMEM] + [VMEM] * 5 + [ANY] + [VMEM],
        out_specs=VMEM,
        scratch_shapes=[pltpu.VMEM((5120, 512), BF16), pltpu.SemaphoreType.DMA((16,))],
        compiler_params=params(32),
        cost_estimate=cost(1340 * 10**6, 8 * MIB),
    )(tab, *pieces, weight, bias)


def pick_kernel(tab, dest, v0, v1, v2, v3a, v3b, own, right, left, far_a, far_b, to_right, to_left, kept):
    visual = (v0[...], v1[...], v2[...], jnp.concatenate([v3a[...], v3b[...]], axis=0))
    targets = dest[...]

    def rows(i2, first, count):
        start = tab[i2 * 4] * 128 + first
        match = (lax.broadcasted_iota(jnp.int32, (count, 256), 0) + start) == targets
        select = match.astype(F32)
        return select.astype(BF16), jnp.sum(select, axis=1, keepdims=True) > 0.0

    def fill(i2, first, count, text, text_row, out, out_row):
        select, present = rows(i2, first, count)
        for j in range(4):
            at = slice(j * 512, (j + 1) * 512)
            picked = jnp.dot(select, visual[j], preferred_element_type=F32).astype(BF16)
            out[out_row : out_row + count, at] = jnp.where(present, picked, text[text_row : text_row + count, at])

    fill(2, 0, 128, left, 64, to_right, 0)
    fill(3, 0, 64, far_a, 0, to_right, 128)
    fill(3, 64, 64, far_b, 0, to_left, 0)
    fill(1, 0, 128, right, 0, to_left, 64)
    fill(0, 0, 128, own, 0, kept, 0)


def pick(tab, dest, visual, text):
    return pl.pallas_call(
        pick_kernel,
        out_shape=[jax.ShapeDtypeStruct((n, 2048), BF16) for n in (192, 192, 128)],
        in_specs=[SMEM] + [VMEM] * 11,
        out_specs=[VMEM] * 3,
        compiler_params=params(32),
        cost_estimate=cost(540 * 10**6, 6 * MIB),
    )(tab, dest, *visual, *text)


def product_kernel(tab, to_right, to_left, kept, gain, w0, w1, w2, w3a, w3b, far_a, far_b, right, left, own, scaled):
    @pl.when(pl.program_id(0) == 0)
    def _():
        for j in range(4):
            at = slice(j * 512, (j + 1) * 512)
            scale = gain[tab[j]]

            def times(ref, first, count):
                return (ref[first : first + count, at].astype(F32) * scale).astype(BF16)

            scaled[0:64, at] = times(to_right, 128, 64)
            scaled[64:128, at] = times(to_left, 0, 64)
            scaled[128:256, at] = times(to_right, 0, 128)
            scaled[256:384, at] = times(to_left, 64, 128)
            scaled[384:512, at] = times(kept, 0, 128)

    total = jnp.dot(scaled[:, 0:512], w0[...], preferred_element_type=F32)
    total = total + jnp.dot(scaled[:, 512:1024], w1[...], preferred_element_type=F32)
    total = total + jnp.dot(scaled[:, 1024:1536], w2[...], preferred_element_type=F32)
    total = total + jnp.dot(scaled[:, 1536:1792], w3a[...], preferred_element_type=F32)
    total = total + jnp.dot(scaled[:, 1792:2048], w3b[...], preferred_element_type=F32)
    far_a[...] = total[0:64].astype(BF16)
    far_b[...] = total[64:128].astype(BF16)
    right[...] = total[128:256].astype(BF16)
    left[...] = total[256:384].astype(BF16)
    own[...] = total[384:512]


def product(tab, picked, gain, weights):
    def block(count):
        return pl.BlockSpec((count, 512), lambda n: (0, n))

    return pl.pallas_call(
        product_kernel,
        out_shape=[jax.ShapeDtypeStruct((n, 2048), BF16) for n in (64, 64, 128, 128)]
        + [jax.ShapeDtypeStruct((128, 2048), F32)],
        grid=(4,),
        in_specs=[SMEM] + [VMEM] * 4 + [block(n) for n in (512, 512, 512, 256, 256)],
        out_specs=[block(n) for n in (64, 64, 128, 128, 128)],
        scratch_shapes=[pltpu.VMEM((512, 2048), BF16)],
        compiler_params=params(40),
        cost_estimate=cost(4300 * 10**6, 14 * MIB),
    )(tab, *picked, gain, *weights)


def place_kernel(tab, own, right, left, far_a, far_b, out, scale, sems):
    copies = []
    for j in range(4):
        at = pl.ds(j * 512, 512)

        def columns(i2):
            return pl.ds(pl.multiple_of(tab[i2 * 4 + j] * 512, 512), 512)

        copies += [
            (own.at[:, at], out.at[:, columns(0)]),
            (right.at[pl.ds(0, 128), at], out.at[:, columns(1)]),
            (left.at[pl.ds(64, 128), at], out.at[:, columns(2)]),
            (far_a.at[:, at], out.at[pl.ds(0, 64), columns(3)]),
            (far_b.at[:, at], out.at[pl.ds(64, 64), columns(3)]),
        ]
    copies = [pltpu.make_async_copy(a, b, sems.at[i]) for i, (a, b) in enumerate(copies)]
    for copy in copies:
        copy.start()

    def squares(values):
        values = values.astype(F32)
        return jnp.sum(values * values, axis=1, keepdims=True)

    far = jnp.concatenate([squares(far_a[...]), squares(far_b[...])], axis=0)
    total = squares(own[...]) + squares(right[0:128]) + squares(left[64:192]) + far
    scale[...] = jnp.broadcast_to(lax.rsqrt(total * (1.0 / 8192.0) + 1e-06), (128, 128))
    for copy in copies:
        copy.wait()


def place_rows(tab, pieces):
    return pl.pallas_call(
        place_kernel,
        out_shape=[jax.ShapeDtypeStruct((128, 8192), BF16), jax.ShapeDtypeStruct((128, 128), F32)],
        in_specs=[SMEM] + [VMEM] * 5,
        out_specs=[ANY, VMEM],
        scratch_shapes=[pltpu.SemaphoreType.DMA((20,))],
        compiler_params=params(32),
        cost_estimate=cost(4 * 10**6, 5 * MIB),
    )(tab, *pieces)


def per_device(
    patches,
    patch_counts,
    dest_pos,
    merge_gain,
    merge_bias,
    up_weight,
    up_bias,
    down_weight,
    down_bias,
    text_embed,
    norm_gain,
    kv_weight,
    kv_bias,
):
    tab = jnp.asarray(TABLE)[lax.axis_index("mb") * 16 + lax.axis_index("tp")]
    up_full = lax.all_gather(up_weight, ("enc", "mb"), axis=0, tiled=True)
    down_part = lax.ppermute(down_weight, ("enc", "mb", "tp"), SWAP)
    down_full = lax.all_gather(down_part, ("enc", "mb"), axis=0, tiled=True)

    merged = merge(patches[0, 0], merge_gain[None], merge_bias[None])
    right, left, far_a, far_b = ring(merged, 1, axis=1)
    near = jnp.concatenate([merged, right, left, jnp.concatenate([far_a, far_b], axis=1)], axis=0)
    group = (near, *ring(near, 2))

    text_right, text_left, text_own = pack(tab, text_embed[0, 0])
    right = hop(text_right, 2, 1)
    left = hop(text_left, 2, -1)
    text = (text_own, right, left, hop(right[128:192], 2, 1), hop(left[0:64], 2, -1))
    weights = (kv_weight, *ring(kv_weight, 1))

    hidden = up(tab, group, up_full, up_bias.reshape(16, 1, 320))
    right, left, far_a, far_b = ring(hidden, 1)
    near = jnp.concatenate([hidden, right, left, jnp.concatenate([far_a, far_b], axis=0)], axis=1)
    units = (near, *ring(near, 2))
    visual = down(tab, units, down_full, down_bias.reshape(16, 1, 512))
    visual = (visual, *ring(visual, 1))

    live_rows = patch_counts[0, 0] // 4
    live = (jnp.arange(SLOT, dtype=jnp.int32)[None, :] < live_rows[:, None]).reshape(-1)
    dest = jnp.where(live, dest_pos[0, 0], -1)[None]
    to_right, to_left, kept = pick(tab, dest, visual, text)
    right = hop(to_right, 2, 1)
    left = hop(to_left, 2, -1)
    pieces = (kept, right, left, hop(right[128:192], 2, 1), hop(left[0:64], 2, -1))

    far_a, far_b, to_right, to_left, own = product(
        tab, (to_right, to_left, kept), norm_gain.reshape(16, 1, 512), weights
    )
    far_a = hop(far_a, 2, 1).astype(F32)
    far_b = hop(far_b, 2, -1).astype(F32)
    to_right, to_left = to_right.astype(F32), to_left.astype(F32)
    to_right = jnp.concatenate([to_right[:64] + far_a, to_right[64:]], axis=0).astype(BF16)
    to_left = jnp.concatenate([to_left[:64], to_left[64:] + far_b], axis=0).astype(BF16)
    right = hop(to_right, 2, 1).astype(F32)
    left = hop(to_left, 2, -1).astype(F32)
    embedded, scale = place_rows(tab, pieces)
    keys_values = ((own + right + left) * scale[:, :1] + kv_bias).astype(BF16)
    return (embedded[None, None], keys_values[None, None])


def solution(mesh):
    return jax.shard_map(
        per_device,
        mesh=mesh,
        in_specs=(
            P("enc", "mb", "tp", None),
            P("enc", "mb", None),
            P("enc", "mb", None),
            P(),
            P(),
            P(("enc", "mb"), "tp"),
            P(),
            P("tp", ("enc", "mb")),
            P(),
            P("enc", "mb", "tp", None),
            P(),
            P("tp", None),
            P(),
        ),
        out_specs=(P("enc", "mb", "tp", None), P("enc", "mb", "tp", None)),
        check_vma=False,
    )
```

```python
import jax
import jax.numpy as jnp
import numpy as np
from jax import lax
from jax.experimental import pallas as pl
from jax.experimental.pallas import tpu as pltpu
from jax.sharding import PartitionSpec as P

SLOT = 8
RING = (0, -1, 1, 2)
MIB = 1 << 20
BF16, F32 = jnp.bfloat16, jnp.float32


def place(core, tp, which, step):
    y, x = tp // 4, tp % 4
    if (core == 0) == (which == 1):
        return y * 4 + (x + step) % 4
    return (y + step) % 4 * 4 + x


TABLE = np.array(
    [
        [place(core, place(core, tp, 2, o2), 1, o1) for o2 in RING for o1 in RING]
        for core in range(2)
        for tp in range(16)
    ],
    np.int32,
)
HOPS = {
    (which, step): [(c * 16 + t, c * 16 + place(c, t, which, step)) for c in range(2) for t in range(16)]
    for which in (1, 2)
    for step in (1, -1)
}
SHUFFLE = [(a * 16 + b, (a ^ b) * 16 + b) for a in range(16) for b in range(16)]
TURN = [(a * 16 + b, a * 16 + (a ^ b)) for a in range(16) for b in range(16)]
OTHER = [(0, 1), (1, 0)]
CLIMB = [(z * 2 + c, (z + 1 - 2 * c) % 8 * 2 + c) for z in range(8) for c in range(2)]


def climbed(z, core, other):
    step = -1 if (core == 0) != other else 1
    first = core ^ int(other)
    near = [(z + step * k) % 8 * 2 + (first ^ j) for k in (1, 2, 3) for j in (0, 1)]
    return near + [(z + 4) % 8 * 2 + first]


STACK = np.array(
    [
        [z * 2 + c, z * 2 + 1 - c] + climbed(z, c, False) + climbed(z, c, True)
        for z in range(8)
        for c in range(2)
    ],
    np.int32,
)


def hop(value, which, step):
    return lax.ppermute(value, ("mb", "tp"), HOPS[which, step])


def ring(value, which, axis=0):
    half = value.shape[axis] // 2
    right = hop(value, which, 1)
    left = hop(value, which, -1)
    far_a = hop(lax.slice_in_dim(right, 0, half, axis=axis), which, 1)
    far_b = hop(lax.slice_in_dim(left, half, 2 * half, axis=axis), which, -1)
    return right, left, far_a, far_b


def after(value, *others):
    return lax.optimization_barrier((value, *others))[0]


def cost(flops, moved):
    return pl.CostEstimate(flops=flops, bytes_accessed=moved, transcendentals=0)


def params(mib):
    return pltpu.CompilerParams(vmem_limit_bytes=mib * MIB)


VMEM = pl.BlockSpec(memory_space=pltpu.VMEM)
SMEM = pl.BlockSpec(memory_space=pltpu.SMEM)
ANY = pl.BlockSpec(memory_space=pl.ANY)
HBM = pl.BlockSpec(memory_space=pltpu.HBM)


def merge_kernel(p_ref, gain_ref, bias_ref, out_ref, rows):
    values = p_ref[...].astype(F32)
    center = values - jnp.mean(values, axis=-1, keepdims=True)
    spread = jnp.mean(center * center, axis=-1, keepdims=True)
    normal = center * lax.rsqrt(spread + 1e-06) * gain_ref[...].reshape(1, 1280) + bias_ref[...].reshape(1, 1280)
    for k in range(10):
        rows[k] = normal[:, k * 128 : (k + 1) * 128]
    for j in range(4):
        for k in range(10):
            start = j * 1280 + k * 128
            out_ref[:, start : start + 128] = rows[k, pl.ds(j, 16, stride=4), :].astype(BF16)


def merge(patches, gain, bias):
    return pl.pallas_call(
        merge_kernel,
        out_shape=jax.ShapeDtypeStruct((16, 5120), BF16),
        in_specs=[VMEM] * 3,
        out_specs=VMEM,
        scratch_shapes=[pltpu.VMEM((10, 64, 128), F32)],
        cost_estimate=cost(10**6, 330000),
    )(patches, gain, bias)


def pack_kernel(tab, own, left, right, far, to_right, to_left, kept):
    to_right[0:128] = right[...]
    to_right[128:192] = far[0:64]
    to_left[0:64] = far[64:128]
    to_left[64:192] = left[...]
    kept[...] = own[...]


def pack(tab, text):
    def columns(i2):
        return pl.BlockSpec((128, 512), lambda j, tab: (0, tab[i2 * 4 + j]))

    def block(count):
        return pl.BlockSpec((count, 512), lambda j, tab: (0, j))

    return pl.pallas_call(
        pack_kernel,
        out_shape=[jax.ShapeDtypeStruct((n, 2048), BF16) for n in (192, 192, 128)],
        grid_spec=pltpu.PrefetchScalarGridSpec(
            num_scalar_prefetch=1,
            grid=(4,),
            in_specs=[columns(i2) for i2 in range(4)],
            out_specs=[block(n) for n in (192, 192, 128)],
        ),
        cost_estimate=cost(0, 4 * MIB),
    )(tab, text, text, text, text)


def up_kernel(tab, stack, s0, s1, s2, s3a, s3b, *rest):
    *weights, bias_ref, out_ref, rows, held, sems = rest
    copies = []
    for i2, piece in enumerate((s0, s1, s2, None)):
        for i1 in range(4):
            if piece is None:
                source = (s3a, s3b)[i1 // 2].at[pl.ds(i1 % 2 * 16, 16)]
            else:
                source = piece.at[pl.ds(i1 * 16, 16)]
            target = rows.at[pl.ds(pl.multiple_of(tab[i2 * 4 + i1] * 16, 16), 16)]
            copies.append((source, target))
    blocks = list(weights[:2]) + [w.at[k] for w in weights[2:] for k in range(w.shape[0])]
    for k, block in enumerate(blocks):
        copies.append((block, held.at[pl.ds(pl.multiple_of(stack[k] * 320, 320), 320)]))
    copies = [pltpu.make_async_copy(a, b, sems.at[i]) for i, (a, b) in enumerate(copies)]
    for copy in copies:
        copy.start()
    for copy in copies:
        copy.wait()
    raised = jnp.dot(rows[...], held[...], preferred_element_type=F32) + bias_ref[tab[0]]
    out_ref[...] = (0.5 * raised * (1.0 + lax.erf(raised * np.float32(0.5**0.5)))).astype(BF16)


def up(tab, stack, pieces, weights, bias):
    return pl.pallas_call(
        up_kernel,
        out_shape=jax.ShapeDtypeStruct((256, 320), BF16),
        in_specs=[SMEM] * 2 + [ANY] * 15 + [VMEM],
        out_specs=VMEM,
        scratch_shapes=[
            pltpu.VMEM((256, 5120), BF16),
            pltpu.VMEM((5120, 320), BF16),
            pltpu.SemaphoreType.DMA((32,)),
        ],
        compiler_params=params(32),
        cost_estimate=cost(840 * 10**6, 6 * MIB),
    )(tab, stack, *pieces, *weights, bias)


def down_kernel(tab, h0, h1, h2, h3a, h3b, weight, bias_ref, out_ref, held, sems):
    copies = []
    for k in range(16):
        source = weight.at[pl.ds(pl.multiple_of((tab[k] ^ tab[0]) * 320, 320), 320)]
        copies.append(pltpu.make_async_copy(source, held.at[pl.ds(k * 320, 320)], sems.at[k]))
    for copy in copies:
        copy.start()
    for copy in copies:
        copy.wait()
    total = bias_ref[tab[0]]
    for i2, piece in enumerate((h0[...], h1[...], h2[...], jnp.concatenate([h3a[...], h3b[...]], axis=0))):
        total = total + jnp.dot(piece, held[i2 * 1280 : (i2 + 1) * 1280, :], preferred_element_type=F32)
    out_ref[...] = total.astype(BF16)


def down(tab, pieces, weight, bias):
    return pl.pallas_call(
        down_kernel,
        out_shape=jax.ShapeDtypeStruct((256, 512), BF16),
        in_specs=[SMEM] + [VMEM] * 5 + [HBM, VMEM],
        out_specs=VMEM,
        scratch_shapes=[pltpu.VMEM((5120, 512), BF16), pltpu.SemaphoreType.DMA((16,))],
        compiler_params=params(32),
        cost_estimate=cost(1340 * 10**6, 8 * MIB),
    )(tab, *pieces, weight, bias)


def pick_kernel(tab, dest, v0, v1, v2, v3a, v3b, own, right, left, far_a, far_b, to_right, to_left, kept):
    visual = (v0[...], v1[...], v2[...], jnp.concatenate([v3a[...], v3b[...]], axis=0))
    targets = dest[...]

    def rows(i2, first, count):
        start = tab[i2 * 4] * 128 + first
        match = (lax.broadcasted_iota(jnp.int32, (count, 256), 0) + start) == targets
        select = match.astype(F32)
        return select.astype(BF16), jnp.sum(select, axis=1, keepdims=True) > 0.0

    def fill(i2, first, count, text, text_row, out, out_row):
        select, present = rows(i2, first, count)
        for j in range(4):
            at = slice(j * 512, (j + 1) * 512)
            picked = jnp.dot(select, visual[j], preferred_element_type=F32).astype(BF16)
            out[out_row : out_row + count, at] = jnp.where(present, picked, text[text_row : text_row + count, at])

    fill(2, 0, 128, left, 64, to_right, 0)
    fill(3, 0, 64, far_a, 0, to_right, 128)
    fill(3, 64, 64, far_b, 0, to_left, 0)
    fill(1, 0, 128, right, 0, to_left, 64)
    fill(0, 0, 128, own, 0, kept, 0)


def pick(tab, dest, visual, text):
    return pl.pallas_call(
        pick_kernel,
        out_shape=[jax.ShapeDtypeStruct((n, 2048), BF16) for n in (192, 192, 128)],
        in_specs=[SMEM] + [VMEM] * 11,
        out_specs=[VMEM] * 3,
        compiler_params=params(32),
        cost_estimate=cost(540 * 10**6, 6 * MIB),
    )(tab, dest, *visual, *text)


def product_kernel(tab, to_right, to_left, kept, gain, w0, w1, w2, w3a, w3b, far_a, far_b, right, left, own, scaled):
    @pl.when(pl.program_id(0) == 0)
    def _():
        for j in range(4):
            at = slice(j * 512, (j + 1) * 512)
            scale = gain[tab[j]]

            def times(ref, first, count):
                return (ref[first : first + count, at].astype(F32) * scale).astype(BF16)

            scaled[0:64, at] = times(to_right, 128, 64)
            scaled[64:128, at] = times(to_left, 0, 64)
            scaled[128:256, at] = times(to_right, 0, 128)
            scaled[256:384, at] = times(to_left, 64, 128)
            scaled[384:512, at] = times(kept, 0, 128)

    total = jnp.dot(scaled[:, 0:512], w0[...], preferred_element_type=F32)
    total = total + jnp.dot(scaled[:, 512:1024], w1[...], preferred_element_type=F32)
    total = total + jnp.dot(scaled[:, 1024:1536], w2[...], preferred_element_type=F32)
    total = total + jnp.dot(scaled[:, 1536:1792], w3a[...], preferred_element_type=F32)
    total = total + jnp.dot(scaled[:, 1792:2048], w3b[...], preferred_element_type=F32)
    far_a[...] = total[0:64].astype(BF16)
    far_b[...] = total[64:128].astype(BF16)
    right[...] = total[128:256].astype(BF16)
    left[...] = total[256:384].astype(BF16)
    own[...] = total[384:512]


def product(tab, picked, gain, weights):
    def block(count):
        return pl.BlockSpec((count, 512), lambda n: (0, n))

    return pl.pallas_call(
        product_kernel,
        out_shape=[jax.ShapeDtypeStruct((n, 2048), BF16) for n in (64, 64, 128, 128)]
        + [jax.ShapeDtypeStruct((128, 2048), F32)],
        grid=(4,),
        in_specs=[SMEM] + [VMEM] * 4 + [block(n) for n in (512, 512, 512, 256, 256)],
        out_specs=[block(n) for n in (64, 64, 128, 128, 128)],
        scratch_shapes=[pltpu.VMEM((512, 2048), BF16)],
        compiler_params=params(40),
        cost_estimate=cost(4300 * 10**6, 14 * MIB),
    )(tab, *picked, gain, *weights)


def place_kernel(tab, own, right, left, far_a, far_b, out, scale, sems):
    copies = []
    for j in range(4):
        at = pl.ds(j * 512, 512)

        def columns(i2):
            return pl.ds(pl.multiple_of(tab[i2 * 4 + j] * 512, 512), 512)

        copies += [
            (own.at[:, at], out.at[:, columns(0)]),
            (right.at[pl.ds(0, 128), at], out.at[:, columns(1)]),
            (left.at[pl.ds(64, 128), at], out.at[:, columns(2)]),
            (far_a.at[:, at], out.at[pl.ds(0, 64), columns(3)]),
            (far_b.at[:, at], out.at[pl.ds(64, 64), columns(3)]),
        ]
    copies = [pltpu.make_async_copy(a, b, sems.at[i]) for i, (a, b) in enumerate(copies)]
    for copy in copies:
        copy.start()

    def squares(values):
        values = values.astype(F32)
        return jnp.sum(values * values, axis=1, keepdims=True)

    far = jnp.concatenate([squares(far_a[...]), squares(far_b[...])], axis=0)
    total = squares(own[...]) + squares(right[0:128]) + squares(left[64:192]) + far
    scale[...] = jnp.broadcast_to(lax.rsqrt(total * (1.0 / 8192.0) + 1e-06), (128, 128))
    for copy in copies:
        copy.wait()


def place_rows(tab, pieces):
    return pl.pallas_call(
        place_kernel,
        out_shape=[jax.ShapeDtypeStruct((128, 8192), BF16), jax.ShapeDtypeStruct((128, 128), F32)],
        in_specs=[SMEM] + [VMEM] * 5,
        out_specs=[ANY, VMEM],
        scratch_shapes=[pltpu.SemaphoreType.DMA((20,))],
        compiler_params=params(32),
        cost_estimate=cost(4 * 10**6, 5 * MIB),
    )(tab, *pieces)


def per_device(
    patches,
    patch_counts,
    dest_pos,
    merge_gain,
    merge_bias,
    up_weight,
    up_bias,
    down_weight,
    down_bias,
    text_embed,
    norm_gain,
    kv_weight,
    kv_bias,
):
    tab = jnp.asarray(TABLE)[lax.axis_index("mb") * 16 + lax.axis_index("tp")]
    stack = jnp.asarray(STACK)[lax.axis_index("enc") * 2 + lax.axis_index("mb")]

    def climb(value):
        return lax.ppermute(value, ("enc", "mb"), CLIMB)

    def cross(value):
        return lax.ppermute(value, "mb", OTHER)

    up_other = cross(up_weight)
    merged = merge(after(patches[0, 0], up_other), merge_gain, merge_bias)
    down_part = lax.ppermute(down_weight, ("enc", "mb", "tp"), SHUFFLE)
    climbed = [climb(jnp.stack([up_weight, up_other]))]
    right, left = hop(merged, 1, 1), hop(merged, 1, -1)

    right, left, down_part = lax.optimization_barrier((right, left, down_part, climbed[0]))[:3]
    climbed.append(climb(climbed[0]))
    down_part = lax.ppermute(down_part, ("enc", "mb", "tp"), TURN)
    far = jnp.concatenate([hop(right[:, :2560], 1, 1), hop(left[:, 2560:], 1, -1)], axis=1)
    near = jnp.concatenate([merged, right, left, far], axis=0)

    kv_right, kv_left = hop(kv_weight, 1, 1), hop(kv_weight, 1, -1)
    near, down_part = lax.optimization_barrier((near, down_part, climbed[1], kv_right, kv_left))[:2]
    climbed.append(climb(climbed[1]))
    down_full = lax.all_gather(down_part, ("enc", "mb"), axis=0, tiled=True)
    right, left = hop(near, 2, 1), hop(near, 2, -1)

    right, left = lax.optimization_barrier((right, left, climbed[2]))[:2]
    climbed.append(climb(climbed[2][:1]))
    group = (near, right, left, hop(right[:32], 2, 1), hop(left[32:], 2, -1))
    up_weights = (up_weight, up_other, *climbed, *[cross(value) for value in climbed])
    weights = (kv_weight, kv_right, kv_left, hop(kv_right[:256], 1, 1), hop(kv_left[256:], 1, -1))

    hidden = up(tab, stack, group, up_weights, up_bias.reshape(16, 1, 320))
    right, left, far_a, far_b = ring(hidden, 1)
    text_right, text_left, text_own = pack(tab, text_embed[0, 0])
    text_right = hop(after(text_right, right, left), 2, 1)
    text_left = hop(after(text_left, right, left), 2, -1)
    text = (text_own, text_right, text_left, hop(text_right[128:192], 2, 1), hop(text_left[0:64], 2, -1))
    near = jnp.concatenate([hidden, right, left, jnp.concatenate([far_a, far_b], axis=0)], axis=1)
    units = (near, *ring(after(near, text[1], text[2]), 2))
    down_full = after(down_full, weights[3], weights[4])
    visual = down(tab, units, down_full, down_bias.reshape(16, 1, 512))
    visual = (visual, *ring(visual, 1))

    live_rows = patch_counts[0, 0] // 4
    live = (jnp.arange(SLOT, dtype=jnp.int32)[None, :] < live_rows[:, None]).reshape(-1)
    dest = jnp.where(live, dest_pos[0, 0], -1)[None]
    to_right, to_left, kept = pick(tab, dest, visual, text)
    right = hop(to_right, 2, 1)
    left = hop(to_left, 2, -1)
    pieces = (kept, right, left, hop(right[128:192], 2, 1), hop(left[0:64], 2, -1))

    far_a, far_b, to_right, to_left, own = product(
        tab, (to_right, to_left, kept), norm_gain.reshape(16, 1, 512), weights
    )
    far_a = hop(far_a, 2, 1).astype(F32)
    far_b = hop(far_b, 2, -1).astype(F32)
    to_right, to_left = to_right.astype(F32), to_left.astype(F32)
    to_right = jnp.concatenate([to_right[:64] + far_a, to_right[64:]], axis=0).astype(BF16)
    to_left = jnp.concatenate([to_left[:64], to_left[64:] + far_b], axis=0).astype(BF16)
    right = hop(to_right, 2, 1).astype(F32)
    left = hop(to_left, 2, -1).astype(F32)
    embedded, scale = place_rows(tab, pieces)
    keys_values = ((own + right + left) * scale[:, :1] + kv_bias).astype(BF16)
    return (embedded[None, None], keys_values[None, None])


def solution(mesh):
    return jax.shard_map(
        per_device,
        mesh=mesh,
        in_specs=(
            P("enc", "mb", "tp", None),
            P("enc", "mb", None),
            P("enc", "mb", None),
            P(),
            P(),
            P(("enc", "mb"), "tp"),
            P(),
            P("tp", ("enc", "mb")),
            P(),
            P("enc", "mb", "tp", None),
            P(),
            P("tp", None),
            P(),
        ),
        out_specs=(P("enc", "mb", "tp", None), P("enc", "mb", "tp", None)),
        check_vma=False,
    )
```

```python
import jax
import jax.numpy as jnp
import numpy as np
from jax import lax
from jax.experimental import pallas as pl
from jax.experimental.pallas import tpu as pltpu
from jax.sharding import PartitionSpec as P

SLOT = 8
RING = (0, -1, 1, 2)
MIB = 1 << 20
BF16, F32 = jnp.bfloat16, jnp.float32


def place(core, tp, which, step):
    y, x = tp // 4, tp % 4
    if (core == 0) == (which == 1):
        return y * 4 + (x + step) % 4
    return (y + step) % 4 * 4 + x


TABLE = np.array(
    [
        [place(core, place(core, tp, 2, o2), 1, o1) for o2 in RING for o1 in RING]
        for core in range(2)
        for tp in range(16)
    ],
    np.int32,
)
HOPS = {
    (which, step): [(c * 16 + t, c * 16 + place(c, t, which, step)) for c in range(2) for t in range(16)]
    for which in (1, 2)
    for step in (1, -1, 2)
}
SHUFFLE = [(a * 16 + b, (a ^ b) * 16 + b) for a in range(16) for b in range(16)]
TURN = [(a * 16 + b, a * 16 + (a ^ b)) for a in range(16) for b in range(16)]


def hop(value, which, step):
    return lax.ppermute(value, ("mb", "tp"), HOPS[which, step])


def around(value, which):
    return hop(value, which, 1), hop(value, which, -1), hop(value, which, 2)


def after(value, *others):
    return lax.optimization_barrier((value, *others))[0]


def cost(flops, moved):
    return pl.CostEstimate(flops=flops, bytes_accessed=moved, transcendentals=0)


def params(mib):
    return pltpu.CompilerParams(vmem_limit_bytes=mib * MIB)


VMEM = pl.BlockSpec(memory_space=pltpu.VMEM)
SMEM = pl.BlockSpec(memory_space=pltpu.SMEM)
ANY = pl.BlockSpec(memory_space=pl.ANY)
HBM = pl.BlockSpec(memory_space=pltpu.HBM)


def merge_kernel(p_ref, gain_ref, bias_ref, out_ref, rows):
    values = p_ref[...].astype(F32)
    center = values - jnp.mean(values, axis=-1, keepdims=True)
    spread = jnp.mean(center * center, axis=-1, keepdims=True)
    normal = center * lax.rsqrt(spread + 1e-06) * gain_ref[...].reshape(1, 1280) + bias_ref[...].reshape(1, 1280)
    for k in range(10):
        rows[k] = normal[:, k * 128 : (k + 1) * 128]
    for j in range(4):
        for k in range(10):
            start = j * 1280 + k * 128
            out_ref[:, start : start + 128] = rows[k, pl.ds(j, 16, stride=4), :].astype(BF16)


def merge(patches, gain, bias):
    return pl.pallas_call(
        merge_kernel,
        out_shape=jax.ShapeDtypeStruct((16, 5120), BF16),
        in_specs=[VMEM] * 3,
        out_specs=VMEM,
        scratch_shapes=[pltpu.VMEM((10, 64, 128), F32)],
        compiler_params=params(8),
        cost_estimate=cost(10**6, 330000),
    )(patches, gain, bias)


def pack_kernel(tab, *refs):
    for source, target in zip(refs[:4], refs[4:]):
        target[...] = source[...]


def pack(tab, text):
    def columns(i2):
        return pl.BlockSpec((128, 512), lambda j, tab: (0, tab[i2 * 4 + j]))

    return pl.pallas_call(
        pack_kernel,
        out_shape=[jax.ShapeDtypeStruct((128, 2048), BF16)] * 4,
        grid_spec=pltpu.PrefetchScalarGridSpec(
            num_scalar_prefetch=1,
            grid=(4,),
            in_specs=[columns(i2) for i2 in range(4)],
            out_specs=[pl.BlockSpec((128, 512), lambda j, tab: (0, j))] * 4,
        ),
        compiler_params=params(8),
        cost_estimate=cost(0, 4 * MIB),
    )(tab, text, text, text, text)


def start(copies, sems):
    copies = [pltpu.make_async_copy(a, b, sems.at[i]) for i, (a, b) in enumerate(copies)]
    for copy in copies:
        copy.start()
    return copies


def up_kernel(tab, s0, s1, s2, s3, weight, bias_ref, out_ref, rows, held, sems):
    copies = [(piece, rows.at[pl.ds(i * 64, 64)]) for i, piece in enumerate((s0, s1, s2, s3))]
    copies += [(weight.at[pl.ds(k * 1024, 1024)], held.at[pl.ds(k * 1024, 1024)]) for k in range(5)]
    copies = start(copies, sems)
    for copy in copies[:4]:
        copy.wait()
    raised = bias_ref[tab[0]]
    for k in range(5):
        copies[4 + k].wait()
        at = slice(k * 1024, (k + 1) * 1024)
        raised = raised + jnp.dot(rows[:, at], held[at, :], preferred_element_type=F32)
    hidden = (0.5 * raised * (1.0 + lax.erf(raised * np.float32(0.5**0.5)))).astype(BF16)
    for k in range(16):
        out_ref[pl.ds(pl.multiple_of(tab[k] * 16, 16), 16), :] = hidden[k * 16 : (k + 1) * 16]


def up(tab, pieces, weight, bias):
    return pl.pallas_call(
        up_kernel,
        out_shape=jax.ShapeDtypeStruct((256, 320), BF16),
        in_specs=[SMEM] + [ANY] * 5 + [VMEM],
        out_specs=VMEM,
        scratch_shapes=[
            pltpu.VMEM((256, 5120), BF16),
            pltpu.VMEM((5120, 320), BF16),
            pltpu.SemaphoreType.DMA((9,)),
        ],
        compiler_params=params(56),
        cost_estimate=cost(840 * 10**6, 6 * MIB),
    )(tab, *pieces, weight, bias)


def down_kernel(tab, h0, h1, h2, h3, weight, bias_ref, out_ref, units, held, sems):
    copies = []
    for i2, piece in enumerate((h0, h1, h2, h3)):
        copies.append((piece, units.at[i2]))
        for i1 in range(4):
            k = i2 * 4 + i1
            source = weight.at[pl.ds(pl.multiple_of((tab[k] ^ tab[0]) * 320, 320), 320)]
            copies.append((source, held.at[pl.ds(k * 320, 320)]))
    copies = start(copies, sems)
    total = bias_ref[tab[0]]
    for i2 in range(4):
        for copy in copies[i2 * 5 : i2 * 5 + 5]:
            copy.wait()
        total = total + jnp.dot(units[i2], held[i2 * 1280 : (i2 + 1) * 1280, :], preferred_element_type=F32)
    out_ref[...] = total.astype(BF16)


def down(tab, pieces, weight, bias):
    return pl.pallas_call(
        down_kernel,
        out_shape=jax.ShapeDtypeStruct((256, 512), BF16),
        in_specs=[SMEM] + [ANY] * 5 + [VMEM],
        out_specs=VMEM,
        scratch_shapes=[
            pltpu.VMEM((4, 256, 1280), BF16),
            pltpu.VMEM((5120, 512), BF16),
            pltpu.SemaphoreType.DMA((20,)),
        ],
        compiler_params=params(56),
        cost_estimate=cost(1340 * 10**6, 8 * MIB),
    )(tab, *pieces, weight, bias)


def pick_kernel(tab, dest, v0, v1, v2, v3, *refs):
    visual = (v0[...], v1[...], v2[...], v3[...])
    targets = dest[...]
    for i2 in (3, 2, 1, 0):
        text, out = refs[i2], refs[4 + i2]
        match = (lax.broadcasted_iota(jnp.int32, (128, 256), 0) + tab[i2 * 4] * 128) == targets
        select = match.astype(F32)
        present = jnp.sum(select, axis=1, keepdims=True) > 0.0
        select = select.astype(BF16)
        for j in range(4):
            at = slice(j * 512, (j + 1) * 512)
            picked = jnp.dot(select, visual[j], preferred_element_type=F32).astype(BF16)
            out[:, at] = jnp.where(present, picked, text[:, at])


def pick(tab, dest, visual, text):
    return pl.pallas_call(
        pick_kernel,
        out_shape=[jax.ShapeDtypeStruct((128, 2048), BF16)] * 4,
        in_specs=[SMEM] + [VMEM] * 9,
        out_specs=[VMEM] * 4,
        compiler_params=params(32),
        cost_estimate=cost(540 * 10**6, 6 * MIB),
    )(tab, dest, *visual, *text)


def product_kernel(tab, e0, e1, e2, e3, gain, w0, w1, w2, w3a, w3b, own, left, right, far, scaled):
    @pl.when(pl.program_id(0) == 0)
    def _():
        for j in range(4):
            at = slice(j * 512, (j + 1) * 512)
            scale = gain[tab[j]]
            for i2, rows in enumerate((e0, e1, e2, e3)):
                scaled[i2 * 128 : (i2 + 1) * 128, at] = (rows[:, at].astype(F32) * scale).astype(BF16)

    total = jnp.dot(scaled[:, 0:512], w0[...], preferred_element_type=F32)
    total = total + jnp.dot(scaled[:, 512:1024], w1[...], preferred_element_type=F32)
    total = total + jnp.dot(scaled[:, 1024:1536], w2[...], preferred_element_type=F32)
    total = total + jnp.dot(scaled[:, 1536:1792], w3a[...], preferred_element_type=F32)
    total = total + jnp.dot(scaled[:, 1792:2048], w3b[...], preferred_element_type=F32)
    own[...] = total[0:128]
    left[...] = total[128:256].astype(BF16)
    right[...] = total[256:384].astype(BF16)
    far[...] = total[384:512].astype(BF16)


def product(tab, picked, gain, weights):
    def block(count):
        return pl.BlockSpec((count, 512), lambda n: (0, n))

    return pl.pallas_call(
        product_kernel,
        out_shape=[jax.ShapeDtypeStruct((128, 2048), F32)] + [jax.ShapeDtypeStruct((128, 2048), BF16)] * 3,
        grid=(4,),
        in_specs=[SMEM] + [VMEM] * 5 + [block(n) for n in (512, 512, 512, 256, 256)],
        out_specs=[block(128)] * 4,
        scratch_shapes=[pltpu.VMEM((512, 2048), BF16)],
        compiler_params=params(40),
        cost_estimate=cost(4300 * 10**6, 14 * MIB),
    )(tab, *picked, gain, *weights)


def place_kernel(tab, e0, e1, e2, e3, out, scale, sems):
    copies = []
    for i2, rows in enumerate((e0, e1, e2, e3)):
        for j in range(4):
            columns = pl.ds(pl.multiple_of(tab[i2 * 4 + j] * 512, 512), 512)
            copies.append((rows.at[:, pl.ds(j * 512, 512)], out.at[:, columns]))
    copies = start(copies, sems)
    total = 0.0
    for rows in (e0, e1, e2, e3):
        values = rows[...].astype(F32)
        total = total + jnp.sum(values * values, axis=1, keepdims=True)
    scale[...] = jnp.broadcast_to(lax.rsqrt(total * (1.0 / 8192.0) + 1e-06), (128, 128))
    for copy in copies:
        copy.wait()


def place_rows(tab, pieces):
    return pl.pallas_call(
        place_kernel,
        out_shape=[jax.ShapeDtypeStruct((128, 8192), BF16), jax.ShapeDtypeStruct((128, 128), F32)],
        in_specs=[SMEM] + [VMEM] * 4,
        out_specs=[ANY, VMEM],
        scratch_shapes=[pltpu.SemaphoreType.DMA((16,))],
        compiler_params=params(32),
        cost_estimate=cost(4 * 10**6, 30 * MIB),
    )(tab, *pieces)


def per_device(
    patches,
    patch_counts,
    dest_pos,
    merge_gain,
    merge_bias,
    up_weight,
    up_bias,
    down_weight,
    down_bias,
    text_embed,
    norm_gain,
    kv_weight,
    kv_bias,
):
    tab = jnp.asarray(TABLE)[lax.axis_index("mb") * 16 + lax.axis_index("tp")]
    up_full = lax.all_gather(up_weight, ("enc", "mb"), axis=0, tiled=True)
    down_part = lax.ppermute(down_weight, ("enc", "mb", "tp"), SHUFFLE)

    merged = merge(patches[0, 0], merge_gain, merge_bias)
    near = jnp.concatenate([merged, *around(merged, 1)], axis=0)
    down_part = lax.ppermute(after(down_part, near), ("enc", "mb", "tp"), TURN)
    group = (near, *around(near, 2))
    down_full = lax.all_gather(after(down_part, *group), ("enc", "mb"), axis=0, tiled=True)

    kv_weight = after(kv_weight, near)
    kv_right, kv_left = hop(kv_weight, 1, 1), hop(kv_weight, 1, -1)
    own, to_left, to_right, to_far = pack(tab, text_embed[0, 0])
    text = (own, hop(to_right, 2, 1), hop(to_left, 2, -1), hop(to_far, 2, 2))

    up_full = after(up_full, kv_right, kv_left, *text)
    hidden = up(tab, group, up_full, up_bias.reshape(16, 1, 320))
    near = jnp.concatenate([hidden, *around(hidden, 1)], axis=1)
    right, left = lax.optimization_barrier((kv_right, kv_left, near))[:2]
    weights = (kv_weight, kv_right, kv_left, hop(right[:256], 1, 1), hop(left[256:], 1, -1))
    units = (near, *around(near, 2))
    down_full = after(down_full, weights[3], weights[4])
    visual = down(tab, units, down_full, down_bias.reshape(16, 1, 512))
    visual = (visual, *around(visual, 1))

    live_rows = patch_counts[0, 0] // 4
    live = (jnp.arange(SLOT, dtype=jnp.int32)[None, :] < live_rows[:, None]).reshape(-1)
    dest = jnp.where(live, dest_pos[0, 0], -1)[None]
    picked = pick(tab, dest, visual, text)
    pieces = (picked[0], hop(picked[2], 2, 1), hop(picked[1], 2, -1), hop(picked[3], 2, 2))
    own, to_left, to_right, to_far = product(tab, picked, norm_gain.reshape(16, 1, 512), weights)
    sums = (hop(to_far, 2, 2), hop(to_right, 2, 1), hop(to_left, 2, -1))
    embedded, scale = place_rows(tab, pieces)
    total = own
    for value in sums:
        total = total + value.astype(F32)
    keys_values = (total * scale[:, :1] + kv_bias).astype(BF16)
    return (embedded[None, None], keys_values[None, None])


def solution(mesh):
    return jax.shard_map(
        per_device,
        mesh=mesh,
        in_specs=(
            P("enc", "mb", "tp", None),
            P("enc", "mb", None),
            P("enc", "mb", None),
            P(),
            P(),
            P(("enc", "mb"), "tp"),
            P(),
            P("tp", ("enc", "mb")),
            P(),
            P("enc", "mb", "tp", None),
            P(),
            P("tp", None),
            P(),
        ),
        out_specs=(P("enc", "mb", "tp", None), P("enc", "mb", "tp", None)),
        check_vma=False,
    )
```

```python
import jax
import jax.numpy as jnp
import numpy as np
from jax import lax
from jax.experimental import pallas as pl
from jax.experimental.pallas import tpu as pltpu
from jax.sharding import PartitionSpec as P

SLOT = 8
RING = (0, -1, 1, 2)
MIB = 1 << 20
BF16, F32 = jnp.bfloat16, jnp.float32


def place(core, tp, which, step):
    y, x = tp // 4, tp % 4
    if (core == 0) == (which == 1):
        return y * 4 + (x + step) % 4
    return (y + step) % 4 * 4 + x


TABLE = np.array(
    [
        [place(core, place(core, tp, 2, o2), 1, o1) for o2 in RING for o1 in RING]
        for core in range(2)
        for tp in range(16)
    ],
    np.int32,
)
HOPS = {
    (which, step): [(c * 16 + t, c * 16 + place(c, t, which, step)) for c in range(2) for t in range(16)]
    for which in (1, 2)
    for step in (1, -1, 2)
}
SHUFFLE = [(a * 16 + b, (a ^ b) * 16 + b) for a in range(16) for b in range(16)]
TURN = [(a * 16 + b, a * 16 + (a ^ b)) for a in range(16) for b in range(16)]


def hop(value, which, step):
    return lax.ppermute(value, ("mb", "tp"), HOPS[which, step])


def around(value, which):
    return hop(value, which, 1), hop(value, which, -1), hop(value, which, 2)


def after(value, *others):
    return lax.optimization_barrier((value, *others))[0]


def cost(flops, moved):
    return pl.CostEstimate(flops=flops, bytes_accessed=moved, transcendentals=0)


def params(mib):
    return pltpu.CompilerParams(vmem_limit_bytes=mib * MIB)


VMEM = pl.BlockSpec(memory_space=pltpu.VMEM)
SMEM = pl.BlockSpec(memory_space=pltpu.SMEM)
ANY = pl.BlockSpec(memory_space=pl.ANY)
HBM = pl.BlockSpec(memory_space=pltpu.HBM)


def merge_kernel(p_ref, gain_ref, bias_ref, out_ref, rows):
    values = p_ref[...].astype(F32)
    center = values - jnp.mean(values, axis=-1, keepdims=True)
    spread = jnp.mean(center * center, axis=-1, keepdims=True)
    normal = center * lax.rsqrt(spread + 1e-06) * gain_ref[...].reshape(1, 1280) + bias_ref[...].reshape(1, 1280)
    for k in range(10):
        rows[k] = normal[:, k * 128 : (k + 1) * 128]
    for j in range(4):
        for k in range(10):
            start = j * 1280 + k * 128
            out_ref[:, start : start + 128] = rows[k, pl.ds(j, 16, stride=4), :].astype(BF16)


def merge(patches, gain, bias):
    return pl.pallas_call(
        merge_kernel,
        out_shape=jax.ShapeDtypeStruct((16, 5120), BF16),
        in_specs=[VMEM] * 3,
        out_specs=VMEM,
        scratch_shapes=[pltpu.VMEM((10, 64, 128), F32)],
        compiler_params=params(8),
        cost_estimate=cost(10**6, 330000),
    )(patches, gain, bias)


def pack_kernel(tab, *refs):
    for source, target in zip(refs[:4], refs[4:]):
        target[...] = source[...]


def pack(tab, text):
    def columns(i2):
        return pl.BlockSpec((128, 512), lambda j, tab: (0, tab[i2 * 4 + j]))

    return pl.pallas_call(
        pack_kernel,
        out_shape=[jax.ShapeDtypeStruct((128, 2048), BF16)] * 4,
        grid_spec=pltpu.PrefetchScalarGridSpec(
            num_scalar_prefetch=1,
            grid=(4,),
            in_specs=[columns(i2) for i2 in range(4)],
            out_specs=[pl.BlockSpec((128, 512), lambda j, tab: (0, j))] * 4,
        ),
        compiler_params=params(8),
        cost_estimate=cost(0, 4 * MIB),
    )(tab, text, text, text, text)


def start(copies, sems):
    copies = [pltpu.make_async_copy(a, b, sems.at[i]) for i, (a, b) in enumerate(copies)]
    for copy in copies:
        copy.start()
    return copies


def up_kernel(tab, s0, s1, s2, s3, weight, bias_ref, out_ref, rows, held, sems):
    copies = [(piece, rows.at[pl.ds(i * 64, 64)]) for i, piece in enumerate((s0, s1, s2, s3))]
    copies += [(weight.at[pl.ds(k * 1024, 1024)], held.at[pl.ds(k * 1024, 1024)]) for k in range(5)]
    copies = start(copies, sems)
    for copy in copies[:4]:
        copy.wait()
    raised = bias_ref[tab[0]]
    for k in range(5):
        copies[4 + k].wait()
        at = slice(k * 1024, (k + 1) * 1024)
        raised = raised + jnp.dot(rows[:, at], held[at, :], preferred_element_type=F32)
    hidden = (0.5 * raised * (1.0 + lax.erf(raised * np.float32(0.5**0.5)))).astype(BF16)
    for k in range(16):
        out_ref[pl.ds(pl.multiple_of(tab[k] * 16, 16), 16), :] = hidden[k * 16 : (k + 1) * 16]


def up(tab, pieces, weight, bias):
    return pl.pallas_call(
        up_kernel,
        out_shape=jax.ShapeDtypeStruct((256, 320), BF16),
        in_specs=[SMEM] + [ANY] * 5 + [VMEM],
        out_specs=VMEM,
        scratch_shapes=[
            pltpu.VMEM((256, 5120), BF16),
            pltpu.VMEM((5120, 320), BF16),
            pltpu.SemaphoreType.DMA((9,)),
        ],
        compiler_params=params(56),
        cost_estimate=cost(840 * 10**6, 6 * MIB),
    )(tab, *pieces, weight, bias)


def down_kernel(tab, h0, h1, h2, h3, weight, bias_ref, out_ref, units, held, sems):
    copies = []
    for i2, piece in enumerate((h0, h1, h2, h3)):
        copies.append((piece, units.at[i2]))
        for i1 in range(4):
            k = i2 * 4 + i1
            source = weight.at[pl.ds(pl.multiple_of((tab[k] ^ tab[0]) * 320, 320), 320)]
            copies.append((source, held.at[pl.ds(k * 320, 320)]))
    copies = start(copies, sems)
    total = bias_ref[tab[0]]
    for i2 in range(4):
        for copy in copies[i2 * 5 : i2 * 5 + 5]:
            copy.wait()
        total = total + jnp.dot(units[i2], held[i2 * 1280 : (i2 + 1) * 1280, :], preferred_element_type=F32)
    out_ref[...] = total.astype(BF16)


def down(tab, pieces, weight, bias):
    return pl.pallas_call(
        down_kernel,
        out_shape=jax.ShapeDtypeStruct((256, 512), BF16),
        in_specs=[SMEM] + [ANY] * 5 + [VMEM],
        out_specs=VMEM,
        scratch_shapes=[
            pltpu.VMEM((4, 256, 1280), BF16),
            pltpu.VMEM((5120, 512), BF16),
            pltpu.SemaphoreType.DMA((20,)),
        ],
        compiler_params=params(56),
        cost_estimate=cost(1340 * 10**6, 8 * MIB),
    )(tab, *pieces, weight, bias)


def pick_kernel(tab, dest, v0, v1, v2, v3, *refs):
    visual = (v0[...], v1[...], v2[...], v3[...])
    targets = dest[...]
    for i2 in (3, 2, 1, 0):
        text, out = refs[i2], refs[4 + i2]
        match = (lax.broadcasted_iota(jnp.int32, (128, 256), 0) + tab[i2 * 4] * 128) == targets
        select = match.astype(F32)
        present = jnp.sum(select, axis=1, keepdims=True) > 0.0
        select = select.astype(BF16)
        for j in range(4):
            at = slice(j * 512, (j + 1) * 512)
            picked = jnp.dot(select, visual[j], preferred_element_type=F32).astype(BF16)
            out[:, at] = jnp.where(present, picked, text[:, at])


def pick(tab, dest, visual, text):
    return pl.pallas_call(
        pick_kernel,
        out_shape=[jax.ShapeDtypeStruct((128, 2048), BF16)] * 4,
        in_specs=[SMEM] + [VMEM] * 9,
        out_specs=[VMEM] * 4,
        compiler_params=params(32),
        cost_estimate=cost(540 * 10**6, 6 * MIB),
    )(tab, dest, *visual, *text)


def product_kernel(tab, e0, e1, e2, e3, gain, w0, w1, w2, w3a, w3b, own, left, right, far, scaled):
    @pl.when(pl.program_id(0) == 0)
    def _():
        for j in range(4):
            at = slice(j * 512, (j + 1) * 512)
            scale = gain[tab[j]]
            for i2, rows in enumerate((e0, e1, e2, e3)):
                scaled[i2 * 128 : (i2 + 1) * 128, at] = (rows[:, at].astype(F32) * scale).astype(BF16)

    total = jnp.dot(scaled[:, 0:512], w0[...], preferred_element_type=F32)
    total = total + jnp.dot(scaled[:, 512:1024], w1[...], preferred_element_type=F32)
    total = total + jnp.dot(scaled[:, 1024:1536], w2[...], preferred_element_type=F32)
    total = total + jnp.dot(scaled[:, 1536:1792], w3a[...], preferred_element_type=F32)
    total = total + jnp.dot(scaled[:, 1792:2048], w3b[...], preferred_element_type=F32)
    own[...] = total[0:128]
    left[...] = total[128:256].astype(BF16)
    right[...] = total[256:384].astype(BF16)
    far[...] = total[384:512].astype(BF16)


def product(tab, picked, gain, weights):
    def block(count):
        return pl.BlockSpec((count, 512), lambda n: (0, n))

    return pl.pallas_call(
        product_kernel,
        out_shape=[jax.ShapeDtypeStruct((128, 2048), F32)] + [jax.ShapeDtypeStruct((128, 2048), BF16)] * 3,
        grid=(4,),
        in_specs=[SMEM] + [VMEM] * 5 + [block(n) for n in (512, 512, 512, 256, 256)],
        out_specs=[block(128)] * 4,
        scratch_shapes=[pltpu.VMEM((512, 2048), BF16)],
        compiler_params=params(40),
        cost_estimate=cost(4300 * 10**6, 14 * MIB),
    )(tab, *picked, gain, *weights)


def place_kernel(tab, e0, e1, e2, e3, out, scale, sems):
    copies = []
    for i2, rows in enumerate((e0, e1, e2, e3)):
        for j in range(4):
            columns = pl.ds(pl.multiple_of(tab[i2 * 4 + j] * 512, 512), 512)
            copies.append((rows.at[:, pl.ds(j * 512, 512)], out.at[:, columns]))
    copies = start(copies, sems)
    total = 0.0
    for rows in (e0, e1, e2, e3):
        values = rows[...].astype(F32)
        total = total + jnp.sum(values * values, axis=1, keepdims=True)
    scale[...] = jnp.broadcast_to(lax.rsqrt(total * (1.0 / 8192.0) + 1e-06), (128, 128))
    for copy in copies:
        copy.wait()


def place_rows(tab, pieces):
    return pl.pallas_call(
        place_kernel,
        out_shape=[jax.ShapeDtypeStruct((128, 8192), BF16), jax.ShapeDtypeStruct((128, 128), F32)],
        in_specs=[SMEM] + [VMEM] * 4,
        out_specs=[ANY, VMEM],
        scratch_shapes=[pltpu.SemaphoreType.DMA((16,))],
        compiler_params=params(32),
        cost_estimate=cost(4 * 10**6, 30 * MIB),
    )(tab, *pieces)


def per_device(
    patches,
    patch_counts,
    dest_pos,
    merge_gain,
    merge_bias,
    up_weight,
    up_bias,
    down_weight,
    down_bias,
    text_embed,
    norm_gain,
    kv_weight,
    kv_bias,
):
    tab = jnp.asarray(TABLE)[lax.axis_index("mb") * 16 + lax.axis_index("tp")]
    up_full = lax.all_gather(up_weight, ("enc", "mb"), axis=0, tiled=True)
    down_part = lax.ppermute(down_weight, ("enc", "mb", "tp"), SHUFFLE)

    merged = merge(patches[0, 0], merge_gain, merge_bias)
    near = jnp.concatenate([merged, *around(merged, 1)], axis=0)
    down_part = lax.ppermute(after(down_part, near), ("enc", "mb", "tp"), TURN)
    group = (near, *around(near, 2))
    kv_weight = after(kv_weight, near)
    kv_right, kv_left = hop(kv_weight, 1, 1), hop(kv_weight, 1, -1)
    down_part = after(down_part, *group, kv_right, kv_left)
    down_full = lax.all_gather(down_part, ("enc", "mb"), axis=0, tiled=True)
    far_right, far_left = kv_right[:256], kv_left[256:]

    up_full, far_right, far_left = lax.optimization_barrier((up_full, far_right, far_left))
    hidden = up(tab, group, up_full, up_bias.reshape(16, 1, 320))
    near = jnp.concatenate([hidden, *around(hidden, 1)], axis=1)
    far_right, far_left = lax.optimization_barrier((far_right, far_left, near))[:2]
    weights = (kv_weight, kv_right, kv_left, hop(far_right, 1, 1), hop(far_left, 1, -1))
    own, to_left, to_right, to_far = pack(tab, text_embed[0, 0])
    units = (near, *around(near, 2))
    to_left, to_right, to_far = lax.optimization_barrier((to_left, to_right, to_far, *units[1:3]))[:3]
    text = (own, hop(to_right, 2, 1), hop(to_left, 2, -1), hop(to_far, 2, 2))
    down_full = after(down_full, weights[3], weights[4], *text)
    visual = down(tab, units, down_full, down_bias.reshape(16, 1, 512))
    visual = (visual, *around(visual, 1))

    live_rows = patch_counts[0, 0] // 4
    live = (jnp.arange(SLOT, dtype=jnp.int32)[None, :] < live_rows[:, None]).reshape(-1)
    dest = jnp.where(live, dest_pos[0, 0], -1)[None]
    picked = pick(tab, dest, visual, text)
    pieces = (picked[0], hop(picked[2], 2, 1), hop(picked[1], 2, -1), hop(picked[3], 2, 2))
    own, to_left, to_right, to_far = product(tab, picked, norm_gain.reshape(16, 1, 512), weights)
    sums = (hop(to_far, 2, 2), hop(to_right, 2, 1), hop(to_left, 2, -1))
    embedded, scale = place_rows(tab, pieces)
    total = own
    for value in sums:
        total = total + value.astype(F32)
    keys_values = (total * scale[:, :1] + kv_bias).astype(BF16)
    return (embedded[None, None], keys_values[None, None])


def solution(mesh):
    return jax.shard_map(
        per_device,
        mesh=mesh,
        in_specs=(
            P("enc", "mb", "tp", None),
            P("enc", "mb", None),
            P("enc", "mb", None),
            P(),
            P(),
            P(("enc", "mb"), "tp"),
            P(),
            P("tp", ("enc", "mb")),
            P(),
            P("enc", "mb", "tp", None),
            P(),
            P("tp", None),
            P(),
        ),
        out_specs=(P("enc", "mb", "tp", None), P("enc", "mb", "tp", None)),
        check_vma=False,
    )
```

```python
import jax
import jax.numpy as jnp
import numpy as np
from jax import lax
from jax.experimental import pallas as pl
from jax.experimental.pallas import tpu as pltpu
from jax.sharding import PartitionSpec as P

SLOT = 8
RING = (0, -1, 1, 2)
MIB = 1 << 20
BF16, F32 = jnp.bfloat16, jnp.float32


def place(core, tp, which, step):
    y, x = tp // 4, tp % 4
    if (core == 0) == (which == 1):
        return y * 4 + (x + step) % 4
    return (y + step) % 4 * 4 + x


TABLE = np.array(
    [
        [place(core, place(core, tp, 2, o2), 1, o1) for o2 in RING for o1 in RING]
        for core in range(2)
        for tp in range(16)
    ],
    np.int32,
)
HOPS = {
    (which, step): [(c * 16 + t, c * 16 + place(c, t, which, step)) for c in range(2) for t in range(16)]
    for which in (1, 2)
    for step in (1, -1, 2)
}
SHUFFLE = [(a * 16 + b, (a ^ b) * 16 + b) for a in range(16) for b in range(16)]
TURN = [(a * 16 + b, a * 16 + (a ^ b)) for a in range(16) for b in range(16)]


def hop(value, which, step):
    return lax.ppermute(value, ("mb", "tp"), HOPS[which, step])


def around(value, which):
    return hop(value, which, 1), hop(value, which, -1), hop(value, which, 2)


def after(value, *others):
    return lax.optimization_barrier((value, *others))[0]


def cost(flops, moved):
    return pl.CostEstimate(flops=flops, bytes_accessed=moved, transcendentals=0)


def params(mib):
    return pltpu.CompilerParams(vmem_limit_bytes=mib * MIB)


VMEM = pl.BlockSpec(memory_space=pltpu.VMEM)
SMEM = pl.BlockSpec(memory_space=pltpu.SMEM)
ANY = pl.BlockSpec(memory_space=pl.ANY)
HBM = pl.BlockSpec(memory_space=pltpu.HBM)


def merge_kernel(p_ref, gain_ref, bias_ref, out_ref, rows):
    values = p_ref[...].astype(F32)
    center = values - jnp.mean(values, axis=-1, keepdims=True)
    spread = jnp.mean(center * center, axis=-1, keepdims=True)
    normal = center * lax.rsqrt(spread + 1e-06) * gain_ref[...].reshape(1, 1280) + bias_ref[...].reshape(1, 1280)
    for k in range(10):
        rows[k] = normal[:, k * 128 : (k + 1) * 128]
    for j in range(4):
        for k in range(10):
            start = j * 1280 + k * 128
            out_ref[:, start : start + 128] = rows[k, pl.ds(j, 16, stride=4), :].astype(BF16)


def merge(patches, gain, bias):
    return pl.pallas_call(
        merge_kernel,
        out_shape=jax.ShapeDtypeStruct((16, 5120), BF16),
        in_specs=[VMEM] * 3,
        out_specs=VMEM,
        scratch_shapes=[pltpu.VMEM((10, 64, 128), F32)],
        compiler_params=params(8),
        cost_estimate=cost(10**6, 330000),
    )(patches, gain, bias)


def pack_kernel(tab, *refs):
    for source, target in zip(refs[:4], refs[4:]):
        target[...] = source[...]


def pack(tab, text):
    def columns(i2):
        return pl.BlockSpec((128, 512), lambda j, tab: (0, tab[i2 * 4 + j]))

    return pl.pallas_call(
        pack_kernel,
        out_shape=[jax.ShapeDtypeStruct((128, 2048), BF16)] * 4,
        grid_spec=pltpu.PrefetchScalarGridSpec(
            num_scalar_prefetch=1,
            grid=(4,),
            in_specs=[columns(i2) for i2 in range(4)],
            out_specs=[pl.BlockSpec((128, 512), lambda j, tab: (0, j))] * 4,
        ),
        compiler_params=params(8),
        cost_estimate=cost(0, 4 * MIB),
    )(tab, text, text, text, text)


def start(copies, sems):
    copies = [pltpu.make_async_copy(a, b, sems.at[i]) for i, (a, b) in enumerate(copies)]
    for copy in copies:
        copy.start()
    return copies


def up_kernel(tab, s0, s1, s2, s3, weight, bias_ref, out_ref, rows, held, sems):
    copies = [(piece, rows.at[pl.ds(i * 64, 64)]) for i, piece in enumerate((s0, s1, s2, s3))]
    copies += [(weight.at[pl.ds(k * 1024, 1024)], held.at[pl.ds(k * 1024, 1024)]) for k in range(5)]
    copies = start(copies, sems)
    for copy in copies[:4]:
        copy.wait()
    raised = bias_ref[tab[0]]
    for k in range(5):
        copies[4 + k].wait()
        at = slice(k * 1024, (k + 1) * 1024)
        raised = raised + jnp.dot(rows[:, at], held[at, :], preferred_element_type=F32)
    hidden = (0.5 * raised * (1.0 + lax.erf(raised * np.float32(0.5**0.5)))).astype(BF16)
    for k in range(16):
        out_ref[pl.ds(pl.multiple_of(tab[k] * 16, 16), 16), :] = hidden[k * 16 : (k + 1) * 16]


def up(tab, pieces, weight, bias):
    return pl.pallas_call(
        up_kernel,
        out_shape=jax.ShapeDtypeStruct((256, 320), BF16),
        in_specs=[SMEM] + [ANY] * 5 + [VMEM],
        out_specs=VMEM,
        scratch_shapes=[
            pltpu.VMEM((256, 5120), BF16),
            pltpu.VMEM((5120, 320), BF16),
            pltpu.SemaphoreType.DMA((9,)),
        ],
        compiler_params=params(56),
        cost_estimate=cost(840 * 10**6, 6 * MIB),
    )(tab, *pieces, weight, bias)


def down_kernel(tab, h0, h1, h2, h3, weight, bias_ref, out_ref, units, held, sems):
    copies = []
    for i2, piece in enumerate((h0, h1, h2, h3)):
        copies.append((piece, units.at[i2]))
        for i1 in range(4):
            k = i2 * 4 + i1
            source = weight.at[pl.ds(pl.multiple_of((tab[k] ^ tab[0]) * 320, 320), 320)]
            copies.append((source, held.at[pl.ds(k * 320, 320)]))
    copies = start(copies, sems)
    total = bias_ref[tab[0]]
    for i2 in range(4):
        for copy in copies[i2 * 5 : i2 * 5 + 5]:
            copy.wait()
        total = total + jnp.dot(units[i2], held[i2 * 1280 : (i2 + 1) * 1280, :], preferred_element_type=F32)
    out_ref[...] = total.astype(BF16)


def down(tab, pieces, weight, bias):
    return pl.pallas_call(
        down_kernel,
        out_shape=jax.ShapeDtypeStruct((256, 512), BF16),
        in_specs=[SMEM] + [ANY] * 5 + [VMEM],
        out_specs=VMEM,
        scratch_shapes=[
            pltpu.VMEM((4, 256, 1280), BF16),
            pltpu.VMEM((5120, 512), BF16),
            pltpu.SemaphoreType.DMA((20,)),
        ],
        compiler_params=params(56),
        cost_estimate=cost(1340 * 10**6, 8 * MIB),
    )(tab, *pieces, weight, bias)


def pick_kernel(tab, dest, v0, v1, v2, v3, *refs):
    visual = (v0[...], v1[...], v2[...], v3[...])
    targets = dest[...]
    for i2 in (3, 2, 1, 0):
        text, out = refs[i2], refs[4 + i2]
        match = (lax.broadcasted_iota(jnp.int32, (128, 256), 0) + tab[i2 * 4] * 128) == targets
        select = match.astype(F32)
        present = jnp.sum(select, axis=1, keepdims=True) > 0.0
        select = select.astype(BF16)
        for j in range(4):
            at = slice(j * 512, (j + 1) * 512)
            picked = jnp.dot(select, visual[j], preferred_element_type=F32).astype(BF16)
            out[:, at] = jnp.where(present, picked, text[:, at])


def pick(tab, dest, visual, text):
    return pl.pallas_call(
        pick_kernel,
        out_shape=[jax.ShapeDtypeStruct((128, 2048), BF16)] * 4,
        in_specs=[SMEM] + [VMEM] * 9,
        out_specs=[VMEM] * 4,
        compiler_params=params(32),
        cost_estimate=cost(540 * 10**6, 6 * MIB),
    )(tab, dest, *visual, *text)


def product_kernel(tab, e0, e1, e2, e3, gain, w0, w1, w2, w3a, w3b, own, left, right, far, scaled):
    @pl.when(pl.program_id(0) == 0)
    def _():
        for j in range(4):
            at = slice(j * 512, (j + 1) * 512)
            scale = gain[tab[j]]
            for i2, rows in enumerate((e0, e1, e2, e3)):
                scaled[i2 * 128 : (i2 + 1) * 128, at] = (rows[:, at].astype(F32) * scale).astype(BF16)

    total = jnp.dot(scaled[:, 0:512], w0[...], preferred_element_type=F32)
    total = total + jnp.dot(scaled[:, 512:1024], w1[...], preferred_element_type=F32)
    total = total + jnp.dot(scaled[:, 1024:1536], w2[...], preferred_element_type=F32)
    total = total + jnp.dot(scaled[:, 1536:1792], w3a[...], preferred_element_type=F32)
    total = total + jnp.dot(scaled[:, 1792:2048], w3b[...], preferred_element_type=F32)
    own[...] = total[0:128]
    left[...] = total[128:256].astype(BF16)
    right[...] = total[256:384].astype(BF16)
    far[...] = total[384:512].astype(BF16)


def product(tab, picked, gain, weights):
    def block(count):
        return pl.BlockSpec((count, 512), lambda n: (0, n))

    return pl.pallas_call(
        product_kernel,
        out_shape=[jax.ShapeDtypeStruct((128, 2048), F32)] + [jax.ShapeDtypeStruct((128, 2048), BF16)] * 3,
        grid=(4,),
        in_specs=[SMEM] + [VMEM] * 5 + [block(n) for n in (512, 512, 512, 256, 256)],
        out_specs=[block(128)] * 4,
        scratch_shapes=[pltpu.VMEM((512, 2048), BF16)],
        compiler_params=params(40),
        cost_estimate=cost(4300 * 10**6, 14 * MIB),
    )(tab, *picked, gain, *weights)


def place_kernel(tab, e0, e1, e2, e3, out, scale, sems):
    copies = []
    for i2, rows in enumerate((e0, e1, e2, e3)):
        for j in range(4):
            columns = pl.ds(pl.multiple_of(tab[i2 * 4 + j] * 512, 512), 512)
            copies.append((rows.at[:, pl.ds(j * 512, 512)], out.at[:, columns]))
    copies = start(copies, sems)
    total = 0.0
    for rows in (e0, e1, e2, e3):
        values = rows[...].astype(F32)
        total = total + jnp.sum(values * values, axis=1, keepdims=True)
    scale[...] = jnp.broadcast_to(lax.rsqrt(total * (1.0 / 8192.0) + 1e-06), (128, 128))
    for copy in copies:
        copy.wait()


def place_rows(tab, pieces):
    return pl.pallas_call(
        place_kernel,
        out_shape=[jax.ShapeDtypeStruct((128, 8192), BF16), jax.ShapeDtypeStruct((128, 128), F32)],
        in_specs=[SMEM] + [VMEM] * 4,
        out_specs=[ANY, VMEM],
        scratch_shapes=[pltpu.SemaphoreType.DMA((16,))],
        compiler_params=params(32),
        cost_estimate=cost(4 * 10**6, 30 * MIB),
    )(tab, *pieces)


def per_device(
    patches,
    patch_counts,
    dest_pos,
    merge_gain,
    merge_bias,
    up_weight,
    up_bias,
    down_weight,
    down_bias,
    text_embed,
    norm_gain,
    kv_weight,
    kv_bias,
):
    tab = jnp.asarray(TABLE)[lax.axis_index("mb") * 16 + lax.axis_index("tp")]
    merged = merge(patches[0, 0], merge_gain, merge_bias)
    down_part = lax.ppermute(down_weight, ("enc", "mb", "tp"), SHUFFLE)
    up_weight = after(up_weight, down_part, merged)
    up_full = lax.all_gather(up_weight, ("enc", "mb"), axis=0, tiled=True)
    down_part = lax.ppermute(down_part, ("enc", "mb", "tp"), TURN)

    near = jnp.concatenate([merged, *around(merged, 1)], axis=0)
    near, kv_weight, down_part = lax.optimization_barrier((near, kv_weight, down_part))
    group = (near, *around(near, 2))
    kv_right, kv_left = hop(kv_weight, 1, 1), hop(kv_weight, 1, -1)
    down_part = after(down_part, *group, kv_right, kv_left)
    down_full = lax.all_gather(down_part, ("enc", "mb"), axis=0, tiled=True)
    far_right, far_left = kv_right[:256], kv_left[256:]

    up_full, far_right, far_left = lax.optimization_barrier((up_full, far_right, far_left))
    hidden = up(tab, group, up_full, up_bias.reshape(16, 1, 320))
    near = jnp.concatenate([hidden, *around(hidden, 1)], axis=1)
    far_right, far_left = lax.optimization_barrier((far_right, far_left, near))[:2]
    weights = (kv_weight, kv_right, kv_left, hop(far_right, 1, 1), hop(far_left, 1, -1))
    own, to_left, to_right, to_far = pack(tab, text_embed[0, 0])
    units = (near, *around(near, 2))
    to_left, to_right, to_far = lax.optimization_barrier((to_left, to_right, to_far, *units))[:3]
    text = (own, hop(to_right, 2, 1), hop(to_left, 2, -1), hop(to_far, 2, 2))
    down_full = after(down_full, weights[3], weights[4])
    visual = down(tab, units, down_full, down_bias.reshape(16, 1, 512))
    visual = (visual, *around(after(visual, *text), 1))

    live_rows = patch_counts[0, 0] // 4
    live = (jnp.arange(SLOT, dtype=jnp.int32)[None, :] < live_rows[:, None]).reshape(-1)
    dest = jnp.where(live, dest_pos[0, 0], -1)[None]
    picked = pick(tab, dest, visual, text)
    pieces = (picked[0], hop(picked[2], 2, 1), hop(picked[1], 2, -1), hop(picked[3], 2, 2))
    own, to_left, to_right, to_far = product(tab, picked, norm_gain.reshape(16, 1, 512), weights)
    sums = (hop(to_far, 2, 2), hop(to_right, 2, 1), hop(to_left, 2, -1))
    embedded, scale = place_rows(tab, pieces)
    total = own
    for value in sums:
        total = total + value.astype(F32)
    keys_values = (total * scale[:, :1] + kv_bias).astype(BF16)
    return (embedded[None, None], keys_values[None, None])


def solution(mesh):
    return jax.shard_map(
        per_device,
        mesh=mesh,
        in_specs=(
            P("enc", "mb", "tp", None),
            P("enc", "mb", None),
            P("enc", "mb", None),
            P(),
            P(),
            P(("enc", "mb"), "tp"),
            P(),
            P("tp", ("enc", "mb")),
            P(),
            P("enc", "mb", "tp", None),
            P(),
            P("tp", None),
            P(),
        ),
        out_specs=(P("enc", "mb", "tp", None), P("enc", "mb", "tp", None)),
        check_vma=False,
    )
```

```python
import jax
import jax.numpy as jnp
import numpy as np
from jax import lax
from jax.experimental import pallas as pl
from jax.experimental.pallas import tpu as pltpu
from jax.sharding import PartitionSpec as P

SLOT = 8
RING = (0, -1, 1, 2)
MIB = 1 << 20
BF16, F32 = jnp.bfloat16, jnp.float32


def place(core, tp, which, step):
    y, x = tp // 4, tp % 4
    if (core == 0) == (which == 1):
        return y * 4 + (x + step) % 4
    return (y + step) % 4 * 4 + x


TABLE = np.array(
    [
        [place(core, place(core, tp, 2, o2), 1, o1) for o2 in RING for o1 in RING]
        for core in range(2)
        for tp in range(16)
    ],
    np.int32,
)
HOPS = {
    (which, step): [(c * 16 + t, c * 16 + place(c, t, which, step)) for c in range(2) for t in range(16)]
    for which in (1, 2)
    for step in (1, -1, 2)
}
SHUFFLE = [(a * 16 + b, (a ^ b) * 16 + b) for a in range(16) for b in range(16)]
TURN = [(a * 16 + b, a * 16 + (a ^ b)) for a in range(16) for b in range(16)]


def hop(value, which, step):
    return lax.ppermute(value, ("mb", "tp"), HOPS[which, step])


def around(value, which):
    return hop(value, which, 1), hop(value, which, -1), hop(value, which, 2)


def ring(value, which):
    half = value.shape[0] // 2
    right, left = hop(value, which, 1), hop(value, which, -1)
    return right, left, hop(right[:half], which, 1), hop(left[half:], which, -1)


def trade(to_right, to_left, to_far):
    right = hop(to_right, 2, 1)
    left = hop(to_left, 2, -1)
    return right, left, hop(to_far, 2, 2), hop(left[128:192], 2, -1)


def after(value, *others):
    return lax.optimization_barrier((value, *others))[0]


def cost(flops, moved):
    return pl.CostEstimate(flops=flops, bytes_accessed=moved, transcendentals=0)


def params(mib):
    return pltpu.CompilerParams(vmem_limit_bytes=mib * MIB)


VMEM = pl.BlockSpec(memory_space=pltpu.VMEM)
SMEM = pl.BlockSpec(memory_space=pltpu.SMEM)
ANY = pl.BlockSpec(memory_space=pl.ANY)
HBM = pl.BlockSpec(memory_space=pltpu.HBM)


def merge_kernel(p_ref, gain_ref, bias_ref, out_ref, rows):
    values = p_ref[...].astype(F32)
    center = values - jnp.mean(values, axis=-1, keepdims=True)
    spread = jnp.mean(center * center, axis=-1, keepdims=True)
    normal = center * lax.rsqrt(spread + 1e-06) * gain_ref[...].reshape(1, 1280) + bias_ref[...].reshape(1, 1280)
    for k in range(10):
        rows[k] = normal[:, k * 128 : (k + 1) * 128]
    for j in range(4):
        for k in range(10):
            start = j * 1280 + k * 128
            out_ref[:, start : start + 128] = rows[k, pl.ds(j, 16, stride=4), :].astype(BF16)


def merge(patches, gain, bias):
    return pl.pallas_call(
        merge_kernel,
        out_shape=jax.ShapeDtypeStruct((16, 5120), BF16),
        in_specs=[VMEM] * 3,
        out_specs=VMEM,
        scratch_shapes=[pltpu.VMEM((10, 64, 128), F32)],
        compiler_params=params(8),
        cost_estimate=cost(10**6, 330000),
    )(patches, gain, bias)


def pack_kernel(tab, own, left, right, far, kept, to_left, to_right, to_far):
    kept[...] = own[...]
    to_left[0:128] = left[...]
    to_left[128:192] = far[64:128]
    to_right[...] = right[...]
    to_far[...] = far[0:64]


def pack(tab, text):
    def columns(i2):
        return pl.BlockSpec((128, 512), lambda j, tab: (0, tab[i2 * 4 + j]))

    rows = (128, 192, 128, 64)
    return pl.pallas_call(
        pack_kernel,
        out_shape=[jax.ShapeDtypeStruct((n, 2048), BF16) for n in rows],
        grid_spec=pltpu.PrefetchScalarGridSpec(
            num_scalar_prefetch=1,
            grid=(4,),
            in_specs=[columns(i2) for i2 in range(4)],
            out_specs=[pl.BlockSpec((n, 512), lambda j, tab: (0, j)) for n in rows],
        ),
        compiler_params=params(8),
        cost_estimate=cost(0, 4 * MIB),
    )(tab, text, text, text, text)


def start(copies, sems):
    copies = [pltpu.make_async_copy(a, b, sems.at[i]) for i, (a, b) in enumerate(copies)]
    for copy in copies:
        copy.start()
    return copies


def up_kernel(tab, s0, s1, s2, s3a, s3b, weight, bias_ref, out_ref, rows, held, sems):
    copies = [(piece, rows.at[pl.ds(i * 64, 64)]) for i, piece in enumerate((s0, s1, s2))]
    copies += [(s3a, rows.at[pl.ds(192, 32)]), (s3b, rows.at[pl.ds(224, 32)])]
    copies += [(weight.at[pl.ds(k * 1024, 1024)], held.at[pl.ds(k * 1024, 1024)]) for k in range(5)]
    copies = start(copies, sems)
    for copy in copies[:5]:
        copy.wait()
    raised = bias_ref[tab[0]]
    for k in range(5):
        copies[5 + k].wait()
        at = slice(k * 1024, (k + 1) * 1024)
        raised = raised + jnp.dot(rows[:, at], held[at, :], preferred_element_type=F32)
    hidden = (0.5 * raised * (1.0 + lax.erf(raised * np.float32(0.5**0.5)))).astype(BF16)
    for k in range(16):
        out_ref[pl.ds(pl.multiple_of(tab[k] * 16, 16), 16), :] = hidden[k * 16 : (k + 1) * 16]


def up(tab, pieces, weight, bias):
    return pl.pallas_call(
        up_kernel,
        out_shape=jax.ShapeDtypeStruct((256, 320), BF16),
        in_specs=[SMEM] + [ANY] * 6 + [VMEM],
        out_specs=VMEM,
        scratch_shapes=[
            pltpu.VMEM((256, 5120), BF16),
            pltpu.VMEM((5120, 320), BF16),
            pltpu.SemaphoreType.DMA((10,)),
        ],
        compiler_params=params(56),
        cost_estimate=cost(840 * 10**6, 6 * MIB),
    )(tab, *pieces, weight, bias)


def down_kernel(tab, h0, h1, h2, h3a, h3b, weight, bias_ref, out_ref, units, held, sems):
    copies = []
    for k in range(16):
        source = weight.at[pl.ds(pl.multiple_of((tab[k] ^ tab[0]) * 320, 320), 320)]
        copies.append((source, held.at[pl.ds(k * 320, 320)]))
        if k % 4 == 3 and k < 15:
            copies.append(((h0, h1, h2)[k // 4], units.at[k // 4]))
    copies.append((h3a, units.at[3, pl.ds(0, 128)]))
    copies.append((h3b, units.at[3, pl.ds(128, 128)]))
    copies = start(copies, sems)
    total = bias_ref[tab[0]]
    for i2 in range(4):
        for copy in copies[i2 * 5 : i2 * 5 + 5 + i2 // 3]:
            copy.wait()
        total = total + jnp.dot(units[i2], held[i2 * 1280 : (i2 + 1) * 1280, :], preferred_element_type=F32)
    out_ref[...] = total.astype(BF16)


def down(tab, pieces, weight, bias):
    return pl.pallas_call(
        down_kernel,
        out_shape=jax.ShapeDtypeStruct((256, 512), BF16),
        in_specs=[SMEM] + [ANY] * 6 + [VMEM],
        out_specs=VMEM,
        scratch_shapes=[
            pltpu.VMEM((4, 256, 1280), BF16),
            pltpu.VMEM((5120, 512), BF16),
            pltpu.SemaphoreType.DMA((21,)),
        ],
        compiler_params=params(56),
        cost_estimate=cost(1340 * 10**6, 8 * MIB),
    )(tab, *pieces, weight, bias)


def pick_kernel(tab, dest, v0, v1, v2, v3, own, right, left, far_a, far_b, kept, to_left, to_right):
    visual = (v0[...], v1[...], v2[...], v3[...])
    targets = dest[...]

    def fill(i2, first, count, text, out, out_row):
        rows = lax.broadcasted_iota(jnp.int32, (count, 256), 0) + (tab[i2 * 4] * 128 + first)
        select = (rows == targets).astype(F32)
        present = jnp.sum(select, axis=1, keepdims=True) > 0.0
        select = select.astype(BF16)
        for j in range(4):
            at = slice(j * 512, (j + 1) * 512)
            picked = jnp.dot(select, visual[j], preferred_element_type=F32).astype(BF16)
            out[out_row : out_row + count, at] = jnp.where(present, picked, text[0:count, at])

    fill(3, 0, 64, far_a, to_left, 128)
    fill(3, 64, 64, far_b, to_left, 192)
    fill(1, 0, 128, right, to_left, 0)
    fill(2, 0, 128, left, to_right, 0)
    fill(0, 0, 128, own, kept, 0)


def pick(tab, dest, visual, text):
    return pl.pallas_call(
        pick_kernel,
        out_shape=[jax.ShapeDtypeStruct((n, 2048), BF16) for n in (128, 256, 128)],
        in_specs=[SMEM] + [VMEM] * 10,
        out_specs=[VMEM] * 3,
        compiler_params=params(32),
        cost_estimate=cost(540 * 10**6, 6 * MIB),
    )(tab, dest, *visual, *text)


def product_kernel(tab, kept, to_left, to_right, gain, w0, w1, w2, w3a, w3b, own, left, far, right, scaled):
    @pl.when(pl.program_id(0) == 0)
    def _():
        for j in range(4):
            at = slice(j * 512, (j + 1) * 512)
            scale = gain[tab[j]]
            row = 0
            for rows in (kept, to_left, to_right):
                count = rows.shape[0]
                scaled[row : row + count, at] = (rows[:, at].astype(F32) * scale).astype(BF16)
                row += count

    total = jnp.dot(scaled[:, 0:512], w0[...], preferred_element_type=F32)
    total = total + jnp.dot(scaled[:, 512:1024], w1[...], preferred_element_type=F32)
    total = total + jnp.dot(scaled[:, 1024:1536], w2[...], preferred_element_type=F32)
    total = total + jnp.dot(scaled[:, 1536:1792], w3a[...], preferred_element_type=F32)
    total = total + jnp.dot(scaled[:, 1792:2048], w3b[...], preferred_element_type=F32)
    own[...] = total[0:128]
    left[...] = total[128:256].astype(BF16)
    far[...] = total[256:384].astype(BF16)
    right[...] = total[384:512].astype(BF16)


def product(tab, picked, gain, weights):
    def block(count):
        return pl.BlockSpec((count, 512), lambda n: (0, n))

    return pl.pallas_call(
        product_kernel,
        out_shape=[jax.ShapeDtypeStruct((128, 2048), F32)] + [jax.ShapeDtypeStruct((128, 2048), BF16)] * 3,
        grid=(4,),
        in_specs=[SMEM] + [VMEM] * 4 + [block(n) for n in (512, 512, 512, 256, 256)],
        out_specs=[block(128)] * 4,
        scratch_shapes=[pltpu.VMEM((512, 2048), BF16)],
        compiler_params=params(40),
        cost_estimate=cost(4300 * 10**6, 14 * MIB),
    )(tab, *picked, gain, *weights)


def place_kernel(tab, own, right, left, far, out, scale, sems):
    copies = []
    total = 0.0
    for i2, rows in enumerate((own, right, left, far)):
        for j in range(4):
            columns = pl.ds(pl.multiple_of(tab[i2 * 4 + j] * 512, 512), 512)
            copies.append((rows.at[pl.ds(0, 128), pl.ds(j * 512, 512)], out.at[:, columns]))
    copies = start(copies, sems)
    for rows in (own, right, left, far):
        values = rows[0:128].astype(F32)
        total = total + jnp.sum(values * values, axis=1, keepdims=True)
    scale[...] = jnp.broadcast_to(lax.rsqrt(total * (1.0 / 8192.0) + 1e-06), (128, 128))
    for copy in copies:
        copy.wait()


def place_rows(tab, pieces):
    return pl.pallas_call(
        place_kernel,
        out_shape=[jax.ShapeDtypeStruct((128, 8192), BF16), jax.ShapeDtypeStruct((128, 128), F32)],
        in_specs=[SMEM] + [VMEM] * 4,
        out_specs=[ANY, VMEM],
        scratch_shapes=[pltpu.SemaphoreType.DMA((16,))],
        compiler_params=params(32),
        cost_estimate=cost(4 * 10**6, 30 * MIB),
    )(tab, *pieces)


def per_device(
    patches,
    patch_counts,
    dest_pos,
    merge_gain,
    merge_bias,
    up_weight,
    up_bias,
    down_weight,
    down_bias,
    text_embed,
    norm_gain,
    kv_weight,
    kv_bias,
):
    tab = jnp.asarray(TABLE)[lax.axis_index("mb") * 16 + lax.axis_index("tp")]
    up_full = lax.all_gather(up_weight, ("enc", "mb"), axis=0, tiled=True)
    down_part = lax.ppermute(down_weight, ("enc", "mb", "tp"), SHUFFLE)

    merged = merge(patches[0, 0], merge_gain, merge_bias)
    near = jnp.concatenate([merged, *around(merged, 1)], axis=0)
    down_part = lax.ppermute(after(down_part, near), ("enc", "mb", "tp"), TURN)
    kv_weight = after(kv_weight, near)
    kv_right, kv_left = hop(kv_weight, 1, 1), hop(kv_weight, 1, -1)
    group = (near, *ring(near, 2))
    down_part = after(down_part, *group[:3])
    down_full = lax.all_gather(down_part, ("enc", "mb"), axis=0, tiled=True)
    far_right, far_left = kv_right[:256], kv_left[256:]

    up_full, far_right, far_left = lax.optimization_barrier((up_full, far_right, far_left))
    hidden = up(tab, group, up_full, up_bias.reshape(16, 1, 320))
    near = jnp.concatenate([hidden, *around(hidden, 1)], axis=1)
    far_right, far_left = lax.optimization_barrier((far_right, far_left, near))[:2]
    weights = (kv_weight, kv_right, kv_left, hop(far_right, 1, 1), hop(far_left, 1, -1))
    units = (near, *ring(near, 2))
    own, to_left, to_right, to_far = pack(tab, text_embed[0, 0])
    to_left, to_right, to_far = lax.optimization_barrier((to_left, to_right, to_far, *units))[:3]
    text = (own, *trade(to_right, to_left, to_far))
    down_full = after(down_full, weights[3], weights[4])
    visual = down(tab, units, down_full, down_bias.reshape(16, 1, 512))
    visual = (visual, *around(after(visual, *text), 1))

    live_rows = patch_counts[0, 0] // 4
    live = (jnp.arange(SLOT, dtype=jnp.int32)[None, :] < live_rows[:, None]).reshape(-1)
    dest = jnp.where(live, dest_pos[0, 0], -1)[None]
    picked = pick(tab, dest, visual, text)
    right, left = hop(picked[2], 2, 1), hop(picked[1], 2, -1)
    own, to_left, to_far, to_right = product(tab, picked, norm_gain.reshape(16, 1, 512), weights)
    pieces = (picked[0], right, left, hop(after(left, to_far)[128:256], 2, -1))
    sums = (hop(to_far, 2, 2), hop(to_right, 2, 1), hop(to_left, 2, -1))
    embedded, scale = place_rows(tab, pieces)
    total = own
    for value in sums:
        total = total + value.astype(F32)
    keys_values = (total * scale[:, :1] + kv_bias).astype(BF16)
    return (embedded[None, None], keys_values[None, None])


def solution(mesh):
    return jax.shard_map(
        per_device,
        mesh=mesh,
        in_specs=(
            P("enc", "mb", "tp", None),
            P("enc", "mb", None),
            P("enc", "mb", None),
            P(),
            P(),
            P(("enc", "mb"), "tp"),
            P(),
            P("tp", ("enc", "mb")),
            P(),
            P("enc", "mb", "tp", None),
            P(),
            P("tp", None),
            P(),
        ),
        out_specs=(P("enc", "mb", "tp", None), P("enc", "mb", "tp", None)),
        check_vma=False,
    )
```

```python
import jax
import jax.numpy as jnp
import numpy as np
from jax import lax
from jax.experimental import pallas as pl
from jax.experimental.pallas import tpu as pltpu
from jax.sharding import PartitionSpec as P

SLOT = 8
RING = (0, -1, 1, 2)
MIB = 1 << 20
BF16, F32 = jnp.bfloat16, jnp.float32


def place(core, tp, which, step):
    y, x = tp // 4, tp % 4
    if (core == 0) == (which == 1):
        return y * 4 + (x + step) % 4
    return (y + step) % 4 * 4 + x


TABLE = np.array(
    [
        [place(core, place(core, tp, 2, o2), 1, o1) for o2 in RING for o1 in RING]
        for core in range(2)
        for tp in range(16)
    ],
    np.int32,
)
HOPS = {
    (which, step): [(c * 16 + t, c * 16 + place(c, t, which, step)) for c in range(2) for t in range(16)]
    for which in (1, 2)
    for step in (1, -1, 2)
}
LINES = {
    (axis, step): [
        (c * 16 + t, c * 16 + place(1 if axis == "y" else 0, t, 1, step)) for c in range(2) for t in range(16)
    ]
    for axis in "yx"
    for step in (1, -1, 2)
}
SHUFFLE = [
    ((z * 2 + c) * 16 + y * 4 + x, ((y * 2 + z % 2) * 2 + c) * 16 + z // 2 * 4 + x)
    for z in range(8)
    for c in range(2)
    for y in range(4)
    for x in range(4)
]


def hop(value, which, step):
    return lax.ppermute(value, ("mb", "tp"), HOPS[which, step])


def around(value, which):
    return hop(value, which, 1), hop(value, which, -1), hop(value, which, 2)


def line(value, axis, step):
    return lax.ppermute(value, ("mb", "tp"), LINES[axis, step])


def after(value, *others):
    return lax.optimization_barrier((value, *others))[0]


def cost(flops, moved):
    return pl.CostEstimate(flops=flops, bytes_accessed=moved, transcendentals=0)


def params(mib):
    return pltpu.CompilerParams(vmem_limit_bytes=mib * MIB)


VMEM = pl.BlockSpec(memory_space=pltpu.VMEM)
SMEM = pl.BlockSpec(memory_space=pltpu.SMEM)
ANY = pl.BlockSpec(memory_space=pl.ANY)
HBM = pl.BlockSpec(memory_space=pltpu.HBM)


def merge_kernel(p_ref, gain_ref, bias_ref, out_ref, rows):
    values = p_ref[...].astype(F32)
    center = values - jnp.mean(values, axis=-1, keepdims=True)
    spread = jnp.mean(center * center, axis=-1, keepdims=True)
    normal = center * lax.rsqrt(spread + 1e-06) * gain_ref[...].reshape(1, 1280) + bias_ref[...].reshape(1, 1280)
    for k in range(10):
        rows[k] = normal[:, k * 128 : (k + 1) * 128]
    for j in range(4):
        for k in range(10):
            start = j * 1280 + k * 128
            out_ref[:, start : start + 128] = rows[k, pl.ds(j, 16, stride=4), :].astype(BF16)


def merge(patches, gain, bias):
    return pl.pallas_call(
        merge_kernel,
        out_shape=jax.ShapeDtypeStruct((16, 5120), BF16),
        in_specs=[VMEM] * 3,
        out_specs=VMEM,
        scratch_shapes=[pltpu.VMEM((10, 64, 128), F32)],
        compiler_params=params(8),
        cost_estimate=cost(10**6, 330000),
    )(patches, gain, bias)


def pack_kernel(tab, *refs):
    for source, target in zip(refs[:4], refs[4:]):
        target[...] = source[...]


def pack(tab, text):
    def columns(i2):
        return pl.BlockSpec((128, 512), lambda j, tab: (0, tab[i2 * 4 + j]))

    return pl.pallas_call(
        pack_kernel,
        out_shape=[jax.ShapeDtypeStruct((128, 2048), BF16)] * 4,
        grid_spec=pltpu.PrefetchScalarGridSpec(
            num_scalar_prefetch=1,
            grid=(4,),
            in_specs=[columns(i2) for i2 in range(4)],
            out_specs=[pl.BlockSpec((128, 512), lambda j, tab: (0, j))] * 4,
        ),
        compiler_params=params(8),
        cost_estimate=cost(0, 4 * MIB),
    )(tab, text, text, text, text)


def start(copies, sems):
    copies = [pltpu.make_async_copy(a, b, sems.at[i]) for i, (a, b) in enumerate(copies)]
    for copy in copies:
        copy.start()
    return copies


def up_kernel(tab, s0, s1, s2, s3, weight, bias_ref, out_ref, rows, held, sems):
    copies = [(piece, rows.at[pl.ds(i * 64, 64)]) for i, piece in enumerate((s0, s1, s2, s3))]
    copies += [(weight.at[pl.ds(k * 1024, 1024)], held.at[pl.ds(k * 1024, 1024)]) for k in range(5)]
    copies = start(copies, sems)
    for copy in copies[:4]:
        copy.wait()
    raised = bias_ref[tab[0]]
    for k in range(5):
        copies[4 + k].wait()
        at = slice(k * 1024, (k + 1) * 1024)
        raised = raised + jnp.dot(rows[:, at], held[at, :], preferred_element_type=F32)
    hidden = (0.5 * raised * (1.0 + lax.erf(raised * np.float32(0.5**0.5)))).astype(BF16)
    for k in range(16):
        out_ref[pl.ds(pl.multiple_of(tab[k] * 16, 16), 16), :] = hidden[k * 16 : (k + 1) * 16]


def up(tab, pieces, weight, bias):
    return pl.pallas_call(
        up_kernel,
        out_shape=jax.ShapeDtypeStruct((256, 320), BF16),
        in_specs=[SMEM] + [ANY] * 5 + [VMEM],
        out_specs=VMEM,
        scratch_shapes=[
            pltpu.VMEM((256, 5120), BF16),
            pltpu.VMEM((5120, 320), BF16),
            pltpu.SemaphoreType.DMA((9,)),
        ],
        compiler_params=params(56),
        cost_estimate=cost(840 * 10**6, 6 * MIB),
    )(tab, *pieces, weight, bias)


def down_kernel(nat, h0, h1, h2, h3, weight, own, left, right, far, units, held, sems):
    copies = []
    for k, piece in enumerate((h0, h1, h2, h3)):
        copies.append((piece, units.at[k]))
        for j in range(4):
            slot = nat[k * 4] // 4 * 4 + nat[j] % 4
            source = weight.at[pl.ds(pl.multiple_of(slot * 320, 320), 320)]
            copies.append((source, held.at[k, :, pl.ds(j * 512, 512)]))
    copies = start(copies, sems)
    total = 0.0
    for k in range(4):
        for copy in copies[k * 5 : k * 5 + 5]:
            copy.wait()
        total = total + jnp.dot(units[k], held[k], preferred_element_type=F32)
    own[...] = total[:, 0:512]
    left[...] = total[:, 512:1024].astype(BF16)
    right[...] = total[:, 1024:1536].astype(BF16)
    far[...] = total[:, 1536:2048].astype(BF16)


def down(nat, pieces, weight):
    return pl.pallas_call(
        down_kernel,
        out_shape=[jax.ShapeDtypeStruct((256, 512), F32)] + [jax.ShapeDtypeStruct((256, 512), BF16)] * 3,
        in_specs=[SMEM] + [ANY] * 5,
        out_specs=[VMEM] * 4,
        scratch_shapes=[
            pltpu.VMEM((4, 256, 320), BF16),
            pltpu.VMEM((4, 320, 2048), BF16),
            pltpu.SemaphoreType.DMA((20,)),
        ],
        compiler_params=params(56),
        cost_estimate=cost(1340 * 10**6, 8 * MIB),
    )(nat, *pieces, weight)


def pick_kernel(tab, dest, v0, v1, v2, v3, *refs):
    visual = (v0[...], v1[...], v2[...], v3[...])
    targets = dest[...]
    for i2 in (3, 2, 1, 0):
        text, out = refs[i2], refs[4 + i2]
        match = (lax.broadcasted_iota(jnp.int32, (128, 256), 0) + tab[i2 * 4] * 128) == targets
        select = match.astype(F32)
        present = jnp.sum(select, axis=1, keepdims=True) > 0.0
        select = select.astype(BF16)
        for j in range(4):
            at = slice(j * 512, (j + 1) * 512)
            picked = jnp.dot(select, visual[j], preferred_element_type=F32).astype(BF16)
            out[:, at] = jnp.where(present, picked, text[:, at])


def pick(tab, dest, visual, text):
    return pl.pallas_call(
        pick_kernel,
        out_shape=[jax.ShapeDtypeStruct((128, 2048), BF16)] * 4,
        in_specs=[SMEM] + [VMEM] * 9,
        out_specs=[VMEM] * 4,
        compiler_params=params(32),
        cost_estimate=cost(540 * 10**6, 6 * MIB),
    )(tab, dest, *visual, *text)


def product_kernel(tab, e0, e1, e2, e3, gain, w0, w1, w2, w3a, w3b, own, left, right, far, scaled):
    @pl.when(pl.program_id(0) == 0)
    def _():
        for j in range(4):
            at = slice(j * 512, (j + 1) * 512)
            scale = gain[tab[j]]
            for i2, rows in enumerate((e0, e1, e2, e3)):
                scaled[i2 * 128 : (i2 + 1) * 128, at] = (rows[:, at].astype(F32) * scale).astype(BF16)

    total = jnp.dot(scaled[:, 0:512], w0[...], preferred_element_type=F32)
    total = total + jnp.dot(scaled[:, 512:1024], w1[...], preferred_element_type=F32)
    total = total + jnp.dot(scaled[:, 1024:1536], w2[...], preferred_element_type=F32)
    total = total + jnp.dot(scaled[:, 1536:1792], w3a[...], preferred_element_type=F32)
    total = total + jnp.dot(scaled[:, 1792:2048], w3b[...], preferred_element_type=F32)
    own[...] = total[0:128]
    left[...] = total[128:256].astype(BF16)
    right[...] = total[256:384].astype(BF16)
    far[...] = total[384:512].astype(BF16)


def product(tab, picked, gain, weights):
    def block(count):
        return pl.BlockSpec((count, 512), lambda n: (0, n))

    return pl.pallas_call(
        product_kernel,
        out_shape=[jax.ShapeDtypeStruct((128, 2048), F32)] + [jax.ShapeDtypeStruct((128, 2048), BF16)] * 3,
        grid=(4,),
        in_specs=[SMEM] + [VMEM] * 5 + [block(n) for n in (512, 512, 512, 256, 256)],
        out_specs=[block(128)] * 4,
        scratch_shapes=[pltpu.VMEM((512, 2048), BF16)],
        compiler_params=params(40),
        cost_estimate=cost(4300 * 10**6, 14 * MIB),
    )(tab, *picked, gain, *weights)


def place_kernel(tab, e0, e1, e2, e3, out, scale, sems):
    copies = []
    for i2, rows in enumerate((e0, e1, e2, e3)):
        for j in range(4):
            columns = pl.ds(pl.multiple_of(tab[i2 * 4 + j] * 512, 512), 512)
            copies.append((rows.at[:, pl.ds(j * 512, 512)], out.at[:, columns]))
    copies = start(copies, sems)
    total = 0.0
    for rows in (e0, e1, e2, e3):
        values = rows[...].astype(F32)
        total = total + jnp.sum(values * values, axis=1, keepdims=True)
    scale[...] = jnp.broadcast_to(lax.rsqrt(total * (1.0 / 8192.0) + 1e-06), (128, 128))
    for copy in copies:
        copy.wait()


def place_rows(tab, pieces):
    return pl.pallas_call(
        place_kernel,
        out_shape=[jax.ShapeDtypeStruct((128, 8192), BF16), jax.ShapeDtypeStruct((128, 128), F32)],
        in_specs=[SMEM] + [VMEM] * 4,
        out_specs=[ANY, VMEM],
        scratch_shapes=[pltpu.SemaphoreType.DMA((16,))],
        compiler_params=params(32),
        cost_estimate=cost(4 * 10**6, 30 * MIB),
    )(tab, *pieces)


def per_device(
    patches,
    patch_counts,
    dest_pos,
    merge_gain,
    merge_bias,
    up_weight,
    up_bias,
    down_weight,
    down_bias,
    text_embed,
    norm_gain,
    kv_weight,
    kv_bias,
):
    tab = jnp.asarray(TABLE)[lax.axis_index("mb") * 16 + lax.axis_index("tp")]
    nat = jnp.asarray(TABLE)[lax.axis_index("tp")]
    up_full = lax.all_gather(up_weight, ("enc", "mb"), axis=0, tiled=True)
    down_part = lax.ppermute(down_weight, ("enc", "mb", "tp"), SHUFFLE)

    merged = merge(patches[0, 0], merge_gain, merge_bias)
    near = jnp.concatenate([merged, *around(merged, 1)], axis=0)
    group = (near, *around(near, 2))
    down_full = lax.all_gather(after(down_part, *group), ("enc", "mb"), axis=0, tiled=True)

    kv_weight = after(kv_weight, *group)
    kv_right, kv_left = hop(kv_weight, 1, 1), hop(kv_weight, 1, -1)
    far_right, far_left = kv_right[:256], kv_left[256:]
    own, to_left, to_right, to_far = pack(tab, text_embed[0, 0])
    hidden = up(tab, group, up_full, up_bias.reshape(16, 1, 320))
    units = (hidden, line(hidden, "y", 1), line(hidden, "y", -1), line(hidden, "y", 2))
    moved = (*units, far_right, far_left, to_left, to_right, to_far)
    *units, far_right, far_left, to_left, to_right, to_far = lax.optimization_barrier(moved)

    weights = (kv_weight, kv_right, kv_left, hop(far_right, 1, 1), hop(far_left, 1, -1))
    text = (own, hop(to_right, 2, 1), hop(to_left, 2, -1), hop(to_far, 2, 2))
    down_full = after(down_full, weights[3], weights[4], *text)
    own, to_left, to_right, to_far = down(nat, units, down_full)
    bias = lax.dynamic_slice_in_dim(down_bias, lax.axis_index("tp") * 512, 512, 0)
    total = own + bias
    for value in (line(to_far, "x", 2), line(to_right, "x", 1), line(to_left, "x", -1)):
        total = total + value.astype(F32)
    visual = total.astype(BF16)
    visual = (visual, *around(visual, 1))

    live_rows = patch_counts[0, 0] // 4
    live = (jnp.arange(SLOT, dtype=jnp.int32)[None, :] < live_rows[:, None]).reshape(-1)
    dest = jnp.where(live, dest_pos[0, 0], -1)[None]
    picked = pick(tab, dest, visual, text)
    pieces = (picked[0], hop(picked[2], 2, 1), hop(picked[1], 2, -1), hop(picked[3], 2, 2))
    own, to_left, to_right, to_far = product(tab, picked, norm_gain.reshape(16, 1, 512), weights)
    sums = (hop(to_far, 2, 2), hop(to_right, 2, 1), hop(to_left, 2, -1))
    embedded, scale = place_rows(tab, pieces)
    total = own
    for value in sums:
        total = total + value.astype(F32)
    keys_values = (total * scale[:, :1] + kv_bias).astype(BF16)
    return (embedded[None, None], keys_values[None, None])


def solution(mesh):
    return jax.shard_map(
        per_device,
        mesh=mesh,
        in_specs=(
            P("enc", "mb", "tp", None),
            P("enc", "mb", None),
            P("enc", "mb", None),
            P(),
            P(),
            P(("enc", "mb"), "tp"),
            P(),
            P("tp", ("enc", "mb")),
            P(),
            P("enc", "mb", "tp", None),
            P(),
            P("tp", None),
            P(),
        ),
        out_specs=(P("enc", "mb", "tp", None), P("enc", "mb", "tp", None)),
        check_vma=False,
    )
```

```python
import jax
import jax.numpy as jnp
import numpy as np
from jax import lax
from jax.experimental import pallas as pl
from jax.experimental.pallas import tpu as pltpu
from jax.sharding import PartitionSpec as P

SLOT = 8
RING = (0, -1, 1, 2)
MIB = 1 << 20
BF16, F32 = jnp.bfloat16, jnp.float32


def place(core, tp, which, step):
    y, x = tp // 4, tp % 4
    if (core == 0) == (which == 1):
        return y * 4 + (x + step) % 4
    return (y + step) % 4 * 4 + x


TABLE = np.array(
    [
        [place(core, place(core, tp, 2, o2), 1, o1) for o2 in RING for o1 in RING]
        for core in range(2)
        for tp in range(16)
    ],
    np.int32,
)
HOPS = {
    (which, step): [(c * 16 + t, c * 16 + place(c, t, which, step)) for c in range(2) for t in range(16)]
    for which in (1, 2)
    for step in (1, -1, 2)
}
LINES = {
    (axis, step): [
        (c * 16 + t, c * 16 + place(1 if axis == "y" else 0, t, 1, step)) for c in range(2) for t in range(16)
    ]
    for axis in "yx"
    for step in (1, -1, 2)
}
SHUFFLE = [
    ((z * 2 + c) * 16 + y * 4 + x, (z // 2 * 4 + x) * 16 + y * 4 + z % 2 * 2 + c)
    for z in range(8)
    for c in range(2)
    for y in range(4)
    for x in range(4)
]


def hop(value, which, step):
    return lax.ppermute(value, ("mb", "tp"), HOPS[which, step])


def around(value, which):
    return hop(value, which, 1), hop(value, which, -1), hop(value, which, 2)


def line(value, axis, step):
    return lax.ppermute(value, ("mb", "tp"), LINES[axis, step])


def after(value, *others):
    return lax.optimization_barrier((value, *others))[0]


def cost(flops, moved):
    return pl.CostEstimate(flops=flops, bytes_accessed=moved, transcendentals=0)


def params(mib):
    return pltpu.CompilerParams(vmem_limit_bytes=mib * MIB)


VMEM = pl.BlockSpec(memory_space=pltpu.VMEM)
SMEM = pl.BlockSpec(memory_space=pltpu.SMEM)
ANY = pl.BlockSpec(memory_space=pl.ANY)
HBM = pl.BlockSpec(memory_space=pltpu.HBM)


def merge_kernel(p_ref, gain_ref, bias_ref, out_ref, rows):
    values = p_ref[...].astype(F32)
    center = values - jnp.mean(values, axis=-1, keepdims=True)
    spread = jnp.mean(center * center, axis=-1, keepdims=True)
    normal = center * lax.rsqrt(spread + 1e-06) * gain_ref[...].reshape(1, 1280) + bias_ref[...].reshape(1, 1280)
    for k in range(10):
        rows[k] = normal[:, k * 128 : (k + 1) * 128]
    for j in range(4):
        for k in range(10):
            start = j * 1280 + k * 128
            out_ref[:, start : start + 128] = rows[k, pl.ds(j, 16, stride=4), :].astype(BF16)


def merge(patches, gain, bias):
    return pl.pallas_call(
        merge_kernel,
        out_shape=jax.ShapeDtypeStruct((16, 5120), BF16),
        in_specs=[VMEM] * 3,
        out_specs=VMEM,
        scratch_shapes=[pltpu.VMEM((10, 64, 128), F32)],
        compiler_params=params(8),
        cost_estimate=cost(10**6, 330000),
    )(patches, gain, bias)


def pack_kernel(tab, *refs):
    for source, target in zip(refs[:4], refs[4:]):
        target[...] = source[...]


def pack(tab, text):
    def columns(i2):
        return pl.BlockSpec((128, 512), lambda j, tab: (0, tab[i2 * 4 + j]))

    return pl.pallas_call(
        pack_kernel,
        out_shape=[jax.ShapeDtypeStruct((128, 2048), BF16)] * 4,
        grid_spec=pltpu.PrefetchScalarGridSpec(
            num_scalar_prefetch=1,
            grid=(4,),
            in_specs=[columns(i2) for i2 in range(4)],
            out_specs=[pl.BlockSpec((128, 512), lambda j, tab: (0, j))] * 4,
        ),
        compiler_params=params(8),
        cost_estimate=cost(0, 4 * MIB),
    )(tab, text, text, text, text)


def start(copies, sems):
    copies = [pltpu.make_async_copy(a, b, sems.at[i]) for i, (a, b) in enumerate(copies)]
    for copy in copies:
        copy.start()
    return copies


def up_kernel(tab, s0, s1, s2, s3, weight, bias_ref, out_ref, rows, held, sems):
    copies = [(piece, rows.at[pl.ds(i * 64, 64)]) for i, piece in enumerate((s0, s1, s2, s3))]
    copies += [(weight.at[pl.ds(k * 1024, 1024)], held.at[pl.ds(k * 1024, 1024)]) for k in range(5)]
    copies = start(copies, sems)
    for copy in copies[:4]:
        copy.wait()
    raised = bias_ref[tab[0]]
    for k in range(5):
        copies[4 + k].wait()
        at = slice(k * 1024, (k + 1) * 1024)
        raised = raised + jnp.dot(rows[:, at], held[at, :], preferred_element_type=F32)
    hidden = (0.5 * raised * (1.0 + lax.erf(raised * np.float32(0.5**0.5)))).astype(BF16)
    for k in range(16):
        out_ref[pl.ds(pl.multiple_of(tab[k] * 16, 16), 16), :] = hidden[k * 16 : (k + 1) * 16]


def up(tab, pieces, weight, bias):
    return pl.pallas_call(
        up_kernel,
        out_shape=jax.ShapeDtypeStruct((256, 320), BF16),
        in_specs=[SMEM] + [ANY] * 5 + [VMEM],
        out_specs=VMEM,
        scratch_shapes=[
            pltpu.VMEM((256, 5120), BF16),
            pltpu.VMEM((5120, 320), BF16),
            pltpu.SemaphoreType.DMA((9,)),
        ],
        compiler_params=params(56),
        cost_estimate=cost(840 * 10**6, 6 * MIB),
    )(tab, *pieces, weight, bias)


def down_kernel(nat, h0, h1, h2, h3, weight, own, left, right, far, units, held, sems):
    copies = []
    for k, piece in enumerate((h0, h1, h2, h3)):
        copies.append((piece, units.at[k]))
        for j in range(4):
            slot = nat[j * 4] // 4 * 4 + nat[k] % 4
            source = weight.at[pl.ds(pl.multiple_of(slot * 320, 320), 320)]
            copies.append((source, held.at[k, :, pl.ds(j * 512, 512)]))
    copies = start(copies, sems)
    total = 0.0
    for k in range(4):
        for copy in copies[k * 5 : k * 5 + 5]:
            copy.wait()
        total = total + jnp.dot(units[k], held[k], preferred_element_type=F32)
    own[...] = total[:, 0:512]
    left[...] = total[:, 512:1024].astype(BF16)
    right[...] = total[:, 1024:1536].astype(BF16)
    far[...] = total[:, 1536:2048].astype(BF16)


def down(nat, pieces, weight):
    return pl.pallas_call(
        down_kernel,
        out_shape=[jax.ShapeDtypeStruct((256, 512), F32)] + [jax.ShapeDtypeStruct((256, 512), BF16)] * 3,
        in_specs=[SMEM] + [ANY] * 5,
        out_specs=[VMEM] * 4,
        scratch_shapes=[
            pltpu.VMEM((4, 256, 320), BF16),
            pltpu.VMEM((4, 320, 2048), BF16),
            pltpu.SemaphoreType.DMA((20,)),
        ],
        compiler_params=params(56),
        cost_estimate=cost(1340 * 10**6, 8 * MIB),
    )(nat, *pieces, weight)


def pick_kernel(tab, dest, v0, v1, v2, v3, *refs):
    visual = (v0[...], v1[...], v2[...], v3[...])
    targets = dest[...]
    for i2 in (3, 2, 1, 0):
        text, out = refs[i2], refs[4 + i2]
        match = (lax.broadcasted_iota(jnp.int32, (128, 256), 0) + tab[i2 * 4] * 128) == targets
        select = match.astype(F32)
        present = jnp.sum(select, axis=1, keepdims=True) > 0.0
        select = select.astype(BF16)
        for j in range(4):
            at = slice(j * 512, (j + 1) * 512)
            picked = jnp.dot(select, visual[j], preferred_element_type=F32).astype(BF16)
            out[:, at] = jnp.where(present, picked, text[:, at])


def pick(tab, dest, visual, text):
    return pl.pallas_call(
        pick_kernel,
        out_shape=[jax.ShapeDtypeStruct((128, 2048), BF16)] * 4,
        in_specs=[SMEM] + [VMEM] * 9,
        out_specs=[VMEM] * 4,
        compiler_params=params(32),
        cost_estimate=cost(540 * 10**6, 6 * MIB),
    )(tab, dest, *visual, *text)


def product_kernel(tab, e0, e1, e2, e3, gain, w0, w1, w2, w3a, w3b, own, left, right, far, scaled):
    @pl.when(pl.program_id(0) == 0)
    def _():
        for j in range(4):
            at = slice(j * 512, (j + 1) * 512)
            scale = gain[tab[j]]
            for i2, rows in enumerate((e0, e1, e2, e3)):
                scaled[i2 * 128 : (i2 + 1) * 128, at] = (rows[:, at].astype(F32) * scale).astype(BF16)

    total = jnp.dot(scaled[:, 0:512], w0[...], preferred_element_type=F32)
    total = total + jnp.dot(scaled[:, 512:1024], w1[...], preferred_element_type=F32)
    total = total + jnp.dot(scaled[:, 1024:1536], w2[...], preferred_element_type=F32)
    total = total + jnp.dot(scaled[:, 1536:1792], w3a[...], preferred_element_type=F32)
    total = total + jnp.dot(scaled[:, 1792:2048], w3b[...], preferred_element_type=F32)
    own[...] = total[0:128]
    left[...] = total[128:256].astype(BF16)
    right[...] = total[256:384].astype(BF16)
    far[...] = total[384:512].astype(BF16)


def product(tab, picked, gain, weights):
    def block(count):
        return pl.BlockSpec((count, 512), lambda n: (0, n))

    return pl.pallas_call(
        product_kernel,
        out_shape=[jax.ShapeDtypeStruct((128, 2048), F32)] + [jax.ShapeDtypeStruct((128, 2048), BF16)] * 3,
        grid=(4,),
        in_specs=[SMEM] + [VMEM] * 5 + [block(n) for n in (512, 512, 512, 256, 256)],
        out_specs=[block(128)] * 4,
        scratch_shapes=[pltpu.VMEM((512, 2048), BF16)],
        compiler_params=params(56),
        cost_estimate=cost(4300 * 10**6, 14 * MIB),
    )(tab, *picked, gain, *weights)


def place_kernel(tab, e0, e1, e2, e3, out, scale, sems):
    copies = []
    for i2, rows in enumerate((e0, e1, e2, e3)):
        for j in range(4):
            columns = pl.ds(pl.multiple_of(tab[i2 * 4 + j] * 512, 512), 512)
            copies.append((rows.at[:, pl.ds(j * 512, 512)], out.at[:, columns]))
    copies = start(copies, sems)
    total = 0.0
    for rows in (e0, e1, e2, e3):
        values = rows[...].astype(F32)
        total = total + jnp.sum(values * values, axis=1, keepdims=True)
    scale[...] = jnp.broadcast_to(lax.rsqrt(total * (1.0 / 8192.0) + 1e-06), (128, 128))
    for copy in copies:
        copy.wait()


def place_rows(tab, pieces):
    return pl.pallas_call(
        place_kernel,
        out_shape=[jax.ShapeDtypeStruct((128, 8192), BF16), jax.ShapeDtypeStruct((128, 128), F32)],
        in_specs=[SMEM] + [VMEM] * 4,
        out_specs=[ANY, VMEM],
        scratch_shapes=[pltpu.SemaphoreType.DMA((16,))],
        compiler_params=params(32),
        cost_estimate=cost(4 * 10**6, 30 * MIB),
    )(tab, *pieces)


def per_device(
    patches,
    patch_counts,
    dest_pos,
    merge_gain,
    merge_bias,
    up_weight,
    up_bias,
    down_weight,
    down_bias,
    text_embed,
    norm_gain,
    kv_weight,
    kv_bias,
):
    tab = jnp.asarray(TABLE)[lax.axis_index("mb") * 16 + lax.axis_index("tp")]
    nat = jnp.asarray(TABLE)[lax.axis_index("tp")]
    up_full = lax.all_gather(up_weight, ("enc", "mb"), axis=0, tiled=True)
    down_part = lax.ppermute(down_weight, ("enc", "mb", "tp"), SHUFFLE)

    merged = merge(patches[0, 0], merge_gain, merge_bias)
    near = jnp.concatenate([merged, *around(merged, 1)], axis=0)
    group = (near, *around(near, 2))
    down_full = lax.all_gather(after(down_part, *group), ("enc", "mb"), axis=0, tiled=True)

    kv_weight = after(kv_weight, *group)
    kv_right, kv_left = hop(kv_weight, 1, 1), hop(kv_weight, 1, -1)
    far_right, far_left = kv_right[:256], kv_left[256:]
    own, to_left, to_right, to_far = pack(tab, text_embed[0, 0])
    hidden = up(tab, group, up_full, up_bias.reshape(16, 1, 320))
    units = (hidden, line(hidden, "x", 1), line(hidden, "x", -1), line(hidden, "x", 2))
    moved = (*units, far_right, far_left, to_left, to_right, to_far)
    *units, far_right, far_left, to_left, to_right, to_far = lax.optimization_barrier(moved)

    weights = (kv_weight, kv_right, kv_left, hop(far_right, 1, 1), hop(far_left, 1, -1))
    text = (own, hop(to_right, 2, 1), hop(to_left, 2, -1), hop(to_far, 2, 2))
    down_full = after(down_full, weights[3], weights[4], *text)
    own, to_left, to_right, to_far = down(nat, units, down_full)
    bias = lax.dynamic_slice_in_dim(down_bias, lax.axis_index("tp") * 512, 512, 0)
    total = own + bias
    for value in (line(to_far, "y", 2), line(to_right, "y", 1), line(to_left, "y", -1)):
        total = total + value.astype(F32)
    visual = total.astype(BF16)
    visual = (visual, *around(visual, 1))

    live_rows = patch_counts[0, 0] // 4
    live = (jnp.arange(SLOT, dtype=jnp.int32)[None, :] < live_rows[:, None]).reshape(-1)
    dest = jnp.where(live, dest_pos[0, 0], -1)[None]
    picked = pick(tab, dest, visual, text)
    pieces = (picked[0], hop(picked[2], 2, 1), hop(picked[1], 2, -1), hop(picked[3], 2, 2))
    own, to_left, to_right, to_far = product(tab, picked, norm_gain.reshape(16, 1, 512), weights)
    sums = (hop(to_far, 2, 2), hop(to_right, 2, 1), hop(to_left, 2, -1))
    embedded, scale = place_rows(tab, pieces)
    total = own
    for value in sums:
        total = total + value.astype(F32)
    keys_values = (total * scale[:, :1] + kv_bias).astype(BF16)
    return (embedded[None, None], keys_values[None, None])


def solution(mesh):
    return jax.shard_map(
        per_device,
        mesh=mesh,
        in_specs=(
            P("enc", "mb", "tp", None),
            P("enc", "mb", None),
            P("enc", "mb", None),
            P(),
            P(),
            P(("enc", "mb"), "tp"),
            P(),
            P("tp", ("enc", "mb")),
            P(),
            P("enc", "mb", "tp", None),
            P(),
            P("tp", None),
            P(),
        ),
        out_specs=(P("enc", "mb", "tp", None), P("enc", "mb", "tp", None)),
        check_vma=False,
    )
```

```python
import jax
import jax.numpy as jnp
import numpy as np
from jax import lax
from jax.experimental import pallas as pl
from jax.experimental.pallas import tpu as pltpu
from jax.sharding import PartitionSpec as P

SLOT = 8
RING = (0, -1, 1, 2)
MIB = 1 << 20
BF16, F32 = jnp.bfloat16, jnp.float32


def place(core, tp, which, step):
    y, x = tp // 4, tp % 4
    if (core == 0) == (which == 1):
        return y * 4 + (x + step) % 4
    return (y + step) % 4 * 4 + x


TABLE = np.array(
    [
        [place(core, place(core, tp, 2, o2), 1, o1) for o2 in RING for o1 in RING]
        for core in range(2)
        for tp in range(16)
    ],
    np.int32,
)
HOPS = {
    (which, step): [(c * 16 + t, c * 16 + place(c, t, which, step)) for c in range(2) for t in range(16)]
    for which in (1, 2)
    for step in (1, -1, 2)
}
LINES = {
    (axis, step): [
        (c * 16 + t, c * 16 + place(1 if axis == "y" else 0, t, 1, step)) for c in range(2) for t in range(16)
    ]
    for axis in "yx"
    for step in (1, -1, 2)
}
SHUFFLE = [
    ((z * 2 + c) * 16 + y * 4 + x, (z // 2 * 4 + x) * 16 + y * 4 + z % 2 * 2 + c)
    for z in range(8)
    for c in range(2)
    for y in range(4)
    for x in range(4)
]

OTHER = [(0, 1), (1, 0)]
CLIMB = [(z * 2 + c, (z + 1 - 2 * c) % 8 * 2 + c) for z in range(8) for c in range(2)]


def climbed(z, core, other):
    step = -1 if (core == 0) != other else 1
    first = core ^ int(other)
    near = [(z + step * k) % 8 * 2 + (first ^ j) for k in (1, 2, 3) for j in (0, 1)]
    return near + [(z + 4) % 8 * 2 + first]


STACK = np.array(
    [
        [z * 2 + c, z * 2 + 1 - c] + climbed(z, c, False) + climbed(z, c, True)
        for z in range(8)
        for c in range(2)
    ],
    np.int32,
)


def hop(value, which, step):
    return lax.ppermute(value, ("mb", "tp"), HOPS[which, step])


def around(value, which):
    return hop(value, which, 1), hop(value, which, -1), hop(value, which, 2)


def line(value, axis, step):
    return lax.ppermute(value, ("mb", "tp"), LINES[axis, step])


def after(value, *others):
    return lax.optimization_barrier((value, *others))[0]


def cost(flops, moved):
    return pl.CostEstimate(flops=flops, bytes_accessed=moved, transcendentals=0)


def params(mib):
    return pltpu.CompilerParams(vmem_limit_bytes=mib * MIB)


VMEM = pl.BlockSpec(memory_space=pltpu.VMEM)
SMEM = pl.BlockSpec(memory_space=pltpu.SMEM)
ANY = pl.BlockSpec(memory_space=pl.ANY)
HBM = pl.BlockSpec(memory_space=pltpu.HBM)


def merge_kernel(p_ref, gain_ref, bias_ref, out_ref, rows):
    values = p_ref[...].astype(F32)
    center = values - jnp.mean(values, axis=-1, keepdims=True)
    spread = jnp.mean(center * center, axis=-1, keepdims=True)
    normal = center * lax.rsqrt(spread + 1e-06) * gain_ref[...].reshape(1, 1280) + bias_ref[...].reshape(1, 1280)
    for k in range(10):
        rows[k] = normal[:, k * 128 : (k + 1) * 128]
    for j in range(4):
        for k in range(10):
            start = j * 1280 + k * 128
            out_ref[:, start : start + 128] = rows[k, pl.ds(j, 16, stride=4), :].astype(BF16)


def merge(patches, gain, bias):
    return pl.pallas_call(
        merge_kernel,
        out_shape=jax.ShapeDtypeStruct((16, 5120), BF16),
        in_specs=[VMEM] * 3,
        out_specs=VMEM,
        scratch_shapes=[pltpu.VMEM((10, 64, 128), F32)],
        compiler_params=params(8),
        cost_estimate=cost(10**6, 330000),
    )(patches, gain, bias)


def pack_kernel(tab, *refs):
    for source, target in zip(refs[:4], refs[4:]):
        target[...] = source[...]


def pack(tab, text):
    def columns(i2):
        return pl.BlockSpec((128, 512), lambda j, tab: (0, tab[i2 * 4 + j]))

    return pl.pallas_call(
        pack_kernel,
        out_shape=[jax.ShapeDtypeStruct((128, 2048), BF16)] * 4,
        grid_spec=pltpu.PrefetchScalarGridSpec(
            num_scalar_prefetch=1,
            grid=(4,),
            in_specs=[columns(i2) for i2 in range(4)],
            out_specs=[pl.BlockSpec((128, 512), lambda j, tab: (0, j))] * 4,
        ),
        compiler_params=params(8),
        cost_estimate=cost(0, 4 * MIB),
    )(tab, text, text, text, text)


def start(copies, sems):
    copies = [pltpu.make_async_copy(a, b, sems.at[i]) for i, (a, b) in enumerate(copies)]
    for copy in copies:
        copy.start()
    return copies


def up_kernel(tab, stack, s0, s1, s2, s3, *rest):
    *weights, bias_ref, out_ref, rows, held, sems = rest
    copies = [(piece, rows.at[pl.ds(i * 64, 64)]) for i, piece in enumerate((s0, s1, s2, s3))]
    blocks = list(weights[:2]) + [w.at[k] for w in weights[2:] for k in range(w.shape[0])]
    for k, block in enumerate(blocks):
        copies.append((block, held.at[pl.ds(pl.multiple_of(stack[k] * 320, 320), 320)]))
    for copy in start(copies, sems):
        copy.wait()
    raised = bias_ref[tab[0]] + jnp.dot(rows[...], held[...], preferred_element_type=F32)
    hidden = (0.5 * raised * (1.0 + lax.erf(raised * np.float32(0.5**0.5)))).astype(BF16)
    for k in range(16):
        out_ref[pl.ds(pl.multiple_of(tab[k] * 16, 16), 16), :] = hidden[k * 16 : (k + 1) * 16]


def up(tab, stack, pieces, weights, bias):
    return pl.pallas_call(
        up_kernel,
        out_shape=jax.ShapeDtypeStruct((256, 320), BF16),
        in_specs=[SMEM] * 2 + [ANY] * 14 + [VMEM],
        out_specs=VMEM,
        scratch_shapes=[
            pltpu.VMEM((256, 5120), BF16),
            pltpu.VMEM((5120, 320), BF16),
            pltpu.SemaphoreType.DMA((20,)),
        ],
        compiler_params=params(24),
        cost_estimate=cost(840 * 10**6, 6 * MIB),
    )(tab, stack, *pieces, *weights, bias)


def down_kernel(nat, h0, h1, h2, h3, weight, own, left, right, far, units, held, sems):
    copies = []
    for k, piece in enumerate((h0, h1, h2, h3)):
        copies.append((piece, units.at[k]))
        for j in range(4):
            slot = nat[j * 4] // 4 * 4 + nat[k] % 4
            source = weight.at[pl.ds(pl.multiple_of(slot * 320, 320), 320)]
            copies.append((source, held.at[k, :, pl.ds(j * 512, 512)]))
    copies = start(copies, sems)
    total = 0.0
    for k in range(4):
        for copy in copies[k * 5 : k * 5 + 5]:
            copy.wait()
        total = total + jnp.dot(units[k], held[k], preferred_element_type=F32)
    own[...] = total[:, 0:512]
    left[...] = total[:, 512:1024].astype(BF16)
    right[...] = total[:, 1024:1536].astype(BF16)
    far[...] = total[:, 1536:2048].astype(BF16)


def down(nat, pieces, weight):
    return pl.pallas_call(
        down_kernel,
        out_shape=[jax.ShapeDtypeStruct((256, 512), F32)] + [jax.ShapeDtypeStruct((256, 512), BF16)] * 3,
        in_specs=[SMEM] + [ANY] * 5,
        out_specs=[VMEM] * 4,
        scratch_shapes=[
            pltpu.VMEM((4, 256, 320), BF16),
            pltpu.VMEM((4, 320, 2048), BF16),
            pltpu.SemaphoreType.DMA((20,)),
        ],
        compiler_params=params(56),
        cost_estimate=cost(1340 * 10**6, 8 * MIB),
    )(nat, *pieces, weight)


def pick_kernel(tab, dest, v0, v1, v2, v3, *refs):
    visual = (v0[...], v1[...], v2[...], v3[...])
    targets = dest[...]
    for i2 in (3, 2, 1, 0):
        text, out = refs[i2], refs[4 + i2]
        match = (lax.broadcasted_iota(jnp.int32, (128, 256), 0) + tab[i2 * 4] * 128) == targets
        select = match.astype(F32)
        present = jnp.sum(select, axis=1, keepdims=True) > 0.0
        select = select.astype(BF16)
        for j in range(4):
            at = slice(j * 512, (j + 1) * 512)
            picked = jnp.dot(select, visual[j], preferred_element_type=F32).astype(BF16)
            out[:, at] = jnp.where(present, picked, text[:, at])


def pick(tab, dest, visual, text):
    return pl.pallas_call(
        pick_kernel,
        out_shape=[jax.ShapeDtypeStruct((128, 2048), BF16)] * 4,
        in_specs=[SMEM] + [VMEM] * 9,
        out_specs=[VMEM] * 4,
        compiler_params=params(32),
        cost_estimate=cost(540 * 10**6, 6 * MIB),
    )(tab, dest, *visual, *text)


def product_kernel(tab, e0, e1, e2, e3, gain, w0, w1, w2, w3a, w3b, own, left, right, far, scaled):
    @pl.when(pl.program_id(0) == 0)
    def _():
        for j in range(4):
            at = slice(j * 512, (j + 1) * 512)
            scale = gain[tab[j]]
            for i2, rows in enumerate((e0, e1, e2, e3)):
                scaled[i2 * 128 : (i2 + 1) * 128, at] = (rows[:, at].astype(F32) * scale).astype(BF16)

    total = jnp.dot(scaled[:, 0:512], w0[...], preferred_element_type=F32)
    total = total + jnp.dot(scaled[:, 512:1024], w1[...], preferred_element_type=F32)
    total = total + jnp.dot(scaled[:, 1024:1536], w2[...], preferred_element_type=F32)
    total = total + jnp.dot(scaled[:, 1536:1792], w3a[...], preferred_element_type=F32)
    total = total + jnp.dot(scaled[:, 1792:2048], w3b[...], preferred_element_type=F32)
    own[...] = total[0:128]
    left[...] = total[128:256].astype(BF16)
    right[...] = total[256:384].astype(BF16)
    far[...] = total[384:512].astype(BF16)


def product(tab, picked, gain, weights):
    def block(count):
        return pl.BlockSpec((count, 512), lambda n: (0, n))

    return pl.pallas_call(
        product_kernel,
        out_shape=[jax.ShapeDtypeStruct((128, 2048), F32)] + [jax.ShapeDtypeStruct((128, 2048), BF16)] * 3,
        grid=(4,),
        in_specs=[SMEM] + [VMEM] * 5 + [block(n) for n in (512, 512, 512, 256, 256)],
        out_specs=[block(128)] * 4,
        scratch_shapes=[pltpu.VMEM((512, 2048), BF16)],
        compiler_params=params(56),
        cost_estimate=cost(4300 * 10**6, 14 * MIB),
    )(tab, *picked, gain, *weights)


def place_kernel(tab, e0, e1, e2, e3, out, scale, sems):
    copies = []
    for i2, rows in enumerate((e0, e1, e2, e3)):
        for j in range(4):
            columns = pl.ds(pl.multiple_of(tab[i2 * 4 + j] * 512, 512), 512)
            copies.append((rows.at[:, pl.ds(j * 512, 512)], out.at[:, columns]))
    copies = start(copies, sems)
    total = 0.0
    for rows in (e0, e1, e2, e3):
        values = rows[...].astype(F32)
        total = total + jnp.sum(values * values, axis=1, keepdims=True)
    scale[...] = jnp.broadcast_to(lax.rsqrt(total * (1.0 / 8192.0) + 1e-06), (128, 128))
    for copy in copies:
        copy.wait()


def place_rows(tab, pieces):
    return pl.pallas_call(
        place_kernel,
        out_shape=[jax.ShapeDtypeStruct((128, 8192), BF16), jax.ShapeDtypeStruct((128, 128), F32)],
        in_specs=[SMEM] + [VMEM] * 4,
        out_specs=[ANY, VMEM],
        scratch_shapes=[pltpu.SemaphoreType.DMA((16,))],
        compiler_params=params(32),
        cost_estimate=cost(4 * 10**6, 30 * MIB),
    )(tab, *pieces)


def per_device(
    patches,
    patch_counts,
    dest_pos,
    merge_gain,
    merge_bias,
    up_weight,
    up_bias,
    down_weight,
    down_bias,
    text_embed,
    norm_gain,
    kv_weight,
    kv_bias,
):
    tab = jnp.asarray(TABLE)[lax.axis_index("mb") * 16 + lax.axis_index("tp")]
    nat = jnp.asarray(TABLE)[lax.axis_index("tp")]
    stack = jnp.asarray(STACK)[lax.axis_index("enc") * 2 + lax.axis_index("mb")]

    def climb(value):
        return lax.ppermute(value, ("enc", "mb"), CLIMB)

    def cross(value):
        return lax.ppermute(value, "mb", OTHER)

    down_part = lax.ppermute(down_weight, ("enc", "mb", "tp"), SHUFFLE)
    up_other = cross(up_weight)
    first = climb(jnp.stack([up_weight, up_other]))
    merged = merge(after(patches[0, 0], up_other), merge_gain, merge_bias)
    near = jnp.concatenate([merged, *around(merged, 1)], axis=0)
    near, first, down_part = lax.optimization_barrier((near, first, down_part))
    down_full = lax.all_gather(down_part, ("enc", "mb"), axis=0, tiled=True)
    second = climb(first)
    group = (near, *around(near, 2))
    third = climb(second)
    climbed = (first, second, third, climb(third[:1]))
    up_weights = (up_weight, up_other, *climbed, *[cross(value) for value in climbed])

    kv_weight = after(kv_weight, *group, third)
    kv_right, kv_left = hop(kv_weight, 1, 1), hop(kv_weight, 1, -1)
    far_right, far_left = kv_right[:256], kv_left[256:]
    own, to_left, to_right, to_far = pack(tab, text_embed[0, 0])
    hidden = up(tab, stack, group, up_weights, up_bias.reshape(16, 1, 320))
    units = (hidden, line(hidden, "x", 1), line(hidden, "x", -1), line(hidden, "x", 2))
    moved = (*units, far_right, far_left, to_left, to_right, to_far)
    *units, far_right, far_left, to_left, to_right, to_far = lax.optimization_barrier(moved)

    weights = (kv_weight, kv_right, kv_left, hop(far_right, 1, 1), hop(far_left, 1, -1))
    text = (own, hop(to_right, 2, 1), hop(to_left, 2, -1), hop(to_far, 2, 2))
    down_full = after(down_full, weights[3], weights[4], *text)
    own, to_left, to_right, to_far = down(nat, units, down_full)
    bias = lax.dynamic_slice_in_dim(down_bias, lax.axis_index("tp") * 512, 512, 0)
    total = own + bias
    for value in (line(to_far, "y", 2), line(to_right, "y", 1), line(to_left, "y", -1)):
        total = total + value.astype(F32)
    visual = total.astype(BF16)
    visual = (visual, *around(visual, 1))

    live_rows = patch_counts[0, 0] // 4
    live = (jnp.arange(SLOT, dtype=jnp.int32)[None, :] < live_rows[:, None]).reshape(-1)
    dest = jnp.where(live, dest_pos[0, 0], -1)[None]
    picked = pick(tab, dest, visual, text)
    pieces = (picked[0], hop(picked[2], 2, 1), hop(picked[1], 2, -1), hop(picked[3], 2, 2))
    own, to_left, to_right, to_far = product(tab, picked, norm_gain.reshape(16, 1, 512), weights)
    sums = (hop(to_far, 2, 2), hop(to_right, 2, 1), hop(to_left, 2, -1))
    embedded, scale = place_rows(tab, pieces)
    total = own
    for value in sums:
        total = total + value.astype(F32)
    keys_values = (total * scale[:, :1] + kv_bias).astype(BF16)
    return (embedded[None, None], keys_values[None, None])


def solution(mesh):
    return jax.shard_map(
        per_device,
        mesh=mesh,
        in_specs=(
            P("enc", "mb", "tp", None),
            P("enc", "mb", None),
            P("enc", "mb", None),
            P(),
            P(),
            P(("enc", "mb"), "tp"),
            P(),
            P("tp", ("enc", "mb")),
            P(),
            P("enc", "mb", "tp", None),
            P(),
            P("tp", None),
            P(),
        ),
        out_specs=(P("enc", "mb", "tp", None), P("enc", "mb", "tp", None)),
        check_vma=False,
    )
```

```python
import jax
import jax.numpy as jnp
import numpy as np
from jax import lax
from jax.experimental import pallas as pl
from jax.experimental.pallas import tpu as pltpu
from jax.sharding import PartitionSpec as P

SLOT = 8
RING = (0, -1, 1, 2)
MIB = 1 << 20
BF16, F32 = jnp.bfloat16, jnp.float32


def place(core, tp, which, step):
    y, x = tp // 4, tp % 4
    if (core == 0) == (which == 1):
        return y * 4 + (x + step) % 4
    return (y + step) % 4 * 4 + x


TABLE = np.array(
    [
        [place(core, place(core, tp, 2, o2), 1, o1) for o2 in RING for o1 in RING]
        for core in range(2)
        for tp in range(16)
    ],
    np.int32,
)
HOPS = {
    (which, step): [(c * 16 + t, c * 16 + place(c, t, which, step)) for c in range(2) for t in range(16)]
    for which in (1, 2)
    for step in (1, -1, 2)
}
LINES = {
    (axis, step): [
        (c * 16 + t, c * 16 + place(1 if axis == "y" else 0, t, 1, step)) for c in range(2) for t in range(16)
    ]
    for axis in "yx"
    for step in (1, -1, 2)
}
SHUFFLE = [
    ((z * 2 + c) * 16 + y * 4 + x, (z // 2 * 4 + x) * 16 + y * 4 + z % 2 * 2 + c)
    for z in range(8)
    for c in range(2)
    for y in range(4)
    for x in range(4)
]


def hop(value, which, step):
    return lax.ppermute(value, ("mb", "tp"), HOPS[which, step])


def around(value, which):
    return hop(value, which, 1), hop(value, which, -1), hop(value, which, 2)


def line(value, axis, step):
    return lax.ppermute(value, ("mb", "tp"), LINES[axis, step])


def after(value, *others):
    return lax.optimization_barrier((value, *others))[0]


def cost(flops, moved):
    return pl.CostEstimate(flops=flops, bytes_accessed=moved, transcendentals=0)


def params(mib):
    return pltpu.CompilerParams(vmem_limit_bytes=mib * MIB)


VMEM = pl.BlockSpec(memory_space=pltpu.VMEM)
SMEM = pl.BlockSpec(memory_space=pltpu.SMEM)
ANY = pl.BlockSpec(memory_space=pl.ANY)
HBM = pl.BlockSpec(memory_space=pltpu.HBM)


def merge_kernel(p_ref, gain_ref, bias_ref, out_ref, rows):
    values = p_ref[...].astype(F32)
    center = values - jnp.mean(values, axis=-1, keepdims=True)
    spread = jnp.mean(center * center, axis=-1, keepdims=True)
    normal = center * lax.rsqrt(spread + 1e-06) * gain_ref[...].reshape(1, 1280) + bias_ref[...].reshape(1, 1280)
    for k in range(10):
        rows[k] = normal[:, k * 128 : (k + 1) * 128]
    for j in range(4):
        for k in range(10):
            start = j * 1280 + k * 128
            out_ref[:, start : start + 128] = rows[k, pl.ds(j, 16, stride=4), :].astype(BF16)


def merge(patches, gain, bias):
    return pl.pallas_call(
        merge_kernel,
        out_shape=jax.ShapeDtypeStruct((16, 5120), BF16),
        in_specs=[VMEM] * 3,
        out_specs=VMEM,
        scratch_shapes=[pltpu.VMEM((10, 64, 128), F32)],
        compiler_params=params(8),
        cost_estimate=cost(10**6, 330000),
    )(patches, gain, bias)


def pack_kernel(tab, *refs):
    for source, target in zip(refs[:4], refs[4:]):
        target[...] = source[...]


def pack(tab, text):
    def columns(i2):
        return pl.BlockSpec((128, 512), lambda j, tab: (0, tab[i2 * 4 + j]))

    return pl.pallas_call(
        pack_kernel,
        out_shape=[jax.ShapeDtypeStruct((128, 2048), BF16)] * 4,
        grid_spec=pltpu.PrefetchScalarGridSpec(
            num_scalar_prefetch=1,
            grid=(4,),
            in_specs=[columns(i2) for i2 in range(4)],
            out_specs=[pl.BlockSpec((128, 512), lambda j, tab: (0, j))] * 4,
        ),
        compiler_params=params(8),
        cost_estimate=cost(0, 4 * MIB),
    )(tab, text, text, text, text)


def start(copies, sems):
    copies = [pltpu.make_async_copy(a, b, sems.at[i]) for i, (a, b) in enumerate(copies)]
    for copy in copies:
        copy.start()
    return copies


def up_kernel(tab, s0, s1, s2, s3, weight, bias_ref, out_ref, rows, held, sems):
    copies = [(piece, rows.at[pl.ds(i * 64, 64)]) for i, piece in enumerate((s0, s1, s2, s3))]
    copies += [(weight.at[pl.ds(k * 1024, 1024)], held.at[pl.ds(k * 1024, 1024)]) for k in range(5)]
    copies = start(copies, sems)
    for copy in copies[:4]:
        copy.wait()
    raised = bias_ref[tab[0]]
    for k in range(5):
        copies[4 + k].wait()
        at = slice(k * 1024, (k + 1) * 1024)
        raised = raised + jnp.dot(rows[:, at], held[at, :], preferred_element_type=F32)
    hidden = (0.5 * raised * (1.0 + lax.erf(raised * np.float32(0.5**0.5)))).astype(BF16)
    for k in range(16):
        out_ref[pl.ds(pl.multiple_of(tab[k] * 16, 16), 16), :] = hidden[k * 16 : (k + 1) * 16]


def up(tab, pieces, weight, bias):
    return pl.pallas_call(
        up_kernel,
        out_shape=jax.ShapeDtypeStruct((256, 320), BF16),
        in_specs=[SMEM] + [ANY] * 5 + [VMEM],
        out_specs=VMEM,
        scratch_shapes=[
            pltpu.VMEM((256, 5120), BF16),
            pltpu.VMEM((5120, 320), BF16),
            pltpu.SemaphoreType.DMA((9,)),
        ],
        compiler_params=params(56),
        cost_estimate=cost(840 * 10**6, 6 * MIB),
    )(tab, *pieces, weight, bias)


def down_kernel(nat, h0, h1, h2, h3, weight, own, left, right, far, units, held, sems):
    copies = []
    for k, piece in enumerate((h0, h1, h2, h3)):
        copies.append((piece, units.at[k]))
        for j in range(4):
            slot = nat[j * 4] // 4 * 4 + nat[k] % 4
            source = weight.at[pl.ds(pl.multiple_of(slot * 320, 320), 320)]
            copies.append((source, held.at[k, :, pl.ds(j * 512, 512)]))
    copies = start(copies, sems)
    total = 0.0
    for k in range(4):
        for copy in copies[k * 5 : k * 5 + 5]:
            copy.wait()
        total = total + jnp.dot(units[k], held[k], preferred_element_type=F32)
    own[...] = total[:, 0:512]
    left[...] = total[:, 512:1024].astype(BF16)
    right[...] = total[:, 1024:1536].astype(BF16)
    far[...] = total[:, 1536:2048].astype(BF16)


def down(nat, pieces, weight):
    return pl.pallas_call(
        down_kernel,
        out_shape=[jax.ShapeDtypeStruct((256, 512), F32)] + [jax.ShapeDtypeStruct((256, 512), BF16)] * 3,
        in_specs=[SMEM] + [ANY] * 5,
        out_specs=[VMEM] * 4,
        scratch_shapes=[
            pltpu.VMEM((4, 256, 320), BF16),
            pltpu.VMEM((4, 320, 2048), BF16),
            pltpu.SemaphoreType.DMA((20,)),
        ],
        compiler_params=params(56),
        cost_estimate=cost(1340 * 10**6, 8 * MIB),
    )(nat, *pieces, weight)


def pick_kernel(tab, dest, v0, v1, v2, v3, *refs):
    visual = (v0[...], v1[...], v2[...], v3[...])
    targets = dest[...]
    for i2 in (3, 2, 1, 0):
        text, out = refs[i2], refs[4 + i2]
        match = (lax.broadcasted_iota(jnp.int32, (128, 256), 0) + tab[i2 * 4] * 128) == targets
        select = match.astype(F32)
        present = jnp.sum(select, axis=1, keepdims=True) > 0.0
        select = select.astype(BF16)
        for j in range(4):
            at = slice(j * 512, (j + 1) * 512)
            picked = jnp.dot(select, visual[j], preferred_element_type=F32).astype(BF16)
            out[:, at] = jnp.where(present, picked, text[:, at])


def pick(tab, dest, visual, text):
    return pl.pallas_call(
        pick_kernel,
        out_shape=[jax.ShapeDtypeStruct((128, 2048), BF16)] * 4,
        in_specs=[SMEM] + [VMEM] * 9,
        out_specs=[VMEM] * 4,
        compiler_params=params(32),
        cost_estimate=cost(540 * 10**6, 6 * MIB),
    )(tab, dest, *visual, *text)


def scaled_rows(gain, tab, j, rows):
    return (rows[:, j * 512 : (j + 1) * 512].astype(F32) * gain[tab[j]]).astype(BF16)


def text_kernel(tab, t0, t1, t2, t3, gain, w0, w1, w2, out, scaled):
    @pl.when(pl.program_id(0) == 0)
    def _():
        for i2, rows in enumerate((t0, t1, t2, t3)):
            for j in range(3):
                scaled[i2 * 128 : (i2 + 1) * 128, j * 512 : (j + 1) * 512] = scaled_rows(gain, tab, j, rows)

    total = jnp.dot(scaled[:, 0:512], w0[...], preferred_element_type=F32)
    total = total + jnp.dot(scaled[:, 512:1024], w1[...], preferred_element_type=F32)
    out[...] = total + jnp.dot(scaled[:, 1024:1536], w2[...], preferred_element_type=F32)


def text_far_kernel(tab, t0, t1, t2, t3, gain, near, w3a, w3b, out, scaled):
    @pl.when(pl.program_id(0) == 0)
    def _():
        for i2, rows in enumerate((t0, t1, t2, t3)):
            scaled[i2 * 128 : (i2 + 1) * 128, :] = scaled_rows(gain, tab, 3, rows)

    total = near[...] + jnp.dot(scaled[:, 0:256], w3a[...], preferred_element_type=F32)
    total = total + jnp.dot(scaled[:, 256:512], w3b[...], preferred_element_type=F32)
    out[...] = total.astype(BF16)


def block(count):
    return pl.BlockSpec((count, 512), lambda n: (0, n))


def text_product(tab, text, gain, weights):
    return pl.pallas_call(
        text_kernel,
        out_shape=jax.ShapeDtypeStruct((512, 2048), F32),
        grid=(4,),
        in_specs=[SMEM] + [VMEM] * 5 + [block(512)] * 3,
        out_specs=block(512),
        scratch_shapes=[pltpu.VMEM((512, 1536), BF16)],
        compiler_params=params(28),
        cost_estimate=cost(3200 * 10**6, 14 * MIB),
    )(tab, *text, gain, *weights)


def text_far_product(tab, text, gain, near, weights):
    return pl.pallas_call(
        text_far_kernel,
        out_shape=jax.ShapeDtypeStruct((512, 2048), BF16),
        grid=(4,),
        in_specs=[SMEM] + [VMEM] * 5 + [block(512)] + [block(256)] * 2,
        out_specs=block(512),
        scratch_shapes=[pltpu.VMEM((512, 512), BF16)],
        compiler_params=params(28),
        cost_estimate=cost(1100 * 10**6, 8 * MIB),
    )(tab, *text, gain, near, *weights)


def product_kernel(tab, dest, v0, v1, v2, v3, gain, text, w0, w1, w2, w3a, w3b, own, left, right, far, scaled, select):
    @pl.when(pl.program_id(0) == 0)
    def _():
        for j, visual in enumerate((v0, v1, v2, v3)):
            scaled[:, j * 512 : (j + 1) * 512] = (visual[...].astype(F32) * gain[tab[j]]).astype(BF16)
        for i2 in range(4):
            places = lax.broadcasted_iota(jnp.int32, (128, 256), 0) + tab[i2 * 4] * 128
            select[i2 * 128 : (i2 + 1) * 128, :] = (places == dest[...]).astype(F32).astype(BF16)

    total = jnp.dot(scaled[:, 0:512], w0[...], preferred_element_type=F32)
    total = total + jnp.dot(scaled[:, 512:1024], w1[...], preferred_element_type=F32)
    total = total + jnp.dot(scaled[:, 1024:1536], w2[...], preferred_element_type=F32)
    total = total + jnp.dot(scaled[:, 1536:1792], w3a[...], preferred_element_type=F32)
    total = total + jnp.dot(scaled[:, 1792:2048], w3b[...], preferred_element_type=F32)
    total = total.astype(BF16)
    for i2, out in ((3, far), (2, right), (1, left), (0, own)):
        rows = slice(i2 * 128, (i2 + 1) * 128)
        chosen = select[rows, :]
        present = jnp.sum(chosen.astype(F32), axis=1, keepdims=True) > 0.0
        picked = jnp.dot(chosen, total, preferred_element_type=F32).astype(BF16)
        out[...] = jnp.where(present, picked, text[rows, :])


def product(tab, dest, visual, gain, text, weights):
    return pl.pallas_call(
        product_kernel,
        out_shape=[jax.ShapeDtypeStruct((128, 2048), BF16)] * 4,
        grid=(4,),
        in_specs=[SMEM] + [VMEM] * 6 + [block(n) for n in (512, 512, 512, 512, 256, 256)],
        out_specs=[block(128)] * 4,
        scratch_shapes=[pltpu.VMEM((256, 2048), BF16), pltpu.VMEM((512, 256), BF16)],
        compiler_params=params(28),
        cost_estimate=cost(2700 * 10**6, 14 * MIB),
    )(tab, dest, *visual, gain, text, *weights)


def place_kernel(tab, e0, e1, e2, e3, out, scale, sems):
    copies = []
    for i2, rows in enumerate((e0, e1, e2, e3)):
        for j in range(4):
            columns = pl.ds(pl.multiple_of(tab[i2 * 4 + j] * 512, 512), 512)
            copies.append((rows.at[:, pl.ds(j * 512, 512)], out.at[:, columns]))
    copies = start(copies, sems)
    total = 0.0
    for rows in (e0, e1, e2, e3):
        values = rows[...].astype(F32)
        total = total + jnp.sum(values * values, axis=1, keepdims=True)
    scale[...] = jnp.broadcast_to(lax.rsqrt(total * (1.0 / 8192.0) + 1e-06), (128, 128))
    for copy in copies:
        copy.wait()


def place_rows(tab, pieces):
    return pl.pallas_call(
        place_kernel,
        out_shape=[jax.ShapeDtypeStruct((128, 8192), BF16), jax.ShapeDtypeStruct((128, 128), F32)],
        in_specs=[SMEM] + [VMEM] * 4,
        out_specs=[ANY, VMEM],
        scratch_shapes=[pltpu.SemaphoreType.DMA((16,))],
        compiler_params=params(32),
        cost_estimate=cost(4 * 10**6, 30 * MIB),
    )(tab, *pieces)


def per_device(
    patches,
    patch_counts,
    dest_pos,
    merge_gain,
    merge_bias,
    up_weight,
    up_bias,
    down_weight,
    down_bias,
    text_embed,
    norm_gain,
    kv_weight,
    kv_bias,
):
    tab = jnp.asarray(TABLE)[lax.axis_index("mb") * 16 + lax.axis_index("tp")]
    nat = jnp.asarray(TABLE)[lax.axis_index("tp")]
    up_full = lax.all_gather(up_weight, ("enc", "mb"), axis=0, tiled=True)
    down_part = lax.ppermute(down_weight, ("enc", "mb", "tp"), SHUFFLE)

    merged = merge(patches[0, 0], merge_gain, merge_bias)
    near = jnp.concatenate([merged, *around(merged, 1)], axis=0)
    group = (near, *around(near, 2))
    down_full = lax.all_gather(after(down_part, *group), ("enc", "mb"), axis=0, tiled=True)

    kv_weight = after(kv_weight, *group)
    kv_right, kv_left = hop(kv_weight, 1, 1), hop(kv_weight, 1, -1)
    far_right, far_left = kv_right[:256], kv_left[256:]
    own, to_left, to_right, to_far = pack(tab, text_embed[0, 0])
    hidden = up(tab, group, up_full, up_bias.reshape(16, 1, 320))
    units = (hidden, line(hidden, "x", 1), line(hidden, "x", -1), line(hidden, "x", 2))
    text = (own, hop(to_right, 2, 1), hop(to_left, 2, -1), hop(to_far, 2, 2))
    *units, far_right, far_left = lax.optimization_barrier((*units, far_right, far_left, *text))[:6]
    far = (hop(far_right, 1, 1), hop(far_left, 1, -1))
    gain = norm_gain.reshape(16, 1, 512)
    text_sums = text_product(tab, text, gain, (kv_weight, kv_right, kv_left))
    down_full, *far = lax.optimization_barrier((down_full, *far, text_sums))[:3]
    own, to_left, to_right, to_far = down(nat, units, down_full)
    text_sums = text_far_product(tab, text, gain, after(text_sums, to_far), far)
    bias = lax.dynamic_slice_in_dim(down_bias, lax.axis_index("tp") * 512, 512, 0)
    total = own + bias
    for value in (line(to_far, "y", 2), line(to_right, "y", 1), line(to_left, "y", -1)):
        total = total + value.astype(F32)
    visual = total.astype(BF16)
    visual = (visual, *around(after(visual, text_sums), 1))
    weights = (kv_weight, kv_right, kv_left, *far)

    live_rows = patch_counts[0, 0] // 4
    live = (jnp.arange(SLOT, dtype=jnp.int32)[None, :] < live_rows[:, None]).reshape(-1)
    dest = jnp.where(live, dest_pos[0, 0], -1)[None]
    picked = pick(tab, dest, visual, text)
    pieces = (picked[0], hop(picked[2], 2, 1), hop(picked[1], 2, -1), hop(picked[3], 2, 2))
    own, to_left, to_right, to_far = product(tab, dest, visual, gain, text_sums, weights)
    sums = (hop(to_far, 2, 2), hop(to_right, 2, 1), hop(to_left, 2, -1))
    embedded, scale = place_rows(tab, pieces)
    total = own.astype(F32)
    for value in sums:
        total = total + value.astype(F32)
    keys_values = (total * scale[:, :1] + kv_bias).astype(BF16)
    return (embedded[None, None], keys_values[None, None])


def solution(mesh):
    return jax.shard_map(
        per_device,
        mesh=mesh,
        in_specs=(
            P("enc", "mb", "tp", None),
            P("enc", "mb", None),
            P("enc", "mb", None),
            P(),
            P(),
            P(("enc", "mb"), "tp"),
            P(),
            P("tp", ("enc", "mb")),
            P(),
            P("enc", "mb", "tp", None),
            P(),
            P("tp", None),
            P(),
        ),
        out_specs=(P("enc", "mb", "tp", None), P("enc", "mb", "tp", None)),
        check_vma=False,
    )
```

```python
import jax
import jax.numpy as jnp
import numpy as np
from jax import lax
from jax.experimental import pallas as pl
from jax.experimental.pallas import tpu as pltpu
from jax.sharding import PartitionSpec as P

SLOT = 8
RING = (0, -1, 1, 2)
MIB = 1 << 20
BF16, F32 = jnp.bfloat16, jnp.float32


def place(core, tp, which, step):
    y, x = tp // 4, tp % 4
    if (core == 0) == (which == 1):
        return y * 4 + (x + step) % 4
    return (y + step) % 4 * 4 + x


TABLE = np.array(
    [
        [place(core, place(core, tp, 2, o2), 1, o1) for o2 in RING for o1 in RING]
        for core in range(2)
        for tp in range(16)
    ],
    np.int32,
)
HOPS = {
    (which, step): [(c * 16 + t, c * 16 + place(c, t, which, step)) for c in range(2) for t in range(16)]
    for which in (1, 2)
    for step in (1, -1, 2)
}
LINES = {
    (axis, step): [
        (c * 16 + t, c * 16 + place(1 if axis == "y" else 0, t, 1, step)) for c in range(2) for t in range(16)
    ]
    for axis in "yx"
    for step in (1, -1, 2)
}
SHUFFLE = [
    ((z * 2 + c) * 16 + y * 4 + x, (z // 2 * 4 + x) * 16 + y * 4 + z % 2 * 2 + c)
    for z in range(8)
    for c in range(2)
    for y in range(4)
    for x in range(4)
]


def hop(value, which, step):
    return lax.ppermute(value, ("mb", "tp"), HOPS[which, step])


def around(value, which):
    return hop(value, which, 1), hop(value, which, -1), hop(value, which, 2)


def line(value, axis, step):
    return lax.ppermute(value, ("mb", "tp"), LINES[axis, step])


def after(value, *others):
    return lax.optimization_barrier((value, *others))[0]


def cost(flops, moved):
    return pl.CostEstimate(flops=flops, bytes_accessed=moved, transcendentals=0)


def params(mib):
    return pltpu.CompilerParams(vmem_limit_bytes=mib * MIB)


VMEM = pl.BlockSpec(memory_space=pltpu.VMEM)
SMEM = pl.BlockSpec(memory_space=pltpu.SMEM)
ANY = pl.BlockSpec(memory_space=pl.ANY)
HBM = pl.BlockSpec(memory_space=pltpu.HBM)


def merge_kernel(p_ref, gain_ref, bias_ref, out_ref, rows):
    values = p_ref[...].astype(F32)
    center = values - jnp.mean(values, axis=-1, keepdims=True)
    spread = jnp.mean(center * center, axis=-1, keepdims=True)
    normal = center * lax.rsqrt(spread + 1e-06) * gain_ref[...].reshape(1, 1280) + bias_ref[...].reshape(1, 1280)
    for k in range(10):
        rows[k] = normal[:, k * 128 : (k + 1) * 128]
    for j in range(4):
        for k in range(10):
            start = j * 1280 + k * 128
            out_ref[:, start : start + 128] = rows[k, pl.ds(j, 16, stride=4), :].astype(BF16)


def merge(patches, gain, bias):
    return pl.pallas_call(
        merge_kernel,
        out_shape=jax.ShapeDtypeStruct((16, 5120), BF16),
        in_specs=[VMEM] * 3,
        out_specs=VMEM,
        scratch_shapes=[pltpu.VMEM((10, 64, 128), F32)],
        compiler_params=params(8),
        cost_estimate=cost(10**6, 330000),
    )(patches, gain, bias)


def pack_kernel(tab, *refs):
    for source, target in zip(refs[:4], refs[4:]):
        target[...] = source[...]


def pack(tab, text):
    def columns(i2):
        return pl.BlockSpec((128, 512), lambda j, tab: (0, tab[i2 * 4 + j]))

    return pl.pallas_call(
        pack_kernel,
        out_shape=[jax.ShapeDtypeStruct((128, 2048), BF16)] * 4,
        grid_spec=pltpu.PrefetchScalarGridSpec(
            num_scalar_prefetch=1,
            grid=(4,),
            in_specs=[columns(i2) for i2 in range(4)],
            out_specs=[pl.BlockSpec((128, 512), lambda j, tab: (0, j))] * 4,
        ),
        compiler_params=params(8),
        cost_estimate=cost(0, 4 * MIB),
    )(tab, text, text, text, text)


def start(copies, sems):
    copies = [pltpu.make_async_copy(a, b, sems.at[i]) for i, (a, b) in enumerate(copies)]
    for copy in copies:
        copy.start()
    return copies


def up_kernel(tab, s0, s1, s2, s3, weight, bias_ref, out_ref, rows, held, sems):
    copies = [(piece, rows.at[pl.ds(i * 64, 64)]) for i, piece in enumerate((s0, s1, s2, s3))]
    copies += [
        (weight.at[pl.ds(k * 1024, 1024), pl.ds(512, 320)], held.at[pl.ds(k * 1024, 1024)]) for k in range(5)
    ]
    copies = start(copies, sems)
    for copy in copies[:4]:
        copy.wait()
    raised = bias_ref[tab[0]]
    for k in range(5):
        copies[4 + k].wait()
        at = slice(k * 1024, (k + 1) * 1024)
        raised = raised + jnp.dot(rows[:, at], held[at, :], preferred_element_type=F32)
    hidden = (0.5 * raised * (1.0 + lax.erf(raised * np.float32(0.5**0.5)))).astype(BF16)
    for k in range(16):
        out_ref[pl.ds(pl.multiple_of(tab[k] * 16, 16), 16), :] = hidden[k * 16 : (k + 1) * 16]


def up(tab, pieces, weight, bias):
    return pl.pallas_call(
        up_kernel,
        out_shape=jax.ShapeDtypeStruct((256, 320), BF16),
        in_specs=[SMEM] + [ANY] * 5 + [VMEM],
        out_specs=VMEM,
        scratch_shapes=[
            pltpu.VMEM((256, 5120), BF16),
            pltpu.VMEM((5120, 320), BF16),
            pltpu.SemaphoreType.DMA((9,)),
        ],
        compiler_params=params(56),
        cost_estimate=cost(840 * 10**6, 6 * MIB),
    )(tab, *pieces, weight, bias)


def down_kernel(nat, h0, h1, h2, h3, weight, own, left, right, far, units, held, sems):
    copies = []
    for k, piece in enumerate((h0, h1, h2, h3)):
        copies.append((piece, units.at[k]))
        for j in range(4):
            slot = nat[j * 4] // 4 * 4 + nat[k] % 4
            source = weight.at[pl.ds(pl.multiple_of(slot * 320, 320), 320), pl.ds(0, 512)]
            copies.append((source, held.at[k, :, pl.ds(j * 512, 512)]))
    copies = start(copies, sems)
    total = 0.0
    for k in range(4):
        for copy in copies[k * 5 : k * 5 + 5]:
            copy.wait()
        total = total + jnp.dot(units[k], held[k], preferred_element_type=F32)
    own[...] = total[:, 0:512]
    left[...] = total[:, 512:1024].astype(BF16)
    right[...] = total[:, 1024:1536].astype(BF16)
    far[...] = total[:, 1536:2048].astype(BF16)


def down(nat, pieces, weight):
    return pl.pallas_call(
        down_kernel,
        out_shape=[jax.ShapeDtypeStruct((256, 512), F32)] + [jax.ShapeDtypeStruct((256, 512), BF16)] * 3,
        in_specs=[SMEM] + [ANY] * 5,
        out_specs=[VMEM] * 4,
        scratch_shapes=[
            pltpu.VMEM((4, 256, 320), BF16),
            pltpu.VMEM((4, 320, 2048), BF16),
            pltpu.SemaphoreType.DMA((20,)),
        ],
        compiler_params=params(56),
        cost_estimate=cost(1340 * 10**6, 8 * MIB),
    )(nat, *pieces, weight)


def pick_kernel(tab, dest, v0, v1, v2, v3, *refs):
    visual = (v0[...], v1[...], v2[...], v3[...])
    targets = dest[...]
    for i2 in (3, 2, 1, 0):
        text, out = refs[i2], refs[4 + i2]
        match = (lax.broadcasted_iota(jnp.int32, (128, 256), 0) + tab[i2 * 4] * 128) == targets
        select = match.astype(F32)
        present = jnp.sum(select, axis=1, keepdims=True) > 0.0
        select = select.astype(BF16)
        for j in range(4):
            at = slice(j * 512, (j + 1) * 512)
            picked = jnp.dot(select, visual[j], preferred_element_type=F32).astype(BF16)
            out[:, at] = jnp.where(present, picked, text[:, at])


def pick(tab, dest, visual, text):
    return pl.pallas_call(
        pick_kernel,
        out_shape=[jax.ShapeDtypeStruct((128, 2048), BF16)] * 4,
        in_specs=[SMEM] + [VMEM] * 9,
        out_specs=[VMEM] * 4,
        compiler_params=params(32),
        cost_estimate=cost(540 * 10**6, 6 * MIB),
    )(tab, dest, *visual, *text)


def scaled_rows(gain, tab, j, rows):
    return (rows[:, j * 512 : (j + 1) * 512].astype(F32) * gain[tab[j]]).astype(BF16)


def text_kernel(tab, t0, t1, t2, t3, gain, w0, w1, w2, w3a, w3b, out, scaled):
    @pl.when(pl.program_id(0) == 0)
    def _():
        for i2, rows in enumerate((t0, t1, t2, t3)):
            for j in range(4):
                scaled[i2 * 128 : (i2 + 1) * 128, j * 512 : (j + 1) * 512] = scaled_rows(gain, tab, j, rows)

    total = jnp.dot(scaled[:, 0:512], w0[...], preferred_element_type=F32)
    total = total + jnp.dot(scaled[:, 512:1024], w1[...], preferred_element_type=F32)
    total = total + jnp.dot(scaled[:, 1024:1536], w2[...], preferred_element_type=F32)
    total = total + jnp.dot(scaled[:, 1536:1792], w3a[...], preferred_element_type=F32)
    total = total + jnp.dot(scaled[:, 1792:2048], w3b[...], preferred_element_type=F32)
    out[...] = total.astype(BF16)


def block(count):
    return pl.BlockSpec((count, 512), lambda n: (0, n))


def text_product(tab, text, gain, weights):
    return pl.pallas_call(
        text_kernel,
        out_shape=jax.ShapeDtypeStruct((512, 2048), BF16),
        grid=(4,),
        in_specs=[SMEM] + [VMEM] * 5 + [block(n) for n in (512, 512, 512, 256, 256)],
        out_specs=block(512),
        scratch_shapes=[pltpu.VMEM((512, 2048), BF16)],
        compiler_params=params(28),
        cost_estimate=cost(4300 * 10**6, 14 * MIB),
    )(tab, *text, gain, *weights)


def product_kernel(tab, dest, v0, v1, v2, v3, gain, text, w0, w1, w2, w3a, w3b, own, left, right, far, scaled, select):
    @pl.when(pl.program_id(0) == 0)
    def _():
        for j, visual in enumerate((v0, v1, v2, v3)):
            scaled[:, j * 512 : (j + 1) * 512] = (visual[...].astype(F32) * gain[tab[j]]).astype(BF16)
        for i2 in range(4):
            places = lax.broadcasted_iota(jnp.int32, (128, 256), 0) + tab[i2 * 4] * 128
            select[i2 * 128 : (i2 + 1) * 128, :] = (places == dest[...]).astype(F32).astype(BF16)

    total = jnp.dot(scaled[:, 0:512], w0[...], preferred_element_type=F32)
    total = total + jnp.dot(scaled[:, 512:1024], w1[...], preferred_element_type=F32)
    total = total + jnp.dot(scaled[:, 1024:1536], w2[...], preferred_element_type=F32)
    total = total + jnp.dot(scaled[:, 1536:1792], w3a[...], preferred_element_type=F32)
    total = total + jnp.dot(scaled[:, 1792:2048], w3b[...], preferred_element_type=F32)
    total = total.astype(BF16)
    for i2, out in ((3, far), (2, right), (1, left), (0, own)):
        rows = slice(i2 * 128, (i2 + 1) * 128)
        chosen = select[rows, :]
        present = jnp.sum(chosen.astype(F32), axis=1, keepdims=True) > 0.0
        picked = jnp.dot(chosen, total, preferred_element_type=F32).astype(BF16)
        out[...] = jnp.where(present, picked, text[rows, :])


def product(tab, dest, visual, gain, text, weights):
    return pl.pallas_call(
        product_kernel,
        out_shape=[jax.ShapeDtypeStruct((128, 2048), BF16)] * 4,
        grid=(4,),
        in_specs=[SMEM] + [VMEM] * 6 + [block(n) for n in (512, 512, 512, 512, 256, 256)],
        out_specs=[block(128)] * 4,
        scratch_shapes=[pltpu.VMEM((256, 2048), BF16), pltpu.VMEM((512, 256), BF16)],
        compiler_params=params(28),
        cost_estimate=cost(2700 * 10**6, 14 * MIB),
    )(tab, dest, *visual, gain, text, *weights)


def place_kernel(tab, e0, e1, e2, e3, out, scale, sems):
    copies = []
    for i2, rows in enumerate((e0, e1, e2, e3)):
        for j in range(4):
            columns = pl.ds(pl.multiple_of(tab[i2 * 4 + j] * 512, 512), 512)
            copies.append((rows.at[:, pl.ds(j * 512, 512)], out.at[:, columns]))
    copies = start(copies, sems)
    total = 0.0
    for rows in (e0, e1, e2, e3):
        values = rows[...].astype(F32)
        total = total + jnp.sum(values * values, axis=1, keepdims=True)
    scale[...] = jnp.broadcast_to(lax.rsqrt(total * (1.0 / 8192.0) + 1e-06), (128, 128))
    for copy in copies:
        copy.wait()


def place_rows(tab, pieces):
    return pl.pallas_call(
        place_kernel,
        out_shape=[jax.ShapeDtypeStruct((128, 8192), BF16), jax.ShapeDtypeStruct((128, 128), F32)],
        in_specs=[SMEM] + [VMEM] * 4,
        out_specs=[ANY, VMEM],
        scratch_shapes=[pltpu.SemaphoreType.DMA((16,))],
        compiler_params=params(32),
        cost_estimate=cost(4 * 10**6, 30 * MIB),
    )(tab, *pieces)


def per_device(
    patches,
    patch_counts,
    dest_pos,
    merge_gain,
    merge_bias,
    up_weight,
    up_bias,
    down_weight,
    down_bias,
    text_embed,
    norm_gain,
    kv_weight,
    kv_bias,
):
    tab = jnp.asarray(TABLE)[lax.axis_index("mb") * 16 + lax.axis_index("tp")]
    nat = jnp.asarray(TABLE)[lax.axis_index("tp")]
    down_part = lax.ppermute(down_weight, ("enc", "mb", "tp"), SHUFFLE)
    merged = merge(patches[0, 0], merge_gain, merge_bias)
    packed = jnp.concatenate([after(down_part, merged), up_weight], axis=1)
    packed = lax.all_gather(packed, ("enc", "mb"), axis=0, tiled=True)

    near = jnp.concatenate([merged, *around(merged, 1)], axis=0)
    group = (near, *around(near, 2))
    kv_weight = after(kv_weight, *group)
    kv_right, kv_left = hop(kv_weight, 1, 1), hop(kv_weight, 1, -1)
    own, to_left, to_right, to_far = pack(tab, text_embed[0, 0])
    moved = lax.optimization_barrier((kv_right, kv_left, to_left, to_right, to_far))
    kv_right, kv_left, to_left, to_right, to_far = moved
    far = (hop(kv_right[:256], 1, 1), hop(kv_left[256:], 1, -1))
    text = (own, hop(to_right, 2, 1), hop(to_left, 2, -1), hop(to_far, 2, 2))
    weights = (kv_weight, kv_right, kv_left, *far)

    packed = after(packed, *far, *text)
    hidden = up(tab, group, packed, up_bias.reshape(16, 1, 320))
    units = (hidden, line(hidden, "x", 1), line(hidden, "x", -1), line(hidden, "x", 2))
    gain = norm_gain.reshape(16, 1, 512)
    text_sums = text_product(tab, (after(own, hidden), *text[1:]), gain, weights)
    own, to_left, to_right, to_far = down(nat, units, after(packed, text_sums))
    bias = lax.dynamic_slice_in_dim(down_bias, lax.axis_index("tp") * 512, 512, 0)
    total = own + bias
    for value in (line(to_far, "y", 2), line(to_right, "y", 1), line(to_left, "y", -1)):
        total = total + value.astype(F32)
    visual = total.astype(BF16)
    visual = (visual, *around(after(visual, text_sums), 1))
    weights = (kv_weight, kv_right, kv_left, *far)

    live_rows = patch_counts[0, 0] // 4
    live = (jnp.arange(SLOT, dtype=jnp.int32)[None, :] < live_rows[:, None]).reshape(-1)
    dest = jnp.where(live, dest_pos[0, 0], -1)[None]
    picked = pick(tab, dest, visual, text)
    pieces = (picked[0], hop(picked[2], 2, 1), hop(picked[1], 2, -1), hop(picked[3], 2, 2))
    own, to_left, to_right, to_far = product(tab, dest, visual, gain, text_sums, weights)
    sums = (hop(to_far, 2, 2), hop(to_right, 2, 1), hop(to_left, 2, -1))
    embedded, scale = place_rows(tab, pieces)
    total = own.astype(F32)
    for value in sums:
        total = total + value.astype(F32)
    keys_values = (total * scale[:, :1] + kv_bias).astype(BF16)
    return (embedded[None, None], keys_values[None, None])


def solution(mesh):
    return jax.shard_map(
        per_device,
        mesh=mesh,
        in_specs=(
            P("enc", "mb", "tp", None),
            P("enc", "mb", None),
            P("enc", "mb", None),
            P(),
            P(),
            P(("enc", "mb"), "tp"),
            P(),
            P("tp", ("enc", "mb")),
            P(),
            P("enc", "mb", "tp", None),
            P(),
            P("tp", None),
            P(),
        ),
        out_specs=(P("enc", "mb", "tp", None), P("enc", "mb", "tp", None)),
        check_vma=False,
    )
```

```python
import jax
import jax.numpy as jnp
import numpy as np
from jax import lax
from jax.experimental import pallas as pl
from jax.experimental.pallas import tpu as pltpu
from jax.sharding import PartitionSpec as P

SLOT = 8
RING = (0, -1, 1, 2)
MIB = 1 << 20
BF16, F32 = jnp.bfloat16, jnp.float32


def place(core, tp, which, step):
    y, x = tp // 4, tp % 4
    if (core == 0) == (which == 1):
        return y * 4 + (x + step) % 4
    return (y + step) % 4 * 4 + x


TABLE = np.array(
    [
        [place(core, place(core, tp, 2, o2), 1, o1) for o2 in RING for o1 in RING]
        for core in range(2)
        for tp in range(16)
    ],
    np.int32,
)
HOPS = {
    (which, step): [(c * 16 + t, c * 16 + place(c, t, which, step)) for c in range(2) for t in range(16)]
    for which in (1, 2)
    for step in (1, -1, 2)
}
LINES = {
    (axis, step): [
        (c * 16 + t, c * 16 + place(1 if axis == "y" else 0, t, 1, step)) for c in range(2) for t in range(16)
    ]
    for axis in "yx"
    for step in (1, -1, 2)
}
SHUFFLE = [
    ((z * 2 + c) * 16 + y * 4 + x, (z // 2 * 4 + x) * 16 + y * 4 + z % 2 * 2 + c)
    for z in range(8)
    for c in range(2)
    for y in range(4)
    for x in range(4)
]


def hop(value, which, step):
    return lax.ppermute(value, ("mb", "tp"), HOPS[which, step])


def around(value, which):
    return hop(value, which, 1), hop(value, which, -1), hop(value, which, 2)


def line(value, axis, step):
    return lax.ppermute(value, ("mb", "tp"), LINES[axis, step])


def after(value, *others):
    return lax.optimization_barrier((value, *others))[0]


def cost(flops, moved):
    return pl.CostEstimate(flops=flops, bytes_accessed=moved, transcendentals=0)


def params(mib):
    return pltpu.CompilerParams(vmem_limit_bytes=mib * MIB)


VMEM = pl.BlockSpec(memory_space=pltpu.VMEM)
SMEM = pl.BlockSpec(memory_space=pltpu.SMEM)
ANY = pl.BlockSpec(memory_space=pl.ANY)
HBM = pl.BlockSpec(memory_space=pltpu.HBM)


def merge_kernel(p_ref, gain_ref, bias_ref, out_ref, rows):
    values = p_ref[...].astype(F32)
    center = values - jnp.mean(values, axis=-1, keepdims=True)
    spread = jnp.mean(center * center, axis=-1, keepdims=True)
    normal = center * lax.rsqrt(spread + 1e-06) * gain_ref[...].reshape(1, 1280) + bias_ref[...].reshape(1, 1280)
    for k in range(10):
        rows[k] = normal[:, k * 128 : (k + 1) * 128]
    for j in range(4):
        for k in range(10):
            start = j * 1280 + k * 128
            out_ref[:, start : start + 128] = rows[k, pl.ds(j, 16, stride=4), :].astype(BF16)


def merge(patches, gain, bias):
    return pl.pallas_call(
        merge_kernel,
        out_shape=jax.ShapeDtypeStruct((16, 5120), BF16),
        in_specs=[VMEM] * 3,
        out_specs=VMEM,
        scratch_shapes=[pltpu.VMEM((10, 64, 128), F32)],
        compiler_params=params(8),
        cost_estimate=cost(10**6, 330000),
    )(patches, gain, bias)


def pack_kernel(tab, *refs):
    for source, target in zip(refs[:4], refs[4:]):
        target[...] = source[...]


def pack(tab, text):
    def columns(i2):
        return pl.BlockSpec((128, 512), lambda j, tab: (0, tab[i2 * 4 + j]))

    return pl.pallas_call(
        pack_kernel,
        out_shape=[jax.ShapeDtypeStruct((128, 2048), BF16)] * 4,
        grid_spec=pltpu.PrefetchScalarGridSpec(
            num_scalar_prefetch=1,
            grid=(4,),
            in_specs=[columns(i2) for i2 in range(4)],
            out_specs=[pl.BlockSpec((128, 512), lambda j, tab: (0, j))] * 4,
        ),
        compiler_params=params(8),
        cost_estimate=cost(0, 4 * MIB),
    )(tab, text, text, text, text)


def start(copies, sems):
    copies = [pltpu.make_async_copy(a, b, sems.at[i]) for i, (a, b) in enumerate(copies)]
    for copy in copies:
        copy.start()
    return copies


def up_kernel(tab, s0, s1, s2, s3, weight, bias_ref, out_ref, rows, held, sems):
    copies = [(piece, rows.at[pl.ds(i * 64, 64)]) for i, piece in enumerate((s0, s1, s2, s3))]
    copies += [(weight.at[pl.ds(k * 1024, 1024)], held.at[pl.ds(k * 1024, 1024)]) for k in range(5)]
    copies = start(copies, sems)
    for copy in copies[:4]:
        copy.wait()
    raised = bias_ref[tab[0]]
    for k in range(5):
        copies[4 + k].wait()
        at = slice(k * 1024, (k + 1) * 1024)
        raised = raised + jnp.dot(rows[:, at], held[at, :], preferred_element_type=F32)
    hidden = (0.5 * raised * (1.0 + lax.erf(raised * np.float32(0.5**0.5)))).astype(BF16)
    for k in range(16):
        out_ref[pl.ds(pl.multiple_of(tab[k] * 16, 16), 16), :] = hidden[k * 16 : (k + 1) * 16]


def up(tab, pieces, weight, bias):
    return pl.pallas_call(
        up_kernel,
        out_shape=jax.ShapeDtypeStruct((256, 320), BF16),
        in_specs=[SMEM] + [ANY] * 5 + [VMEM],
        out_specs=VMEM,
        scratch_shapes=[
            pltpu.VMEM((256, 5120), BF16),
            pltpu.VMEM((5120, 320), BF16),
            pltpu.SemaphoreType.DMA((9,)),
        ],
        compiler_params=params(56),
        cost_estimate=cost(840 * 10**6, 6 * MIB),
    )(tab, *pieces, weight, bias)


def down_kernel(nat, h0, h1, h2, h3, weight, own, left, right, far, units, held, sems):
    copies = []
    for k, piece in enumerate((h0, h1, h2, h3)):
        copies.append((piece, units.at[k]))
        for j in range(4):
            slot = nat[j * 4] // 4 * 4 + nat[k] % 4
            source = weight.at[pl.ds(pl.multiple_of(slot * 320, 320), 320)]
            copies.append((source, held.at[k, :, pl.ds(j * 512, 512)]))
    copies = start(copies, sems)
    total = 0.0
    for k in range(4):
        for copy in copies[k * 5 : k * 5 + 5]:
            copy.wait()
        total = total + jnp.dot(units[k], held[k], preferred_element_type=F32)
    own[...] = total[:, 0:512]
    left[...] = total[:, 512:1024].astype(BF16)
    right[...] = total[:, 1024:1536].astype(BF16)
    far[...] = total[:, 1536:2048].astype(BF16)


def down(nat, pieces, weight):
    return pl.pallas_call(
        down_kernel,
        out_shape=[jax.ShapeDtypeStruct((256, 512), F32)] + [jax.ShapeDtypeStruct((256, 512), BF16)] * 3,
        in_specs=[SMEM] + [ANY] * 5,
        out_specs=[VMEM] * 4,
        scratch_shapes=[
            pltpu.VMEM((4, 256, 320), BF16),
            pltpu.VMEM((4, 320, 2048), BF16),
            pltpu.SemaphoreType.DMA((20,)),
        ],
        compiler_params=params(56),
        cost_estimate=cost(1340 * 10**6, 8 * MIB),
    )(nat, *pieces, weight)


def pick_kernel(tab, dest, v0, v1, v2, v3, *refs):
    visual = (v0[...], v1[...], v2[...], v3[...])
    targets = dest[...]
    for i2 in (3, 2, 1, 0):
        text, out = refs[i2], refs[4 + i2]
        match = (lax.broadcasted_iota(jnp.int32, (128, 256), 0) + tab[i2 * 4] * 128) == targets
        select = match.astype(F32)
        present = jnp.sum(select, axis=1, keepdims=True) > 0.0
        select = select.astype(BF16)
        for j in range(4):
            at = slice(j * 512, (j + 1) * 512)
            picked = jnp.dot(select, visual[j], preferred_element_type=F32).astype(BF16)
            out[:, at] = jnp.where(present, picked, text[:, at])


def pick(tab, dest, visual, text):
    return pl.pallas_call(
        pick_kernel,
        out_shape=[jax.ShapeDtypeStruct((128, 2048), BF16)] * 4,
        in_specs=[SMEM] + [VMEM] * 9,
        out_specs=[VMEM] * 4,
        compiler_params=params(32),
        cost_estimate=cost(540 * 10**6, 6 * MIB),
    )(tab, dest, *visual, *text)


def product_kernel(tab, e0, e1, e2, e3, gain, w0, w1, w2, w3a, w3b, own, left, right, far, scaled):
    @pl.when(pl.program_id(0) == 0)
    def _():
        for j in range(4):
            at = slice(j * 512, (j + 1) * 512)
            scale = gain[tab[j]]
            for i2, rows in enumerate((e0, e1, e2, e3)):
                scaled[i2 * 128 : (i2 + 1) * 128, at] = (rows[:, at].astype(F32) * scale).astype(BF16)

    total = jnp.dot(scaled[:, 0:512], w0[...], preferred_element_type=F32)
    total = total + jnp.dot(scaled[:, 512:1024], w1[...], preferred_element_type=F32)
    total = total + jnp.dot(scaled[:, 1024:1536], w2[...], preferred_element_type=F32)
    total = total + jnp.dot(scaled[:, 1536:1792], w3a[...], preferred_element_type=F32)
    total = total + jnp.dot(scaled[:, 1792:2048], w3b[...], preferred_element_type=F32)
    own[...] = total[0:128]
    left[...] = total[128:256].astype(BF16)
    right[...] = total[256:384].astype(BF16)
    far[...] = total[384:512].astype(BF16)


def product(tab, picked, gain, weights):
    def block(count):
        return pl.BlockSpec((count, 512), lambda n: (0, n))

    return pl.pallas_call(
        product_kernel,
        out_shape=[jax.ShapeDtypeStruct((128, 2048), F32)] + [jax.ShapeDtypeStruct((128, 2048), BF16)] * 3,
        grid=(4,),
        in_specs=[SMEM] + [VMEM] * 5 + [block(n) for n in (512, 512, 512, 256, 256)],
        out_specs=[block(128)] * 4,
        scratch_shapes=[pltpu.VMEM((512, 2048), BF16)],
        compiler_params=params(28),
        cost_estimate=cost(4300 * 10**6, 14 * MIB),
    )(tab, *picked, gain, *weights)


def place_kernel(tab, e0, e1, e2, e3, out, scale, sems):
    copies = []
    for i2, rows in enumerate((e0, e1, e2, e3)):
        for j in range(4):
            columns = pl.ds(pl.multiple_of(tab[i2 * 4 + j] * 512, 512), 512)
            copies.append((rows.at[:, pl.ds(j * 512, 512)], out.at[:, columns]))
    copies = start(copies, sems)
    total = 0.0
    for rows in (e0, e1, e2, e3):
        values = rows[...].astype(F32)
        total = total + jnp.sum(values * values, axis=1, keepdims=True)
    scale[...] = jnp.broadcast_to(lax.rsqrt(total * (1.0 / 8192.0) + 1e-06), (128, 128))
    for copy in copies:
        copy.wait()


def place_rows(tab, pieces):
    return pl.pallas_call(
        place_kernel,
        out_shape=[jax.ShapeDtypeStruct((128, 8192), BF16), jax.ShapeDtypeStruct((128, 128), F32)],
        in_specs=[SMEM] + [VMEM] * 4,
        out_specs=[ANY, VMEM],
        scratch_shapes=[pltpu.SemaphoreType.DMA((16,))],
        compiler_params=params(32),
        cost_estimate=cost(4 * 10**6, 30 * MIB),
    )(tab, *pieces)


def per_device(
    patches,
    patch_counts,
    dest_pos,
    merge_gain,
    merge_bias,
    up_weight,
    up_bias,
    down_weight,
    down_bias,
    text_embed,
    norm_gain,
    kv_weight,
    kv_bias,
):
    tab = jnp.asarray(TABLE)[lax.axis_index("mb") * 16 + lax.axis_index("tp")]
    nat = jnp.asarray(TABLE)[lax.axis_index("tp")]
    up_full = lax.all_gather(up_weight, ("enc", "mb"), axis=0, tiled=True)
    down_part = lax.ppermute(down_weight, ("enc", "mb", "tp"), SHUFFLE)

    merged = merge(patches[0, 0], merge_gain, merge_bias)
    near = jnp.concatenate([merged, *around(merged, 1)], axis=0)
    near, down_part = lax.optimization_barrier((near, down_part))
    group = (near, *around(near, 2))
    down_full = lax.all_gather(after(down_part, *group), ("enc", "mb"), axis=0, tiled=True)

    kv_weight = after(kv_weight, *group)
    kv_right, kv_left = hop(kv_weight, 1, 1), hop(kv_weight, 1, -1)
    far_right, far_left = kv_right[:256], kv_left[256:]
    own, to_left, to_right, to_far = pack(tab, text_embed[0, 0])
    hidden = up(tab, group, up_full, up_bias.reshape(16, 1, 320))
    units = (hidden, line(hidden, "x", 1), line(hidden, "x", -1), line(hidden, "x", 2))
    moved = (*units, far_right, far_left, to_left, to_right, to_far)
    *units, far_right, far_left, to_left, to_right, to_far = lax.optimization_barrier(moved)

    weights = (kv_weight, kv_right, kv_left, hop(far_right, 1, 1), hop(far_left, 1, -1))
    text = (own, hop(to_right, 2, 1), hop(to_left, 2, -1), hop(to_far, 2, 2))
    down_full = after(down_full, weights[3], weights[4], *text)
    own, to_left, to_right, to_far = down(nat, units, down_full)
    bias = lax.dynamic_slice_in_dim(down_bias, lax.axis_index("tp") * 512, 512, 0)
    total = own + bias
    for value in (line(to_far, "y", 2), line(to_right, "y", 1), line(to_left, "y", -1)):
        total = total + value.astype(F32)
    visual = total.astype(BF16)
    visual = (visual, *around(visual, 1))

    live_rows = patch_counts[0, 0] // 4
    live = (jnp.arange(SLOT, dtype=jnp.int32)[None, :] < live_rows[:, None]).reshape(-1)
    dest = jnp.where(live, dest_pos[0, 0], -1)[None]
    picked = pick(tab, dest, visual, text)
    pieces = (picked[0], hop(picked[2], 2, 1), hop(picked[1], 2, -1), hop(picked[3], 2, 2))
    own, to_left, to_right, to_far = product(tab, picked, norm_gain.reshape(16, 1, 512), weights)
    sums = (hop(to_far, 2, 2), hop(to_right, 2, 1), hop(to_left, 2, -1))
    embedded, scale = place_rows(tab, pieces)
    total = own
    for value in sums:
        total = total + value.astype(F32)
    keys_values = (total * scale[:, :1] + kv_bias).astype(BF16)
    return (embedded[None, None], keys_values[None, None])


def solution(mesh):
    return jax.shard_map(
        per_device,
        mesh=mesh,
        in_specs=(
            P("enc", "mb", "tp", None),
            P("enc", "mb", None),
            P("enc", "mb", None),
            P(),
            P(),
            P(("enc", "mb"), "tp"),
            P(),
            P("tp", ("enc", "mb")),
            P(),
            P("enc", "mb", "tp", None),
            P(),
            P("tp", None),
            P(),
        ),
        out_specs=(P("enc", "mb", "tp", None), P("enc", "mb", "tp", None)),
        check_vma=False,
    )
```

```python
import jax
import jax.numpy as jnp
import numpy as np
from jax import lax
from jax.experimental import pallas as pl
from jax.experimental.pallas import tpu as pltpu
from jax.sharding import PartitionSpec as P

SLOT = 8
RING = (0, -1, 1, 2)
MIB = 1 << 20
BF16, F32 = jnp.bfloat16, jnp.float32


def place(core, tp, which, step):
    y, x = tp // 4, tp % 4
    if (core == 0) == (which == 1):
        return y * 4 + (x + step) % 4
    return (y + step) % 4 * 4 + x


TABLE = np.array(
    [
        [place(core, place(core, tp, 2, o2), 1, o1) for o2 in RING for o1 in RING]
        for core in range(2)
        for tp in range(16)
    ],
    np.int32,
)
HOPS = {
    (which, step): [(c * 16 + t, c * 16 + place(c, t, which, step)) for c in range(2) for t in range(16)]
    for which in (1, 2)
    for step in (1, -1, 2)
}
LINES = {
    (axis, step): [
        (c * 16 + t, c * 16 + place(1 if axis == "y" else 0, t, 1, step)) for c in range(2) for t in range(16)
    ]
    for axis in "yx"
    for step in (1, -1, 2)
}
SHUFFLE = [
    ((z * 2 + c) * 16 + y * 4 + x, (z // 2 * 4 + x) * 16 + y * 4 + z % 2 * 2 + c)
    for z in range(8)
    for c in range(2)
    for y in range(4)
    for x in range(4)
]


def hop(value, which, step):
    return lax.ppermute(value, ("mb", "tp"), HOPS[which, step])


def around(value, which):
    far = hop(value, which, 2)
    return hop(value, which, 1), hop(value, which, -1), far


def line(value, axis, step):
    return lax.ppermute(value, ("mb", "tp"), LINES[axis, step])


def after(value, *others):
    return lax.optimization_barrier((value, *others))[0]


def cost(flops, moved):
    return pl.CostEstimate(flops=flops, bytes_accessed=moved, transcendentals=0)


def params(mib):
    return pltpu.CompilerParams(vmem_limit_bytes=mib * MIB)


VMEM = pl.BlockSpec(memory_space=pltpu.VMEM)
SMEM = pl.BlockSpec(memory_space=pltpu.SMEM)
ANY = pl.BlockSpec(memory_space=pl.ANY)
HBM = pl.BlockSpec(memory_space=pltpu.HBM)


def merge_kernel(p_ref, gain_ref, bias_ref, out_ref, rows):
    values = p_ref[...].astype(F32)
    center = values - jnp.mean(values, axis=-1, keepdims=True)
    spread = jnp.mean(center * center, axis=-1, keepdims=True)
    normal = center * lax.rsqrt(spread + 1e-06) * gain_ref[...].reshape(1, 1280) + bias_ref[...].reshape(1, 1280)
    for k in range(10):
        rows[k] = normal[:, k * 128 : (k + 1) * 128]
    for j in range(4):
        for k in range(10):
            start = j * 1280 + k * 128
            out_ref[:, start : start + 128] = rows[k, pl.ds(j, 16, stride=4), :].astype(BF16)


def merge(patches, gain, bias):
    return pl.pallas_call(
        merge_kernel,
        out_shape=jax.ShapeDtypeStruct((16, 5120), BF16),
        in_specs=[VMEM] * 3,
        out_specs=VMEM,
        scratch_shapes=[pltpu.VMEM((10, 64, 128), F32)],
        compiler_params=params(8),
        cost_estimate=cost(10**6, 330000),
    )(patches, gain, bias)


def pack_kernel(tab, *refs):
    for source, target in zip(refs[:4], refs[4:]):
        target[...] = source[...]


def pack(tab, text):
    def columns(i2):
        return pl.BlockSpec((128, 512), lambda j, tab: (0, tab[i2 * 4 + j]))

    return pl.pallas_call(
        pack_kernel,
        out_shape=[jax.ShapeDtypeStruct((128, 2048), BF16)] * 4,
        grid_spec=pltpu.PrefetchScalarGridSpec(
            num_scalar_prefetch=1,
            grid=(4,),
            in_specs=[columns(i2) for i2 in range(4)],
            out_specs=[pl.BlockSpec((128, 512), lambda j, tab: (0, j))] * 4,
        ),
        compiler_params=params(8),
        cost_estimate=cost(0, 4 * MIB),
    )(tab, text, text, text, text)


def start(copies, sems):
    copies = [pltpu.make_async_copy(a, b, sems.at[i]) for i, (a, b) in enumerate(copies)]
    for copy in copies:
        copy.start()
    return copies


def up_kernel(tab, s0, s1, s2, s3, weight, bias_ref, out_ref, rows, held, sems):
    copies = [(piece, rows.at[pl.ds(i * 64, 64)]) for i, piece in enumerate((s0, s1, s2, s3))]
    copies += [(weight.at[pl.ds(k * 1024, 1024)], held.at[pl.ds(k * 1024, 1024)]) for k in range(5)]
    copies = start(copies, sems)
    for copy in copies[:4]:
        copy.wait()
    raised = bias_ref[tab[0]]
    for k in range(5):
        copies[4 + k].wait()
        at = slice(k * 1024, (k + 1) * 1024)
        raised = raised + jnp.dot(rows[:, at], held[at, :], preferred_element_type=F32)
    hidden = (0.5 * raised * (1.0 + lax.erf(raised * np.float32(0.5**0.5)))).astype(BF16)
    for k in range(16):
        out_ref[pl.ds(pl.multiple_of(tab[k] * 16, 16), 16), :] = hidden[k * 16 : (k + 1) * 16]


def up(tab, pieces, weight, bias):
    return pl.pallas_call(
        up_kernel,
        out_shape=jax.ShapeDtypeStruct((256, 320), BF16),
        in_specs=[SMEM] + [ANY] * 5 + [VMEM],
        out_specs=VMEM,
        scratch_shapes=[
            pltpu.VMEM((256, 5120), BF16),
            pltpu.VMEM((5120, 320), BF16),
            pltpu.SemaphoreType.DMA((9,)),
        ],
        compiler_params=params(56),
        cost_estimate=cost(840 * 10**6, 6 * MIB),
    )(tab, *pieces, weight, bias)


def down_kernel(nat, h0, h1, h2, h3, weight, own, left, right, far, units, held, sems):
    copies = []
    for k, piece in enumerate((h0, h1, h2, h3)):
        copies.append((piece, units.at[k]))
        for j in range(4):
            slot = nat[j * 4] // 4 * 4 + nat[k] % 4
            source = weight.at[pl.ds(pl.multiple_of(slot * 320, 320), 320)]
            copies.append((source, held.at[pl.ds(k * 320, 320), pl.ds(j * 512, 512)]))
    for copy in start(copies, sems):
        copy.wait()
    rows = jnp.concatenate([units[k] for k in range(4)], axis=1)
    total = jnp.dot(rows, held[...], preferred_element_type=F32)
    own[...] = total[:, 0:512]
    left[...] = total[:, 512:1024].astype(BF16)
    right[...] = total[:, 1024:1536].astype(BF16)
    far[...] = total[:, 1536:2048].astype(BF16)


def down(nat, pieces, weight):
    return pl.pallas_call(
        down_kernel,
        out_shape=[jax.ShapeDtypeStruct((256, 512), F32)] + [jax.ShapeDtypeStruct((256, 512), BF16)] * 3,
        in_specs=[SMEM] + [ANY] * 5,
        out_specs=[VMEM] * 4,
        scratch_shapes=[
            pltpu.VMEM((4, 256, 320), BF16),
            pltpu.VMEM((1280, 2048), BF16),
            pltpu.SemaphoreType.DMA((20,)),
        ],
        compiler_params=params(56),
        cost_estimate=cost(1340 * 10**6, 8 * MIB),
    )(nat, *pieces, weight)


def pick_kernel(tab, dest, v0, v1, v2, v3, *refs):
    visual = (v0[...], v1[...], v2[...], v3[...])
    targets = dest[...]
    for i2 in (3, 2, 1, 0):
        text, out = refs[i2], refs[4 + i2]
        match = (lax.broadcasted_iota(jnp.int32, (128, 256), 0) + tab[i2 * 4] * 128) == targets
        select = match.astype(F32)
        present = jnp.sum(select, axis=1, keepdims=True) > 0.0
        select = select.astype(BF16)
        for j in range(4):
            at = slice(j * 512, (j + 1) * 512)
            picked = jnp.dot(select, visual[j], preferred_element_type=F32).astype(BF16)
            out[:, at] = jnp.where(present, picked, text[:, at])


def pick(tab, dest, visual, text):
    return pl.pallas_call(
        pick_kernel,
        out_shape=[jax.ShapeDtypeStruct((128, 2048), BF16)] * 4,
        in_specs=[SMEM] + [VMEM] * 9,
        out_specs=[VMEM] * 4,
        compiler_params=params(32),
        cost_estimate=cost(540 * 10**6, 6 * MIB),
    )(tab, dest, *visual, *text)


def product_kernel(tab, e0, e1, e2, e3, gain, *refs):
    weights, outs, (scaled, held, sems) = refs[:5], refs[5:9], refs[9:]

    def fetch(n):
        copies, row = [], 0
        for i, weight in enumerate(weights):
            count = weight.shape[0]
            source = weight.at[:, pl.ds(n * 512, 512)]
            copies.append(pltpu.make_async_copy(source, held.at[n % 2, pl.ds(row, count)], sems.at[n % 2, i]))
            row += count
        for copy in copies:
            copy.start()
        return copies

    copies = fetch(0)
    for j in range(4):
        at = slice(j * 512, (j + 1) * 512)
        scale = gain[tab[j]]
        for i2, rows in enumerate((e0, e1, e2, e3)):
            scaled[i2 * 128 : (i2 + 1) * 128, at] = (rows[:, at].astype(F32) * scale).astype(BF16)
    for n in range(4):
        later = fetch(n + 1) if n < 3 else []
        for copy in copies:
            copy.wait()
        copies = later
        total = jnp.dot(scaled[...], held[n % 2], preferred_element_type=F32)
        for i2, out in enumerate(outs):
            out[:, n * 512 : (n + 1) * 512] = total[i2 * 128 : (i2 + 1) * 128].astype(out.dtype)


def product(tab, picked, gain, weights):
    return pl.pallas_call(
        product_kernel,
        out_shape=[jax.ShapeDtypeStruct((128, 2048), F32)] + [jax.ShapeDtypeStruct((128, 2048), BF16)] * 3,
        in_specs=[SMEM] + [VMEM] * 5 + [ANY] * 5,
        out_specs=[VMEM] * 4,
        scratch_shapes=[
            pltpu.VMEM((512, 2048), BF16),
            pltpu.VMEM((2, 2048, 512), BF16),
            pltpu.SemaphoreType.DMA((2, 5)),
        ],
        compiler_params=params(56),
        cost_estimate=cost(4300 * 10**6, 14 * MIB),
    )(tab, *picked, gain, *weights)


def place_kernel(tab, e0, e1, e2, e3, out, scale, sems):
    copies = []
    for i2, rows in enumerate((e0, e1, e2, e3)):
        for j in range(4):
            columns = pl.ds(pl.multiple_of(tab[i2 * 4 + j] * 512, 512), 512)
            copies.append((rows.at[:, pl.ds(j * 512, 512)], out.at[:, columns]))
    copies = start(copies, sems)
    total = 0.0
    for rows in (e0, e1, e2, e3):
        values = rows[...].astype(F32)
        total = total + jnp.sum(values * values, axis=1, keepdims=True)
    scale[...] = jnp.broadcast_to(lax.rsqrt(total * (1.0 / 8192.0) + 1e-06), (128, 128))
    for copy in copies:
        copy.wait()


def place_rows(tab, pieces):
    return pl.pallas_call(
        place_kernel,
        out_shape=[jax.ShapeDtypeStruct((128, 8192), BF16), jax.ShapeDtypeStruct((128, 128), F32)],
        in_specs=[SMEM] + [VMEM] * 4,
        out_specs=[ANY, VMEM],
        scratch_shapes=[pltpu.SemaphoreType.DMA((16,))],
        compiler_params=params(32),
        cost_estimate=cost(4 * 10**6, 30 * MIB),
    )(tab, *pieces)


def per_device(
    patches,
    patch_counts,
    dest_pos,
    merge_gain,
    merge_bias,
    up_weight,
    up_bias,
    down_weight,
    down_bias,
    text_embed,
    norm_gain,
    kv_weight,
    kv_bias,
):
    tab = jnp.asarray(TABLE)[lax.axis_index("mb") * 16 + lax.axis_index("tp")]
    nat = jnp.asarray(TABLE)[lax.axis_index("tp")]
    up_full = lax.all_gather(up_weight, ("enc", "mb"), axis=0, tiled=True)
    down_part = lax.ppermute(down_weight, ("enc", "mb", "tp"), SHUFFLE)

    merged = merge(patches[0, 0], merge_gain, merge_bias)
    near = jnp.concatenate([merged, *around(merged, 1)], axis=0)
    group = (near, *around(near, 2))
    down_full = lax.all_gather(after(down_part, *group), ("enc", "mb"), axis=0, tiled=True)

    kv_weight = after(kv_weight, *group)
    kv_right, kv_left = hop(kv_weight, 1, 1), hop(kv_weight, 1, -1)
    far_right, far_left = kv_right[:256], kv_left[256:]
    own, to_left, to_right, to_far = pack(tab, text_embed[0, 0])
    hidden = up(tab, group, up_full, up_bias.reshape(16, 1, 320))
    far = line(hidden, "x", 2)
    units = (hidden, line(hidden, "x", 1), line(hidden, "x", -1), far)
    moved = (*units, far_right, far_left, to_left, to_right, to_far)
    *units, far_right, far_left, to_left, to_right, to_far = lax.optimization_barrier(moved)

    weights = (kv_weight, kv_right, kv_left, hop(far_right, 1, 1), hop(far_left, 1, -1))
    far = hop(to_far, 2, 2)
    text = (own, hop(to_right, 2, 1), hop(to_left, 2, -1), far)
    down_full = after(down_full, weights[3], weights[4], *text)
    own, to_left, to_right, to_far = down(nat, units, down_full)
    bias = lax.dynamic_slice_in_dim(down_bias, lax.axis_index("tp") * 512, 512, 0)
    total = own + bias
    for value in (line(to_far, "y", 2), line(to_right, "y", 1), line(to_left, "y", -1)):
        total = total + value.astype(F32)
    visual = total.astype(BF16)
    visual = (visual, *around(visual, 1))

    live_rows = patch_counts[0, 0] // 4
    live = (jnp.arange(SLOT, dtype=jnp.int32)[None, :] < live_rows[:, None]).reshape(-1)
    dest = jnp.where(live, dest_pos[0, 0], -1)[None]
    picked = pick(tab, dest, visual, text)
    far = hop(picked[3], 2, 2)
    pieces = (picked[0], hop(picked[2], 2, 1), hop(picked[1], 2, -1), far)
    own, to_left, to_right, to_far = product(tab, picked, norm_gain.reshape(16, 1, 512), weights)
    sums = (hop(to_far, 2, 2), hop(to_right, 2, 1), hop(to_left, 2, -1))
    embedded, scale = place_rows(tab, pieces)
    total = own
    for value in sums:
        total = total + value.astype(F32)
    keys_values = (total * scale[:, :1] + kv_bias).astype(BF16)
    return (embedded[None, None], keys_values[None, None])


def solution(mesh):
    return jax.shard_map(
        per_device,
        mesh=mesh,
        in_specs=(
            P("enc", "mb", "tp", None),
            P("enc", "mb", None),
            P("enc", "mb", None),
            P(),
            P(),
            P(("enc", "mb"), "tp"),
            P(),
            P("tp", ("enc", "mb")),
            P(),
            P("enc", "mb", "tp", None),
            P(),
            P("tp", None),
            P(),
        ),
        out_specs=(P("enc", "mb", "tp", None), P("enc", "mb", "tp", None)),
        check_vma=False,
    )
```

```python
import jax
import jax.numpy as jnp
import numpy as np
from jax import lax
from jax.experimental import pallas as pl
from jax.experimental.pallas import tpu as pltpu
from jax.sharding import PartitionSpec as P

SLOT = 8
RING = (0, -1, 1, 2)
MIB = 1 << 20
BF16, F32 = jnp.bfloat16, jnp.float32


def place(core, tp, which, step):
    y, x = tp // 4, tp % 4
    if (core == 0) == (which == 1):
        return y * 4 + (x + step) % 4
    return (y + step) % 4 * 4 + x


TABLE = np.array(
    [
        [place(core, place(core, tp, 2, o2), 1, o1) for o2 in RING for o1 in RING]
        for core in range(2)
        for tp in range(16)
    ],
    np.int32,
)
HOPS = {
    (which, step): [(c * 16 + t, c * 16 + place(c, t, which, step)) for c in range(2) for t in range(16)]
    for which in (1, 2)
    for step in (1, -1, 2)
}
LINES = {
    (axis, step): [
        (c * 16 + t, c * 16 + place(1 if axis == "y" else 0, t, 1, step)) for c in range(2) for t in range(16)
    ]
    for axis in "yx"
    for step in (1, -1, 2)
}
SHUFFLE = [
    ((z * 2 + c) * 16 + y * 4 + x, (z // 2 * 4 + x) * 16 + y * 4 + z % 2 * 2 + c)
    for z in range(8)
    for c in range(2)
    for y in range(4)
    for x in range(4)
]


def hop(value, which, step):
    return lax.ppermute(value, ("mb", "tp"), HOPS[which, step])


def around(value, which):
    return hop(value, which, 1), hop(value, which, -1), hop(value, which, 2)


def line(value, axis, step):
    return lax.ppermute(value, ("mb", "tp"), LINES[axis, step])


def after(value, *others):
    return lax.optimization_barrier((value, *others))[0]


def cost(flops, moved):
    return pl.CostEstimate(flops=flops, bytes_accessed=moved, transcendentals=0)


def params(mib):
    return pltpu.CompilerParams(vmem_limit_bytes=mib * MIB)


VMEM = pl.BlockSpec(memory_space=pltpu.VMEM)
SMEM = pl.BlockSpec(memory_space=pltpu.SMEM)
ANY = pl.BlockSpec(memory_space=pl.ANY)
HBM = pl.BlockSpec(memory_space=pltpu.HBM)


def merge_kernel(p_ref, gain_ref, bias_ref, out_ref, rows):
    values = p_ref[...].astype(F32)
    center = values - jnp.mean(values, axis=-1, keepdims=True)
    spread = jnp.mean(center * center, axis=-1, keepdims=True)
    normal = center * lax.rsqrt(spread + 1e-06) * gain_ref[...].reshape(1, 1280) + bias_ref[...].reshape(1, 1280)
    for k in range(10):
        rows[k] = normal[:, k * 128 : (k + 1) * 128]
    for j in range(4):
        for k in range(10):
            start = j * 1280 + k * 128
            out_ref[:, start : start + 128] = rows[k, pl.ds(j, 16, stride=4), :].astype(BF16)


def merge(patches, gain, bias):
    return pl.pallas_call(
        merge_kernel,
        out_shape=jax.ShapeDtypeStruct((16, 5120), BF16),
        in_specs=[VMEM] * 3,
        out_specs=VMEM,
        scratch_shapes=[pltpu.VMEM((10, 64, 128), F32)],
        compiler_params=params(8),
        cost_estimate=cost(10**6, 330000),
    )(patches, gain, bias)


def pack_kernel(tab, *refs):
    for source, target in zip(refs[:4], refs[4:]):
        target[...] = source[...]


def pack(tab, text):
    def columns(i2):
        return pl.BlockSpec((128, 512), lambda j, tab: (0, tab[i2 * 4 + j]))

    return pl.pallas_call(
        pack_kernel,
        out_shape=[jax.ShapeDtypeStruct((128, 2048), BF16)] * 4,
        grid_spec=pltpu.PrefetchScalarGridSpec(
            num_scalar_prefetch=1,
            grid=(4,),
            in_specs=[columns(i2) for i2 in range(4)],
            out_specs=[pl.BlockSpec((128, 512), lambda j, tab: (0, j))] * 4,
        ),
        compiler_params=params(8),
        cost_estimate=cost(0, 4 * MIB),
    )(tab, text, text, text, text)


def start(copies, sems):
    copies = [pltpu.make_async_copy(a, b, sems.at[i]) for i, (a, b) in enumerate(copies)]
    for copy in copies:
        copy.start()
    return copies


def up_kernel(tab, s0, s1, s2, s3, weight, bias_ref, out_ref, rows, held, sems):
    copies = [(piece, rows.at[pl.ds(i * 64, 64)]) for i, piece in enumerate((s0, s1, s2, s3))]
    copies += [(weight.at[pl.ds(k * 1024, 1024)], held.at[pl.ds(k * 1024, 1024)]) for k in range(5)]
    copies = start(copies, sems)
    for copy in copies[:4]:
        copy.wait()
    raised = bias_ref[tab[0]]
    for k in range(5):
        copies[4 + k].wait()
        at = slice(k * 1024, (k + 1) * 1024)
        raised = raised + jnp.dot(rows[:, at], held[at, :], preferred_element_type=F32)
    hidden = (0.5 * raised * (1.0 + lax.erf(raised * np.float32(0.5**0.5)))).astype(BF16)
    for k in range(16):
        out_ref[pl.ds(pl.multiple_of(tab[k] * 16, 16), 16), :] = hidden[k * 16 : (k + 1) * 16]


def up(tab, pieces, weight, bias):
    return pl.pallas_call(
        up_kernel,
        out_shape=jax.ShapeDtypeStruct((256, 320), BF16),
        in_specs=[SMEM] + [ANY] * 5 + [VMEM],
        out_specs=VMEM,
        scratch_shapes=[
            pltpu.VMEM((256, 5120), BF16),
            pltpu.VMEM((5120, 320), BF16),
            pltpu.SemaphoreType.DMA((9,)),
        ],
        compiler_params=params(56),
        cost_estimate=cost(840 * 10**6, 6 * MIB),
    )(tab, *pieces, weight, bias)


def down_kernel(nat, h0, h1, h2, h3, weight, own, left, right, far, units, held, sems):
    copies = []
    for k, piece in enumerate((h0, h1, h2, h3)):
        copies.append((piece, units.at[k]))
        for j in range(4):
            slot = nat[j * 4] // 4 * 4 + nat[k] % 4
            source = weight.at[pl.ds(pl.multiple_of(slot * 320, 320), 320)]
            copies.append((source, held.at[k, :, pl.ds(j * 512, 512)]))
    copies = start(copies, sems)
    total = 0.0
    for k in range(4):
        for copy in copies[k * 5 : k * 5 + 5]:
            copy.wait()
        total = total + jnp.dot(units[k], held[k], preferred_element_type=F32)
    own[...] = total[:, 0:512]
    left[...] = total[:, 512:1024].astype(BF16)
    right[...] = total[:, 1024:1536].astype(BF16)
    far[...] = total[:, 1536:2048].astype(BF16)


def down(nat, pieces, weight):
    return pl.pallas_call(
        down_kernel,
        out_shape=[jax.ShapeDtypeStruct((256, 512), F32)] + [jax.ShapeDtypeStruct((256, 512), BF16)] * 3,
        in_specs=[SMEM] + [ANY] * 5,
        out_specs=[VMEM] * 4,
        scratch_shapes=[
            pltpu.VMEM((4, 256, 320), BF16),
            pltpu.VMEM((4, 320, 2048), BF16),
            pltpu.SemaphoreType.DMA((20,)),
        ],
        compiler_params=params(56),
        cost_estimate=cost(1340 * 10**6, 8 * MIB),
    )(nat, *pieces, weight)


def pick_kernel(tab, dest, v0, v1, v2, v3, *refs):
    visual = (v0[...], v1[...], v2[...], v3[...])
    targets = dest[...]
    for i2 in (3, 2, 1, 0):
        text, out = refs[i2], refs[4 + i2]
        match = (lax.broadcasted_iota(jnp.int32, (128, 256), 0) + tab[i2 * 4] * 128) == targets
        select = match.astype(F32)
        present = jnp.sum(select, axis=1, keepdims=True) > 0.0
        select = select.astype(BF16)
        for j in range(4):
            at = slice(j * 512, (j + 1) * 512)
            picked = jnp.dot(select, visual[j], preferred_element_type=F32).astype(BF16)
            out[:, at] = jnp.where(present, picked, text[:, at])


def pick(tab, dest, visual, text):
    return pl.pallas_call(
        pick_kernel,
        out_shape=[jax.ShapeDtypeStruct((128, 2048), BF16)] * 4,
        in_specs=[SMEM] + [VMEM] * 9,
        out_specs=[VMEM] * 4,
        compiler_params=params(32),
        cost_estimate=cost(540 * 10**6, 6 * MIB),
    )(tab, dest, *visual, *text)


def product_kernel(tab, e0, e1, e2, e3, gain, w0, w1, w2, w3a, w3b, own, left, right, far, scaled):
    @pl.when(pl.program_id(0) == 0)
    def _():
        for j in range(4):
            at = slice(j * 512, (j + 1) * 512)
            scale = gain[tab[j]]
            for i2, rows in enumerate((e0, e1, e2, e3)):
                scaled[i2 * 128 : (i2 + 1) * 128, at] = (rows[:, at].astype(F32) * scale).astype(BF16)

    total = jnp.dot(scaled[:, 0:512], w0[...], preferred_element_type=F32)
    total = total + jnp.dot(scaled[:, 512:1024], w1[...], preferred_element_type=F32)
    total = total + jnp.dot(scaled[:, 1024:1536], w2[...], preferred_element_type=F32)
    total = total + jnp.dot(scaled[:, 1536:1792], w3a[...], preferred_element_type=F32)
    total = total + jnp.dot(scaled[:, 1792:2048], w3b[...], preferred_element_type=F32)
    own[...] = total[0:128]
    left[...] = total[128:256].astype(BF16)
    right[...] = total[256:384].astype(BF16)
    far[...] = total[384:512].astype(BF16)


def product(tab, picked, gain, weights):
    def block(count):
        return pl.BlockSpec((count, 512), lambda n: (0, n))

    return pl.pallas_call(
        product_kernel,
        out_shape=[jax.ShapeDtypeStruct((128, 2048), F32)] + [jax.ShapeDtypeStruct((128, 2048), BF16)] * 3,
        grid=(4,),
        in_specs=[SMEM] + [VMEM] * 5 + [block(n) for n in (512, 512, 512, 256, 256)],
        out_specs=[block(128)] * 4,
        scratch_shapes=[pltpu.VMEM((512, 2048), BF16)],
        compiler_params=params(56),
        cost_estimate=cost(4300 * 10**6, 14 * MIB),
    )(tab, *picked, gain, *weights)


def place_kernel(tab, e0, e1, e2, e3, out, scale, sems):
    copies = []
    for i2, rows in enumerate((e0, e1, e2, e3)):
        for j in range(4):
            columns = pl.ds(pl.multiple_of(tab[i2 * 4 + j] * 512, 512), 512)
            copies.append((rows.at[:, pl.ds(j * 512, 512)], out.at[:, columns]))
    copies = start(copies, sems)
    total = 0.0
    for rows in (e0, e1, e2, e3):
        values = rows[...].astype(F32)
        total = total + jnp.sum(values * values, axis=1, keepdims=True)
    scale[...] = jnp.broadcast_to(lax.rsqrt(total * (1.0 / 8192.0) + 1e-06), (128, 128))
    for copy in copies:
        copy.wait()


def place_rows(tab, pieces):
    return pl.pallas_call(
        place_kernel,
        out_shape=[jax.ShapeDtypeStruct((128, 8192), BF16), jax.ShapeDtypeStruct((128, 128), F32)],
        in_specs=[SMEM] + [VMEM] * 4,
        out_specs=[ANY, VMEM],
        scratch_shapes=[pltpu.SemaphoreType.DMA((16,))],
        compiler_params=params(32),
        cost_estimate=cost(4 * 10**6, 30 * MIB),
    )(tab, *pieces)


def per_device(
    patches,
    patch_counts,
    dest_pos,
    merge_gain,
    merge_bias,
    up_weight,
    up_bias,
    down_weight,
    down_bias,
    text_embed,
    norm_gain,
    kv_weight,
    kv_bias,
):
    tab = jnp.asarray(TABLE)[lax.axis_index("mb") * 16 + lax.axis_index("tp")]
    nat = jnp.asarray(TABLE)[lax.axis_index("tp")]
    up_full = lax.all_gather(up_weight, ("enc", "mb"), axis=0, tiled=True)
    down_part = lax.ppermute(down_weight, ("enc", "mb", "tp"), SHUFFLE)

    merged = merge(patches[0, 0], merge_gain, merge_bias)
    near = jnp.concatenate([merged, *around(merged, 1)], axis=0)
    group = (near, *around(near, 2))
    down_full = lax.all_gather(after(down_part, *group), ("enc", "mb"), axis=0, tiled=True)

    kv_weight = after(kv_weight, *group)
    kv_right, kv_left = hop(kv_weight, 1, 1), hop(kv_weight, 1, -1)
    far_right, far_left = kv_right[:256], kv_left[256:]
    own, to_left, to_right, to_far = pack(tab, text_embed[0, 0])
    hidden = up(tab, group, up_full, up_bias.reshape(16, 1, 320))
    units = (hidden, line(hidden, "x", 1), line(hidden, "x", -1), line(hidden, "x", 2))
    moved = (*units, far_right, far_left, to_left, to_right, to_far)
    *units, far_right, far_left, to_left, to_right, to_far = lax.optimization_barrier(moved)

    weights = (kv_weight, kv_right, kv_left, hop(far_right, 1, 1), hop(far_left, 1, -1))
    text = (own, hop(to_right, 2, 1), hop(to_left, 2, -1), hop(to_far, 2, 2))
    own, *parts = down(nat, units, after(down_full, text[1]))
    to_left, to_right, to_far = lax.optimization_barrier((*parts, *text[2:], *weights[3:]))[:3]
    bias = lax.dynamic_slice_in_dim(down_bias, lax.axis_index("tp") * 512, 512, 0)
    total = own + bias
    for value in (line(to_far, "y", 2), line(to_right, "y", 1), line(to_left, "y", -1)):
        total = total + value.astype(F32)
    visual = total.astype(BF16)
    visual = (visual, *around(visual, 1))

    live_rows = patch_counts[0, 0] // 4
    live = (jnp.arange(SLOT, dtype=jnp.int32)[None, :] < live_rows[:, None]).reshape(-1)
    dest = jnp.where(live, dest_pos[0, 0], -1)[None]
    picked = pick(tab, dest, visual, text)
    pieces = (picked[0], hop(picked[2], 2, 1), hop(picked[1], 2, -1), hop(picked[3], 2, 2))
    own, to_left, to_right, to_far = product(tab, picked, norm_gain.reshape(16, 1, 512), weights)
    sums = (hop(to_far, 2, 2), hop(to_right, 2, 1), hop(to_left, 2, -1))
    embedded, scale = place_rows(tab, pieces)
    total = own
    for value in sums:
        total = total + value.astype(F32)
    keys_values = (total * scale[:, :1] + kv_bias).astype(BF16)
    return (embedded[None, None], keys_values[None, None])


def solution(mesh):
    return jax.shard_map(
        per_device,
        mesh=mesh,
        in_specs=(
            P("enc", "mb", "tp", None),
            P("enc", "mb", None),
            P("enc", "mb", None),
            P(),
            P(),
            P(("enc", "mb"), "tp"),
            P(),
            P("tp", ("enc", "mb")),
            P(),
            P("enc", "mb", "tp", None),
            P(),
            P("tp", None),
            P(),
        ),
        out_specs=(P("enc", "mb", "tp", None), P("enc", "mb", "tp", None)),
        check_vma=False,
    )
```

```python
import jax
import jax.numpy as jnp
import numpy as np
from jax import lax
from jax.experimental import pallas as pl
from jax.experimental.pallas import tpu as pltpu
from jax.sharding import PartitionSpec as P

SLOT = 8
RING = (0, -1, 1, 2)
MIB = 1 << 20
BF16, F32 = jnp.bfloat16, jnp.float32


def place(core, tp, which, step):
    y, x = tp // 4, tp % 4
    if (core == 0) == (which == 1):
        return y * 4 + (x + step) % 4
    return (y + step) % 4 * 4 + x


TABLE = np.array(
    [
        [place(core, place(core, tp, 2, o2), 1, o1) for o2 in RING for o1 in RING]
        for core in range(2)
        for tp in range(16)
    ],
    np.int32,
)
HOPS = {
    (which, step): [(c * 16 + t, c * 16 + place(c, t, which, step)) for c in range(2) for t in range(16)]
    for which in (1, 2)
    for step in (1, -1, 2)
}
LINES = {
    (axis, step): [
        (c * 16 + t, c * 16 + place(1 if axis == "y" else 0, t, 1, step)) for c in range(2) for t in range(16)
    ]
    for axis in "yx"
    for step in (1, -1, 2)
}
SHUFFLE = [
    ((z * 2 + c) * 16 + y * 4 + x, (z // 2 * 4 + x) * 16 + y * 4 + z % 2 * 2 + c)
    for z in range(8)
    for c in range(2)
    for y in range(4)
    for x in range(4)
]


def hop(value, which, step):
    return lax.ppermute(value, ("mb", "tp"), HOPS[which, step])


def around(value, which):
    return hop(value, which, 1), hop(value, which, -1), hop(value, which, 2)


def line(value, axis, step):
    return lax.ppermute(value, ("mb", "tp"), LINES[axis, step])


def after(value, *others):
    return lax.optimization_barrier((value, *others))[0]


def cost(flops, moved):
    return pl.CostEstimate(flops=flops, bytes_accessed=moved, transcendentals=0)


def params(mib):
    return pltpu.CompilerParams(vmem_limit_bytes=mib * MIB)


VMEM = pl.BlockSpec(memory_space=pltpu.VMEM)
SMEM = pl.BlockSpec(memory_space=pltpu.SMEM)
ANY = pl.BlockSpec(memory_space=pl.ANY)
HBM = pl.BlockSpec(memory_space=pltpu.HBM)


def merge_kernel(p_ref, gain_ref, bias_ref, out_ref, rows):
    values = p_ref[...].astype(F32)
    center = values - jnp.mean(values, axis=-1, keepdims=True)
    spread = jnp.mean(center * center, axis=-1, keepdims=True)
    normal = center * lax.rsqrt(spread + 1e-06) * gain_ref[...].reshape(1, 1280) + bias_ref[...].reshape(1, 1280)
    for k in range(10):
        rows[k] = normal[:, k * 128 : (k + 1) * 128]
    for j in range(4):
        for k in range(10):
            start = j * 1280 + k * 128
            out_ref[:, start : start + 128] = rows[k, pl.ds(j, 16, stride=4), :].astype(BF16)


def merge(patches, gain, bias):
    return pl.pallas_call(
        merge_kernel,
        out_shape=jax.ShapeDtypeStruct((16, 5120), BF16),
        in_specs=[VMEM] * 3,
        out_specs=VMEM,
        scratch_shapes=[pltpu.VMEM((10, 64, 128), F32)],
        compiler_params=params(8),
        cost_estimate=cost(10**6, 330000),
    )(patches, gain, bias)


def pack_kernel(tab, *refs):
    for source, target in zip(refs[:4], refs[4:]):
        target[...] = source[...]


def pack(tab, text):
    def columns(i2):
        return pl.BlockSpec((128, 512), lambda j, tab: (0, tab[i2 * 4 + j]))

    return pl.pallas_call(
        pack_kernel,
        out_shape=[jax.ShapeDtypeStruct((128, 2048), BF16)] * 4,
        grid_spec=pltpu.PrefetchScalarGridSpec(
            num_scalar_prefetch=1,
            grid=(4,),
            in_specs=[columns(i2) for i2 in range(4)],
            out_specs=[pl.BlockSpec((128, 512), lambda j, tab: (0, j))] * 4,
        ),
        compiler_params=params(8),
        cost_estimate=cost(0, 4 * MIB),
    )(tab, text, text, text, text)


def start(copies, sems):
    copies = [pltpu.make_async_copy(a, b, sems.at[i]) for i, (a, b) in enumerate(copies)]
    for copy in copies:
        copy.start()
    return copies


def up_kernel(tab, s0, s1, s2, s3, weight, bias_ref, out_ref, rows, held, sems):
    copies = [(piece, rows.at[pl.ds(i * 64, 64)]) for i, piece in enumerate((s0, s1, s2, s3))]
    copies += [(weight.at[pl.ds(k * 1024, 1024)], held.at[pl.ds(k * 1024, 1024)]) for k in range(5)]
    copies = start(copies, sems)
    for copy in copies[:4]:
        copy.wait()
    raised = bias_ref[tab[0]]
    for k in range(5):
        copies[4 + k].wait()
        at = slice(k * 1024, (k + 1) * 1024)
        raised = raised + jnp.dot(rows[:, at], held[at, :], preferred_element_type=F32)
    hidden = (0.5 * raised * (1.0 + lax.erf(raised * np.float32(0.5**0.5)))).astype(BF16)
    for k in range(16):
        out_ref[pl.ds(pl.multiple_of(tab[k] * 16, 16), 16), :] = hidden[k * 16 : (k + 1) * 16]


def up(tab, pieces, weight, bias):
    return pl.pallas_call(
        up_kernel,
        out_shape=jax.ShapeDtypeStruct((256, 320), BF16),
        in_specs=[SMEM] + [ANY] * 5 + [VMEM],
        out_specs=VMEM,
        scratch_shapes=[
            pltpu.VMEM((256, 5120), BF16),
            pltpu.VMEM((5120, 320), BF16),
            pltpu.SemaphoreType.DMA((9,)),
        ],
        compiler_params=params(56),
        cost_estimate=cost(840 * 10**6, 6 * MIB),
    )(tab, *pieces, weight, bias)


def down_kernel(nat, h0, h1, h2, h3, weight, own, left, right, far, units, held, sems):
    copies = []
    for k, piece in enumerate((h0, h1, h2, h3)):
        copies.append((piece, units.at[k]))
        for j in range(4):
            slot = nat[j * 4] // 4 * 4 + nat[k] % 4
            source = weight.at[pl.ds(pl.multiple_of(slot * 320, 320), 320)]
            copies.append((source, held.at[k, :, pl.ds(j * 512, 512)]))
    copies = start(copies, sems)
    total = 0.0
    for k in range(4):
        for copy in copies[k * 5 : k * 5 + 5]:
            copy.wait()
        total = total + jnp.dot(units[k], held[k], preferred_element_type=F32)
    own[...] = total[:, 0:512]
    left[...] = total[:, 512:1024].astype(BF16)
    right[...] = total[:, 1024:1536].astype(BF16)
    far[...] = total[:, 1536:2048].astype(BF16)


def down(nat, pieces, weight):
    return pl.pallas_call(
        down_kernel,
        out_shape=[jax.ShapeDtypeStruct((256, 512), F32)] + [jax.ShapeDtypeStruct((256, 512), BF16)] * 3,
        in_specs=[SMEM] + [ANY] * 5,
        out_specs=[VMEM] * 4,
        scratch_shapes=[
            pltpu.VMEM((4, 256, 320), BF16),
            pltpu.VMEM((4, 320, 2048), BF16),
            pltpu.SemaphoreType.DMA((20,)),
        ],
        compiler_params=params(56),
        cost_estimate=cost(1340 * 10**6, 8 * MIB),
    )(nat, *pieces, weight)


def pick_kernel(tab, dest, v0, v1, v2, v3, *refs):
    visual = (v0[...], v1[...], v2[...], v3[...])
    targets = dest[...]
    for i2 in (3, 2, 1, 0):
        text, out = refs[i2], refs[4 + i2]
        match = (lax.broadcasted_iota(jnp.int32, (128, 256), 0) + tab[i2 * 4] * 128) == targets
        select = match.astype(F32)
        present = jnp.sum(select, axis=1, keepdims=True) > 0.0
        select = select.astype(BF16)
        for j in range(4):
            at = slice(j * 512, (j + 1) * 512)
            picked = jnp.dot(select, visual[j], preferred_element_type=F32).astype(BF16)
            out[:, at] = jnp.where(present, picked, text[:, at])


def pick(tab, dest, visual, text):
    return pl.pallas_call(
        pick_kernel,
        out_shape=[jax.ShapeDtypeStruct((128, 2048), BF16)] * 4,
        in_specs=[SMEM] + [VMEM] * 9,
        out_specs=[VMEM] * 4,
        compiler_params=params(32),
        cost_estimate=cost(540 * 10**6, 6 * MIB),
    )(tab, dest, *visual, *text)


def stack_kernel(w0, w1, w2, w3a, w3b, out, sems):
    copies, row = [], 0
    for weight in (w0, w1, w2, w3a, w3b):
        count = weight.shape[0]
        copies.append((weight, out.at[pl.ds(row, count)]))
        row += count
    for copy in start(copies, sems):
        copy.wait()


def stack(weights):
    return pl.pallas_call(
        stack_kernel,
        out_shape=jax.ShapeDtypeStruct((2048, 2048), BF16),
        in_specs=[ANY] * 5,
        out_specs=VMEM,
        scratch_shapes=[pltpu.SemaphoreType.DMA((5,))],
        compiler_params=params(16),
        cost_estimate=cost(0, 16 * MIB),
    )(*weights)


def product_kernel(tab, e0, e1, e2, e3, gain, weight, own, left, right, far, scaled):
    for j in range(4):
        at = slice(j * 512, (j + 1) * 512)
        scale = gain[tab[j]]
        for i2, rows in enumerate((e0, e1, e2, e3)):
            scaled[i2 * 128 : (i2 + 1) * 128, at] = (rows[:, at].astype(F32) * scale).astype(BF16)
    for n in range(4):
        at = slice(n * 512, (n + 1) * 512)
        total = jnp.dot(scaled[...], weight[:, at], preferred_element_type=F32)
        for i2, out in enumerate((own, left, right, far)):
            out[:, at] = total[i2 * 128 : (i2 + 1) * 128].astype(out.dtype)


def product(tab, picked, gain, weight):
    return pl.pallas_call(
        product_kernel,
        out_shape=[jax.ShapeDtypeStruct((128, 2048), F32)] + [jax.ShapeDtypeStruct((128, 2048), BF16)] * 3,
        in_specs=[SMEM] + [VMEM] * 6,
        out_specs=[VMEM] * 4,
        scratch_shapes=[pltpu.VMEM((512, 2048), BF16)],
        compiler_params=params(28),
        cost_estimate=cost(4300 * 10**6, 14 * MIB),
    )(tab, *picked, gain, weight)


def place_kernel(tab, e0, e1, e2, e3, out, scale, sems):
    copies = []
    for i2, rows in enumerate((e0, e1, e2, e3)):
        for j in range(4):
            columns = pl.ds(pl.multiple_of(tab[i2 * 4 + j] * 512, 512), 512)
            copies.append((rows.at[:, pl.ds(j * 512, 512)], out.at[:, columns]))
    copies = start(copies, sems)
    total = 0.0
    for rows in (e0, e1, e2, e3):
        values = rows[...].astype(F32)
        total = total + jnp.sum(values * values, axis=1, keepdims=True)
    scale[...] = jnp.broadcast_to(lax.rsqrt(total * (1.0 / 8192.0) + 1e-06), (128, 128))
    for copy in copies:
        copy.wait()


def place_rows(tab, pieces):
    return pl.pallas_call(
        place_kernel,
        out_shape=[jax.ShapeDtypeStruct((128, 8192), BF16), jax.ShapeDtypeStruct((128, 128), F32)],
        in_specs=[SMEM] + [VMEM] * 4,
        out_specs=[ANY, VMEM],
        scratch_shapes=[pltpu.SemaphoreType.DMA((16,))],
        compiler_params=params(32),
        cost_estimate=cost(4 * 10**6, 30 * MIB),
    )(tab, *pieces)


def per_device(
    patches,
    patch_counts,
    dest_pos,
    merge_gain,
    merge_bias,
    up_weight,
    up_bias,
    down_weight,
    down_bias,
    text_embed,
    norm_gain,
    kv_weight,
    kv_bias,
):
    tab = jnp.asarray(TABLE)[lax.axis_index("mb") * 16 + lax.axis_index("tp")]
    nat = jnp.asarray(TABLE)[lax.axis_index("tp")]
    up_full = lax.all_gather(up_weight, ("enc", "mb"), axis=0, tiled=True)
    down_part = lax.ppermute(down_weight, ("enc", "mb", "tp"), SHUFFLE)

    merged = merge(patches[0, 0], merge_gain, merge_bias)
    near = jnp.concatenate([merged, *around(merged, 1)], axis=0)
    group = (near, *around(near, 2))
    down_full = lax.all_gather(after(down_part, *group), ("enc", "mb"), axis=0, tiled=True)

    kv_weight = after(kv_weight, *group)
    kv_right, kv_left = hop(kv_weight, 1, 1), hop(kv_weight, 1, -1)
    far_right, far_left = kv_right[:256], kv_left[256:]
    own, to_left, to_right, to_far = pack(tab, text_embed[0, 0])
    hidden = up(tab, group, up_full, up_bias.reshape(16, 1, 320))
    units = (hidden, line(hidden, "x", 1), line(hidden, "x", -1), line(hidden, "x", 2))
    moved = (*units, far_right, far_left, to_left, to_right, to_far)
    *units, far_right, far_left, to_left, to_right, to_far = lax.optimization_barrier(moved)

    weights = (kv_weight, kv_right, kv_left, hop(far_right, 1, 1), hop(far_left, 1, -1))
    text = (own, hop(to_right, 2, 1), hop(to_left, 2, -1), hop(to_far, 2, 2))
    own, *parts = down(nat, units, after(down_full, text[1]))
    moved = lax.optimization_barrier((*parts, *weights[3:], *text[2:]))
    (to_left, to_right, to_far), weights = moved[:3], stack((*weights[:3], *moved[3:5]))
    bias = lax.dynamic_slice_in_dim(down_bias, lax.axis_index("tp") * 512, 512, 0)
    total = own + bias
    for value in (line(to_far, "y", 2), line(to_right, "y", 1), line(to_left, "y", -1)):
        total = total + value.astype(F32)
    visual = total.astype(BF16)
    visual = (visual, *around(after(visual, weights), 1))

    live_rows = patch_counts[0, 0] // 4
    live = (jnp.arange(SLOT, dtype=jnp.int32)[None, :] < live_rows[:, None]).reshape(-1)
    dest = jnp.where(live, dest_pos[0, 0], -1)[None]
    picked = pick(tab, dest, visual, text)
    pieces = (picked[0], hop(picked[2], 2, 1), hop(picked[1], 2, -1), hop(picked[3], 2, 2))
    own, to_left, to_right, to_far = product(tab, picked, norm_gain.reshape(16, 1, 512), weights)
    sums = (hop(to_far, 2, 2), hop(to_right, 2, 1), hop(to_left, 2, -1))
    embedded, scale = place_rows(tab, pieces)
    total = own
    for value in sums:
        total = total + value.astype(F32)
    keys_values = (total * scale[:, :1] + kv_bias).astype(BF16)
    return (embedded[None, None], keys_values[None, None])


def solution(mesh):
    return jax.shard_map(
        per_device,
        mesh=mesh,
        in_specs=(
            P("enc", "mb", "tp", None),
            P("enc", "mb", None),
            P("enc", "mb", None),
            P(),
            P(),
            P(("enc", "mb"), "tp"),
            P(),
            P("tp", ("enc", "mb")),
            P(),
            P("enc", "mb", "tp", None),
            P(),
            P("tp", None),
            P(),
        ),
        out_specs=(P("enc", "mb", "tp", None), P("enc", "mb", "tp", None)),
        check_vma=False,
    )
```
